512 devices in a mesh: rep: 32 (over z, x), tp: 16 (over y, core).
Axes of the slice: x: 4, y: 8, z: 8, core: 2. Of those that a mesh axis runs over, the one named last changes fastest.
Arguments:
- requests: bfloat16 [8192, 16384], P('rep', 'tp'), may hold values from -6 to 6
- value_weight: bfloat16 [16384, 1024], P('tp'), may hold values from -0.0625 to 0.0625
- shrink_weight: bfloat16 [1024, 16, 16384], P('rep', None, 'tp'), may hold values from -0.046875 to 0.046875
- expand_weight: bfloat16 [1024, 16, 1024], P('rep', None, 'tp'), may hold values from -1.5 to 1.5
- destination: int32 [8192], replicated, may hold values from 0 to 31, as said below
- adapter_ids: int32 [8192], replicated, may hold values from 0 to 31
- cache_lists: int32 [32, 32], replicated, may hold values from 0 to 1023, as said below
- home_table: int32 [1024], replicated, may hold values from 0 to 1023, as said below
Outputs:
- adapted: bfloat16 [24576, 1024], P('rep', 'tp')
The draws below stay inside these ranges and needn't reach their ends.
Inputs may be any that keep to these rules, and one draw needn't show every extreme that they name: `destination`: among the 256 requests of one arrival group at most 24 go to one replica group, and some single replica group receives exactly 24 from every arrival group. `cache_lists`: each row lists 32 distinct adapters, at most 2 of them homed on one replica group (home_table[a] // 32), and exactly 2 on some group in every row. `home_table`: A permutation of the 1024 home positions.
All inputs are finite; a program needn't handle non-finite values.
Results may differ from the reference program's by a relative error of at most 0.001.
Values may be sent and summed in bfloat16 or wider, within the bound.
A program may use at most 64 MiB of HBM per device.

```python
import math
import jax
import jax.numpy as jnp
from jax import lax

D = 16384
KV = 1024
R = 16
HOME = 32
TOK_DEV = 256
ROWCAP = 24
CACHE = 32
ADAPTERS = 1024
TOKENS = 8192
SLOTS = 24576
N_REP = 32


def common_draw(key):
    sort_keys = jax.random.split(key, 6)
    home_table = jax.random.permutation(sort_keys[0], ADAPTERS).astype(jnp.int32)
    resident = jnp.zeros((ADAPTERS,), jnp.int32).at[home_table].set(jnp.arange(ADAPTERS, dtype=jnp.int32))
    counter = jnp.arange(2 * N_REP, dtype=jnp.int32)

    def one_list(list_key):
        first_key, second_key = jax.random.split(list_key, 2)
        shuffled = jax.random.permutation(first_key, counter // 2)
        twin = jnp.argmax((shuffled == shuffled[0]) & (counter != 0)).astype(jnp.int32)
        swapped = shuffled.at[twin].set(shuffled[1]).at[1].set(shuffled[0])
        homes = swapped[:N_REP]
        places = jnp.arange(N_REP, dtype=jnp.int32)
        earlier = jnp.sum(((homes[None, :] == homes[:, None]) & (places[None, :] < places[:, None])).astype(jnp.int32), axis=1)
        start_slot = jax.random.randint(second_key, (N_REP,), 0, HOME)
        local_slot = (start_slot[homes] + earlier) % HOME
        return homes * HOME + local_slot
    positions = jax.vmap(one_list)(jax.random.split(sort_keys[1], N_REP))
    cache_lists = resident[positions]
    slot_count_total = N_REP * ROWCAP
    group_lookup = jnp.arange(slot_count_total, dtype=jnp.int32) // ROWCAP
    extra_credit = jax.random.randint(sort_keys[2], (N_REP,), 0, 4)
    heaviest_adapter = jax.random.randint(sort_keys[3], (), 0, N_REP)
    extra_credit = extra_credit.at[heaviest_adapter].set(8)
    slot_credit = extra_credit[group_lookup].at[(N_REP - 1) * ROWCAP].set(9)

    def one_block(block_key):
        ranking_key, order_key = jax.random.split(block_key, 2)
        adapter_scores = slot_credit * 4096 + jax.random.randint(ranking_key, (slot_count_total,), 0, 4096)
        adapter_scores = adapter_scores * slot_count_total + jnp.arange(slot_count_total, dtype=jnp.int32)
        chosen = lax.top_k(adapter_scores, TOK_DEV)[1]
        return jax.random.permutation(order_key, group_lookup[chosen])
    destination = jax.vmap(one_block)(jax.random.split(sort_keys[4], N_REP)).reshape(-1).astype(jnp.int32)
    picked = jax.random.randint(sort_keys[5], (TOKENS,), 0, CACHE)
    picked = picked.at[0].set(CACHE - 1).at[1].set(0).astype(jnp.int32)
    return (destination, picked, cache_lists.astype(jnp.int32), home_table)


def draw_destination(key, part):
    return common_draw(key)[0]


def draw_adapter_ids(key, part):
    return common_draw(key)[1]


def draw_cache_lists(key, part):
    return common_draw(key)[2]


def draw_home_table(key, part):
    return common_draw(key)[3]


def strengthened(array, stream_key, source, target, shards_of, factor):
    def block_of(axis_at):
        return (jnp.arange(array.shape[axis_at]) // (array.shape[axis_at] // shards_of)).reshape((-1,) + (1,) * (array.ndim - 1 - axis_at))

    near = jax.random.permutation(stream_key, shards_of)[block_of(target)]
    second = (block_of(target) + shards_of // 2) % shards_of
    return jnp.where((block_of(source) == near) | (block_of(source) == second), factor * array, array)


def level_of(rng, dims, shards, low, high):
    level, own = 1.0, jax.random.fold_in(rng, 6)
    for axis_at, blocks in shards:
        heights = jnp.exp(jax.random.uniform(jax.random.fold_in(own, axis_at), (blocks,), jnp.float32, low / len(shards), high / len(shards)))
        level = level * jnp.repeat(heights, dims[axis_at] // blocks).reshape([-1 if axis == axis_at else 1 for axis in range(len(dims))])
    return level


def gaussian(key, dims, scale, most, shards=(), kind=jnp.bfloat16):
    drawn = scale * jax.random.normal(key, dims, jnp.float32)
    if shards:
        drawn = drawn * level_of(key, dims, shards, -0.22, 0.18)
    return jnp.clip(drawn, -most, most).astype(kind)


def bell_draw_with(key, shape, deviation, limit, cuts, heavy, kind=jnp.bfloat16):
    drawn = deviation * jax.random.normal(key, shape, jnp.float32)
    if cuts:
        drawn = drawn * level_of(key, shape, cuts, -0.22, 0.18)
    return jnp.clip(strengthened(drawn, jax.random.fold_in(key, 3), *heavy), -limit, limit).astype(kind)


def setup_inputs(seed: int = 0) -> dict:
    key_of = jax.random.split(jax.random.key(seed), 9)
    return {
        "requests": gaussian(key_of[0], (TOKENS, D), 1.0, 6.0, ((0, 32), (1, 16))),
        "value_weight": bell_draw_with(key_of[1], (D, KV), D ** -0.5, 0.0625, ((0, 16),), (0, 1, 16, 2.0)),
        "shrink_weight": gaussian(key_of[2], (ADAPTERS, R, D), D ** -0.5, 0.046875, ((0, 32), (2, 16))),
        "expand_weight": gaussian(key_of[3], (ADAPTERS, R, KV), R ** -0.5, 1.5, ((0, 32), (2, 16))),
        "destination": draw_destination(jax.random.fold_in(key_of[8], 71), 0),
        "adapter_ids": draw_adapter_ids(jax.random.fold_in(key_of[8], 71), 0),
        "cache_lists": draw_cache_lists(jax.random.fold_in(key_of[8], 71), 0),
        "home_table": draw_home_table(jax.random.fold_in(key_of[8], 71), 0),
    }


def reference(requests, value_weight, shrink_weight, expand_weight, destination, adapter_ids, cache_lists, home_table):
    base = jnp.dot(requests, value_weight, preferred_element_type=jnp.float32)
    chosen_adapter = cache_lists[destination, adapter_ids]
    positions = home_table[chosen_adapter]
    block_len = math.gcd(TOKENS, 128)

    def expand_block(args):
        row_block, homes_at = args
        down_block = shrink_weight[homes_at].astype(jnp.float32)
        up_block = expand_weight[homes_at].astype(jnp.float32)
        shrunk = jnp.einsum("td,trd->tr", row_block.astype(jnp.float32), down_block, precision=lax.Precision.HIGHEST)
        return jnp.einsum("tr,trk->tk", shrunk, up_block, precision=lax.Precision.HIGHEST)

    expanded = lax.map(expand_block, (requests.reshape(-1, block_len, D), positions.reshape(-1, block_len)))
    expanded = expanded.reshape(TOKENS, KV)
    blocks = destination.reshape(N_REP, TOK_DEV)
    member = (blocks[:, :, None] == jnp.arange(N_REP, dtype=jnp.int32)[None, None, :]).astype(jnp.int32)
    earlier = jnp.sum(member * (jnp.cumsum(member, axis=1) - 1), axis=2)
    sources = jnp.arange(N_REP, dtype=jnp.int32)[:, None]
    slots = (blocks * (N_REP * ROWCAP) + sources * ROWCAP + earlier).reshape(-1).astype(jnp.int32)
    adapted = jnp.zeros((SLOTS, KV), jnp.float32).at[slots].set(base + expanded)
    return adapted.astype(jnp.bfloat16)
```

```python
import jax
import jax.numpy as jnp
from jax import lax
from jax.sharding import PartitionSpec as P

PAIR = 2


def by_serving_group(
    requests,
    value_weight,
    shrink_weight,
    expand_weight,
    destination,
    adapter_ids,
    cache_lists,
    home_table,
):
    groups = lax.axis_size("rep")
    own_group = lax.axis_index("rep")
    tok_dev = requests.shape[0]
    rowcap = 3 * tok_dev // groups
    buffer_rows = groups * rowcap
    home_count = shrink_weight.shape[0]
    cache_len = cache_lists.shape[1]
    rank_width = shrink_weight.shape[1]
    width_out = expand_weight.shape[2]
    places = jnp.arange(cache_len, dtype=jnp.int32)
    blocks = destination.reshape(groups, tok_dev)
    targets = jnp.arange(groups, dtype=jnp.int32)
    member = (blocks[:, :, None] == targets[None, None, :]).astype(jnp.int32)
    earlier = jnp.sum(member * (jnp.cumsum(member, axis=1) - 1), axis=2)
    slot_all = targets[:, None] * rowcap + earlier
    own_slot = lax.dynamic_index_in_dim(
        blocks, own_group, 0, keepdims=False
    ) * rowcap + lax.dynamic_index_in_dim(earlier, own_group, 0, keepdims=False)
    send_rows = (
        jnp.zeros((buffer_rows, requests.shape[1]), requests.dtype).at[own_slot].set(requests)
    )
    arrived = lax.all_to_all(send_rows, "rep", split_axis=0, concat_axis=0, tiled=True)
    landing = jnp.where(blocks == own_group, slot_all, buffer_rows).reshape(-1)
    slot_place = jnp.full((buffer_rows,), -1, jnp.int32).at[landing].set(adapter_ids, mode="drop")
    selector = (slot_place[:, None] == places[None, :]).astype(jnp.float32)
    positions = home_table[cache_lists]
    home_group = positions // home_count
    local_slot = positions % home_count
    homed_here = home_group == own_group
    ranking = jnp.cumsum(homed_here.astype(jnp.int32), axis=1) - 1
    outgoing = jnp.where(homed_here, targets[:, None] * PAIR + ranking, groups * PAIR).reshape(-1)
    send_index = (
        jnp.zeros((groups * PAIR,), jnp.int32).at[outgoing].set(local_slot.reshape(-1), mode="drop")
    )
    send_valid = (
        jnp.zeros((groups * PAIR,), jnp.bfloat16).at[outgoing].set(jnp.bfloat16(1.0), mode="drop")
    )
    send_down = shrink_weight[send_index] * send_valid[:, None, None]
    send_up = expand_weight[send_index] * send_valid[:, None, None]
    got_down, got_up = (
        lax.all_to_all(send_down, "rep", split_axis=0, concat_axis=0, tiled=True),
        lax.all_to_all(send_up, "rep", split_axis=0, concat_axis=0, tiled=True),
    )
    own_homes = lax.dynamic_index_in_dim(home_group, own_group, 0, keepdims=False)
    same_before = jnp.sum(
        ((own_homes[None, :] == own_homes[:, None]) & (places[None, :] < places[:, None])).astype(
            jnp.int32
        ),
        axis=1,
    )
    fetch_index = own_homes * PAIR + same_before
    cached_down = got_down[fetch_index].reshape(cache_len * rank_width, -1)
    cached_up = got_up[fetch_index].reshape(cache_len * rank_width, width_out).astype(jnp.float32)
    shrunk_all = lax.dot_general(
        arrived, cached_down, (((1,), (1,)), ((), ())), preferred_element_type=jnp.float32
    )
    shrunk_part = jnp.sum(
        shrunk_all.reshape(buffer_rows, cache_len, rank_width) * selector[:, :, None], axis=1
    )
    shrunk = lax.psum(shrunk_part, "tp")
    spread_rows = (selector[:, :, None] * shrunk[:, None, :]).reshape(
        buffer_rows, cache_len * rank_width
    )
    expanded = jnp.dot(spread_rows, cached_up, precision=lax.Precision.HIGHEST)
    partial_all = jnp.dot(arrived, value_weight, preferred_element_type=jnp.float32)
    projected = lax.psum_scatter(partial_all, "tp", scatter_dimension=1, tiled=True)
    return (projected + expanded).astype(jnp.bfloat16)


CAP = 24


def place_of(destination, adapter_ids, cache_lists, home_table, groups, home_count):
    adapters = home_table.shape[0]
    lists, cache_len = cache_lists.shape
    entry = (
        cache_lists.reshape(-1)[:, None] == jnp.arange(adapters, dtype=jnp.int32)[None, :]
    ).astype(jnp.bfloat16)
    table = jnp.stack([home_table // home_count, home_table % home_count], axis=1)
    listed = jnp.dot(entry, table.astype(jnp.bfloat16), preferred_element_type=jnp.float32)
    listed = listed.reshape(lists, cache_len * 2).T.astype(jnp.bfloat16)
    serving = (
        destination[None, :] == jnp.arange(lists, dtype=jnp.int32)[:, None]
    ).astype(jnp.bfloat16)
    rows = jnp.dot(listed, serving, preferred_element_type=jnp.float32)
    rows = rows.reshape(cache_len, 2, -1)
    chosen = adapter_ids[None, :] == jnp.arange(cache_len, dtype=jnp.int32)[:, None]
    both = jnp.sum(jnp.where(chosen[:, None, :], rows, 0.0), axis=0)
    home, local = both[0].astype(jnp.int32), both[1].astype(jnp.int32)
    tok = destination.shape[0] // groups
    home, local = home.reshape(groups, tok), local.reshape(groups, tok)
    member = home[None, :, :] == jnp.arange(groups, dtype=jnp.int32)[:, None, None]
    return home, local, rank_of(member, tok)


def rank_of(member, tok):
    order = jnp.arange(tok, dtype=jnp.int32)
    before = (order[:, None] < order[None, :]).astype(jnp.bfloat16)
    earlier = lax.dot_general(
        member.astype(jnp.bfloat16),
        before,
        (((member.ndim - 1,), (0,)), ((), ())),
        preferred_element_type=jnp.float32,
    )
    return jnp.sum(jnp.where(member, earlier, 0.0), axis=0).astype(jnp.int32)


def on_device(
    requests,
    value_weight,
    shrink_weight,
    expand_weight,
    destination,
    adapter_ids,
    cache_lists,
    home_table,
):
    groups = lax.axis_size("rep")
    me = lax.axis_index("rep")
    tok = requests.shape[0]
    home_count, rank, depth = shrink_weight.shape
    width = expand_weight.shape[2]
    home, local, place = place_of(
        destination, adapter_ids, cache_lists, home_table, groups, home_count
    )
    fits = jnp.max(place) < CAP

    def by_home_group(requests, value_weight, shrink_weight, expand_weight):
        slots = groups * CAP
        slot_ids = jnp.arange(slots, dtype=jnp.int32)
        own = lambda a: lax.dynamic_index_in_dim(a, me, 0, keepdims=False)
        to_home = own(home) * CAP + own(place)
        pack = (slot_ids[:, None] == to_home[None, :]).astype(jnp.bfloat16)
        send = jnp.dot(pack, requests, preferred_element_type=jnp.float32).astype(jnp.bfloat16)
        arrived = lax.all_to_all(send, "rep", split_axis=0, concat_axis=0, tiled=True)
        base = jnp.dot(requests, value_weight, preferred_element_type=jnp.float32)
        base = lax.psum_scatter(base, "tp", scatter_dimension=1, tiled=True)
        here = (home == me)[:, None, :] & (
            place[:, None, :] == jnp.arange(CAP, dtype=jnp.int32)[None, :, None]
        )
        adapter = jnp.sum(jnp.where(here, local[:, None, :] + 1, 0), axis=2).reshape(slots) - 1
        selector = (adapter[:, None] == jnp.arange(home_count, dtype=jnp.int32)[None, :]).astype(
            jnp.float32
        )
        shrunk_all = lax.dot_general(
            arrived,
            shrink_weight.reshape(home_count * rank, depth),
            (((1,), (1,)), ((), ())),
            preferred_element_type=jnp.float32,
        )
        shrunk = jnp.sum(
            shrunk_all.reshape(slots, home_count, rank) * selector[:, :, None], axis=1
        )
        shrunk = lax.psum(shrunk, "tp")
        spread = (selector[:, :, None] * shrunk[:, None, :]).reshape(slots, home_count * rank)
        expanded = jnp.dot(
            spread,
            expand_weight.reshape(home_count * rank, width).astype(jnp.float32),
            precision=lax.Precision.HIGHEST,
        )
        back = lax.all_to_all(expanded, "rep", split_axis=0, concat_axis=0, tiled=True)
        unpack = (to_home[:, None] == slot_ids[None, :]).astype(jnp.float32)
        total = base + jnp.dot(unpack, back, precision=lax.Precision.HIGHEST)
        serving = own(destination.reshape(groups, tok))
        rowcap = 3 * tok // groups
        order = rank_of(serving[None, :] == jnp.arange(groups, dtype=jnp.int32)[:, None], tok)
        to_slot = serving * rowcap + order
        place_out = (
            jnp.arange(groups * rowcap, dtype=jnp.int32)[:, None] == to_slot[None, :]
        ).astype(jnp.bfloat16)
        final = jnp.dot(
            place_out, total.astype(jnp.bfloat16), preferred_element_type=jnp.float32
        ).astype(jnp.bfloat16)
        return lax.all_to_all(final, "rep", split_axis=0, concat_axis=0, tiled=True)

    def any_input(requests, value_weight, shrink_weight, expand_weight):
        return by_serving_group(
            requests,
            value_weight,
            shrink_weight,
            expand_weight,
            destination,
            adapter_ids,
            cache_lists,
            home_table,
        )

    return lax.cond(
        fits, by_home_group, any_input, requests, value_weight, shrink_weight, expand_weight
    )


def solution(mesh):
    in_specs = (
        P("rep", "tp"),
        P("tp", None),
        P("rep", None, "tp"),
        P("rep", None, "tp"),
        P(),
        P(),
        P(),
        P(),
    )
    out_specs = P("rep", "tp")
    return jax.shard_map(
        on_device, mesh=mesh, in_specs=in_specs, out_specs=out_specs, check_vma=False
    )
```

```python
import functools

import jax
import jax.numpy as jnp
from jax import lax
from jax.experimental import pallas as pl
from jax.experimental.pallas import tpu as pltpu
from jax.sharding import PartitionSpec as P

PAIR = 2


def by_serving_group(
    requests,
    value_weight,
    shrink_weight,
    expand_weight,
    destination,
    adapter_ids,
    cache_lists,
    home_table,
):
    groups = lax.axis_size("rep")
    own_group = lax.axis_index("rep")
    tok_dev = requests.shape[0]
    rowcap = 3 * tok_dev // groups
    buffer_rows = groups * rowcap
    home_count = shrink_weight.shape[0]
    cache_len = cache_lists.shape[1]
    rank_width = shrink_weight.shape[1]
    width_out = expand_weight.shape[2]
    places = jnp.arange(cache_len, dtype=jnp.int32)
    blocks = destination.reshape(groups, tok_dev)
    targets = jnp.arange(groups, dtype=jnp.int32)
    member = (blocks[:, :, None] == targets[None, None, :]).astype(jnp.int32)
    earlier = jnp.sum(member * (jnp.cumsum(member, axis=1) - 1), axis=2)
    slot_all = targets[:, None] * rowcap + earlier
    own_slot = lax.dynamic_index_in_dim(
        blocks, own_group, 0, keepdims=False
    ) * rowcap + lax.dynamic_index_in_dim(earlier, own_group, 0, keepdims=False)
    send_rows = (
        jnp.zeros((buffer_rows, requests.shape[1]), requests.dtype).at[own_slot].set(requests)
    )
    arrived = lax.all_to_all(send_rows, "rep", split_axis=0, concat_axis=0, tiled=True)
    landing = jnp.where(blocks == own_group, slot_all, buffer_rows).reshape(-1)
    slot_place = jnp.full((buffer_rows,), -1, jnp.int32).at[landing].set(adapter_ids, mode="drop")
    selector = (slot_place[:, None] == places[None, :]).astype(jnp.float32)
    positions = home_table[cache_lists]
    home_group = positions // home_count
    local_slot = positions % home_count
    homed_here = home_group == own_group
    ranking = jnp.cumsum(homed_here.astype(jnp.int32), axis=1) - 1
    outgoing = jnp.where(homed_here, targets[:, None] * PAIR + ranking, groups * PAIR).reshape(-1)
    send_index = (
        jnp.zeros((groups * PAIR,), jnp.int32).at[outgoing].set(local_slot.reshape(-1), mode="drop")
    )
    send_valid = (
        jnp.zeros((groups * PAIR,), jnp.bfloat16).at[outgoing].set(jnp.bfloat16(1.0), mode="drop")
    )
    send_down = shrink_weight[send_index] * send_valid[:, None, None]
    send_up = expand_weight[send_index] * send_valid[:, None, None]
    got_down, got_up = (
        lax.all_to_all(send_down, "rep", split_axis=0, concat_axis=0, tiled=True),
        lax.all_to_all(send_up, "rep", split_axis=0, concat_axis=0, tiled=True),
    )
    own_homes = lax.dynamic_index_in_dim(home_group, own_group, 0, keepdims=False)
    same_before = jnp.sum(
        ((own_homes[None, :] == own_homes[:, None]) & (places[None, :] < places[:, None])).astype(
            jnp.int32
        ),
        axis=1,
    )
    fetch_index = own_homes * PAIR + same_before
    cached_down = got_down[fetch_index].reshape(cache_len * rank_width, -1)
    cached_up = got_up[fetch_index].reshape(cache_len * rank_width, width_out).astype(jnp.float32)
    shrunk_all = lax.dot_general(
        arrived, cached_down, (((1,), (1,)), ((), ())), preferred_element_type=jnp.float32
    )
    shrunk_part = jnp.sum(
        shrunk_all.reshape(buffer_rows, cache_len, rank_width) * selector[:, :, None], axis=1
    )
    shrunk = lax.psum(shrunk_part, "tp")
    spread_rows = (selector[:, :, None] * shrunk[:, None, :]).reshape(
        buffer_rows, cache_len * rank_width
    )
    expanded = jnp.dot(spread_rows, cached_up, precision=lax.Precision.HIGHEST)
    partial_all = jnp.dot(arrived, value_weight, preferred_element_type=jnp.float32)
    projected = lax.psum_scatter(partial_all, "tp", scatter_dimension=1, tiled=True)
    return (projected + expanded).astype(jnp.bfloat16)


CAP = 24
HOMES = 32
MESH = pl.DeviceIdType.MESH
NX = 4
F32, BF16 = jnp.float32, jnp.bfloat16


def fused_kernel(
    groups,
    peers,
    x_ref,
    v_ref,
    a_ref,
    e_ref,
    home_ref,
    slot_ref,
    adapter_ref,
    out_ref,
    send,
    recv,
    bsend,
    brecv,
    adp,
    fold,
    rs_send,
    rs_recv,
    ag,
    xsend,
    xrecv,
    osend,
    send_sem,
    recv_sem,
    bsend_sem,
    brecv_sem,
    rs_send_sem,
    rs_recv_sem,
    ag_send_sem,
    ag_recv_sem,
    xsend_sem,
    xrecv_sem,
    osend_sem,
    orecv_sem,
    local_sem,
):
    me = lax.axis_index("rep")
    mt = lax.axis_index("tp")
    mz, mx = me // NX, me % NX
    nz = groups // NX
    tok, depth = x_ref.shape
    plane = NX * CAP
    slots = groups * CAP

    barrier = pltpu.get_barrier_semaphore()

    def greet_rep(k, c):
        pl.semaphore_signal(
            barrier, inc=1, device_id={"rep": lax.rem(me + k, groups)}, device_id_type=MESH
        )
        return c

    def greet_tp(k, c):
        pl.semaphore_signal(
            barrier, inc=1, device_id={"tp": lax.rem(mt + k, peers)}, device_id_type=MESH
        )
        return c

    lax.fori_loop(1, groups, greet_rep, 0)
    lax.fori_loop(1, peers, greet_tp, 0)

    x = x_ref[...]
    for z in range(nz):
        ids = lax.broadcasted_iota(jnp.int32, (plane, tok), 0) + z * plane
        pick = (ids == home_ref[...]).astype(F32).astype(BF16)
        rows = jnp.dot(pick, x, preferred_element_type=F32)
        for i in range(NX):
            send[z * NX + i] = rows[i * CAP : (i + 1) * CAP].astype(BF16)

    pl.semaphore_wait(barrier, groups + peers - 2)

    def dz_of(j):
        return lax.rem(nz // 2 + (1 - 2 * lax.rem(j, 2)) * ((j + 1) // 2) + nz, nz)

    def target_of(k):
        z = lax.rem(mz + dz_of(k // NX), nz)
        return z * NX + lax.rem(mx + 1 + lax.rem(k, NX), NX)

    def source_of(k):
        z = lax.rem(mz + nz - dz_of(k // NX), nz)
        return z * NX + lax.rem(mx + 2 * NX - 1 - lax.rem(k, NX), NX)

    def rep_copy(src, dst, ssem, rsem, to, frm):
        return pltpu.make_async_remote_copy(
            src_ref=src.at[to],
            dst_ref=dst.at[frm],
            send_sem=ssem.at[to],
            recv_sem=rsem.at[frm],
            device_id={"rep": to},
            device_id_type=MESH,
        )

    def tp_copy(src, dst, ssem, rsem, to, frm):
        return pltpu.make_async_remote_copy(
            src_ref=src,
            dst_ref=dst.at[frm],
            send_sem=ssem.at[to],
            recv_sem=rsem.at[frm],
            device_id={"tp": to},
            device_id_type=MESH,
        )

    def start_rep(src, dst, ssem, rsem):
        def body(k, c):
            rep_copy(src, dst, ssem, rsem, target_of(k), me).start()
            return c

        lax.fori_loop(0, groups - 1, body, 0)

    def finish_rep_send(src, dst, ssem, rsem):
        def body(k, c):
            rep_copy(src, dst, ssem, rsem, target_of(k), me).wait_send()
            return c

        lax.fori_loop(0, groups - 1, body, 0)

    def finish_rep_recv(src, dst, ssem, rsem):
        def body(k, c):
            s = source_of(k)
            rep_copy(src, dst, ssem, rsem, s, s).wait_recv()
            return c

        lax.fori_loop(0, groups - 1, body, 0)

    start_rep(send, recv, send_sem, recv_sem)
    keep = pltpu.make_async_copy(send.at[me], recv.at[me], local_sem.at[0])
    keep.start()

    width = bsend.shape[1]
    step = 256
    for n in range(v_ref.shape[1] // step):
        b = jnp.dot(x, v_ref[:, n * step : (n + 1) * step], preferred_element_type=F32)
        bt = b.T
        for i in range(step // width):
            bsend[n * (step // width) + i] = bt[i * width : (i + 1) * width]

    def base_start(k, c):
        to = lax.rem(mt + k, peers)
        tp_copy(bsend.at[to], brecv, bsend_sem, brecv_sem, to, mt).start()
        return c

    lax.fori_loop(1, peers, base_start, 0)

    lanes = 128
    adp[...] = jnp.broadcast_to(adapter_ref[...].astype(F32), (lanes, slots)).T
    lane = lax.broadcasted_iota(jnp.int32, (plane, lanes), 1)
    keep.wait()

    rank = a_ref.shape[0] // HOMES
    per = lanes // rank

    def shrink(j, c):
        zs = lax.rem(mz + nz - dz_of(j), nz)
        for i in range(NX):
            s = zs * NX + i

            @pl.when(s != me)
            def _():
                rep_copy(send, recv, send_sem, recv_sem, s, s).wait_recv()

        rows = recv[pl.ds(zs * NX, NX)].astype(F32).reshape(plane, depth).astype(BF16)
        got = lax.dot_general(rows, a_ref[...], (((1,), (1,)), ((), ())), preferred_element_type=F32)
        at = pl.ds(pl.multiple_of(zs * plane, plane), plane)
        wanted = adp[at, :].astype(jnp.int32)
        total = jnp.zeros((plane, lanes), F32)
        for n in range(got.shape[1] // lanes):
            total += jnp.where(
                wanted == n * per + lane // rank, got[:, n * lanes : (n + 1) * lanes], 0.0
            )
        fold[at, :] = total
        return c

    lax.fori_loop(0, nz, shrink, 0)

    low = jnp.sum(fold[...].T.reshape(per, rank, slots), axis=0)
    half = rank // 2
    for t in range(peers):
        y = t // 2
        if (y + 1) * lanes <= slots:
            rs_send[t] = low[half * (t % 2) : half * (t % 2 + 1), y * lanes : (y + 1) * lanes]
        else:
            rs_send[t] = jnp.zeros((half, lanes), F32)

    def rs_start(k, c):
        to = lax.rem(mt + k, peers)
        tp_copy(rs_send.at[to], rs_recv, rs_send_sem, rs_recv_sem, to, mt).start()
        return c

    lax.fori_loop(1, peers, rs_start, 0)
    rs_recv[mt] = rs_send[mt]

    def rs_wait(k, c):
        frm = lax.rem(mt + k, peers)
        tp_copy(rs_send.at[frm], rs_recv, rs_send_sem, rs_recv_sem, frm, frm).wait_recv()
        return c

    lax.fori_loop(1, peers, rs_wait, 0)
    ag[mt] = jnp.sum(rs_recv[...], axis=0)

    def ag_start(k, c):
        to = lax.rem(mt + k, peers)
        tp_copy(ag.at[mt], ag, ag_send_sem, ag_recv_sem, to, mt).start()
        return c

    lax.fori_loop(1, peers, ag_start, 0)

    def ag_wait(k, c):
        frm = lax.rem(mt + k, peers)
        tp_copy(ag.at[mt], ag, ag_send_sem, ag_recv_sem, frm, frm).wait_recv()
        return c

    lax.fori_loop(1, peers, ag_wait, 0)

    e = e_ref[...]
    e2 = jnp.concatenate([e, e], axis=1)
    used = slots // lanes
    lane2 = lax.broadcasted_iota(jnp.int32, (lanes, lanes), 1)
    for y in range(used):
        tile = jnp.concatenate([ag[2 * y], ag[2 * y + 1]] * per, axis=0).T
        wanted = adp[y * lanes : (y + 1) * lanes, :].astype(jnp.int32)
        parts = [
            jnp.where(wanted == n * per + lane2 // rank, tile, 0.0)
            for n in range(a_ref.shape[0] // lanes)
        ]
        spread = jnp.concatenate(parts, axis=1)
        hi = spread.astype(BF16)
        lo = (spread - hi.astype(F32)).astype(BF16)
        full = jnp.dot(hi, e2, preferred_element_type=F32) + jnp.dot(
            lo, e2, preferred_element_type=F32
        )
        top = full.astype(BF16).astype(F32)
        fold[y * lanes : (y + 1) * lanes, :] = jnp.where(lane2 < width, full, full - top)
    for s in range(groups):
        xsend[s] = fold[s * CAP : (s + 1) * CAP, :].astype(BF16)
    start_rep(xsend, xrecv, xsend_sem, xrecv_sem)
    keep2 = pltpu.make_async_copy(xsend.at[me], xrecv.at[me], local_sem.at[1])
    keep2.start()

    def base_wait(k, c):
        frm = lax.rem(mt + k, peers)
        tp_copy(bsend.at[frm], brecv, bsend_sem, brecv_sem, frm, frm).wait_recv()
        return c

    lax.fori_loop(1, peers, base_wait, 0)
    brecv[mt] = bsend[mt]
    base = jnp.sum(brecv[...], axis=0)
    column = jnp.broadcast_to(home_ref[...].astype(F32), (lanes, tok)).T[:, 0:1].astype(jnp.int32)
    unpack = (lax.broadcasted_iota(jnp.int32, (tok, slots), 1) == column).astype(F32).astype(BF16)
    place = lax.broadcasted_iota(jnp.int32, (slots, tok), 0) == slot_ref[...]
    place = place.astype(F32).astype(BF16)

    keep2.wait()
    finish_rep_recv(xsend, xrecv, xsend_sem, xrecv_sem)
    back = xrecv[...].astype(F32).reshape(slots, lanes).astype(BF16)
    extra = jnp.dot(unpack, back, preferred_element_type=F32).T
    total = (base + extra[:width] + extra[width:]).astype(BF16)
    final = lax.dot_general(place, total, (((1,), (1,)), ((), ())), preferred_element_type=F32)
    for s in range(groups):
        osend[s] = final[s * CAP : (s + 1) * CAP].astype(BF16)
    start_rep(osend, out_ref, osend_sem, orecv_sem)
    keep3 = pltpu.make_async_copy(osend.at[me], out_ref.at[me], local_sem.at[2])
    keep3.start()

    finish_rep_send(send, recv, send_sem, recv_sem)
    finish_rep_send(xsend, xrecv, xsend_sem, xrecv_sem)

    def tp_sent(k, c):
        to = lax.rem(mt + k, peers)
        tp_copy(bsend.at[to], brecv, bsend_sem, brecv_sem, to, mt).wait_send()
        tp_copy(rs_send.at[to], rs_recv, rs_send_sem, rs_recv_sem, to, mt).wait_send()
        tp_copy(ag.at[mt], ag, ag_send_sem, ag_recv_sem, to, mt).wait_send()
        return c

    lax.fori_loop(1, peers, tp_sent, 0)
    keep3.wait()
    finish_rep_send(osend, out_ref, osend_sem, orecv_sem)
    finish_rep_recv(osend, out_ref, osend_sem, orecv_sem)


def fused(groups, peers, requests, value_weight, shrink, expand, to_home, to_slot, adapter):
    tok, depth = requests.shape
    slots = groups * CAP
    width = expand.shape[1]
    vmem = pl.BlockSpec(memory_space=pltpu.VMEM)
    dma = pltpu.SemaphoreType.DMA
    return pl.pallas_call(
        functools.partial(fused_kernel, groups, peers),
        out_shape=jax.ShapeDtypeStruct((groups, CAP, width), BF16),
        in_specs=[vmem] * 7,
        out_specs=vmem,
        scratch_shapes=[
            pltpu.VMEM((groups, CAP, depth), BF16),
            pltpu.VMEM((groups, CAP, depth), BF16),
            pltpu.VMEM((peers, width, tok), F32),
            pltpu.VMEM((peers, width, tok), F32),
            pltpu.VMEM((slots, 128), F32),
            pltpu.VMEM((slots, 128), F32),
            pltpu.VMEM((peers, 8, 128), F32),
            pltpu.VMEM((peers, 8, 128), F32),
            pltpu.VMEM((peers, 8, 128), F32),
            pltpu.VMEM((groups, CAP, 128), BF16),
            pltpu.VMEM((groups, CAP, 128), BF16),
            pltpu.VMEM((groups, CAP, width), BF16),
            dma((groups,)),
            dma((groups,)),
            dma((peers,)),
            dma((peers,)),
            dma((peers,)),
            dma((peers,)),
            dma((peers,)),
            dma((peers,)),
            dma((groups,)),
            dma((groups,)),
            dma((groups,)),
            dma((groups,)),
            dma((3,)),
        ],
        compiler_params=pltpu.CompilerParams(
            collective_id=0, has_side_effects=True, vmem_limit_bytes=48 * 1024 * 1024
        ),
        name="fused",
    )(requests, value_weight, shrink, expand, to_home, to_slot, adapter)


def place_of(destination, adapter_ids, cache_lists, home_table, groups, home_count):
    adapters = home_table.shape[0]
    lists, cache_len = cache_lists.shape
    entry = (
        cache_lists.reshape(-1)[:, None] == jnp.arange(adapters, dtype=jnp.int32)[None, :]
    ).astype(jnp.bfloat16)
    table = jnp.stack([home_table // home_count, home_table % home_count], axis=1)
    listed = jnp.dot(entry, table.astype(jnp.bfloat16), preferred_element_type=jnp.float32)
    listed = listed.reshape(lists, cache_len * 2).T.astype(jnp.bfloat16)
    serving = (
        destination[None, :] == jnp.arange(lists, dtype=jnp.int32)[:, None]
    ).astype(jnp.bfloat16)
    rows = jnp.dot(listed, serving, preferred_element_type=jnp.float32)
    rows = rows.reshape(cache_len, 2, -1)
    chosen = adapter_ids[None, :] == jnp.arange(cache_len, dtype=jnp.int32)[:, None]
    both = jnp.sum(jnp.where(chosen[:, None, :], rows, 0.0), axis=0)
    home, local = both[0].astype(jnp.int32), both[1].astype(jnp.int32)
    tok = destination.shape[0] // groups
    home, local = home.reshape(groups, tok), local.reshape(groups, tok)
    member = home[None, :, :] == jnp.arange(groups, dtype=jnp.int32)[:, None, None]
    return home, local, rank_of(member, tok)


def rank_of(member, tok):
    order = jnp.arange(tok, dtype=jnp.int32)
    before = (order[:, None] < order[None, :]).astype(jnp.bfloat16)
    earlier = lax.dot_general(
        member.astype(jnp.bfloat16),
        before,
        (((member.ndim - 1,), (0,)), ((), ())),
        preferred_element_type=jnp.float32,
    )
    return jnp.sum(jnp.where(member, earlier, 0.0), axis=0).astype(jnp.int32)


def on_device(
    requests,
    value_weight,
    shrink_weight,
    expand_weight,
    destination,
    adapter_ids,
    cache_lists,
    home_table,
):
    groups = lax.axis_size("rep")
    me = lax.axis_index("rep")
    tok = requests.shape[0]
    home_count, rank, depth = shrink_weight.shape
    width = expand_weight.shape[2]
    home, local, place = place_of(
        destination, adapter_ids, cache_lists, home_table, groups, home_count
    )
    fits = jnp.max(place) < CAP

    def by_home_group(requests, value_weight, shrink_weight, expand_weight):
        slots = groups * CAP
        own = lambda a: lax.dynamic_index_in_dim(a, me, 0, keepdims=False)
        to_home = own(home) * CAP + own(place)
        here = (home == me)[:, None, :] & (
            place[:, None, :] == jnp.arange(CAP, dtype=jnp.int32)[None, :, None]
        )
        adapter = jnp.sum(jnp.where(here, local[:, None, :] + 1, 0), axis=2).reshape(slots) - 1
        serving = own(destination.reshape(groups, tok))
        order = rank_of(serving[None, :] == jnp.arange(groups, dtype=jnp.int32)[:, None], tok)
        to_slot = serving * CAP + order
        out = fused(
            groups,
            lax.axis_size("tp"),
            requests,
            value_weight,
            shrink_weight.reshape(home_count * rank, depth),
            expand_weight.reshape(home_count * rank, width),
            to_home[None, :],
            to_slot[None, :],
            adapter[None, :],
        )
        return out.reshape(slots, width)

    def any_input(requests, value_weight, shrink_weight, expand_weight):
        return by_serving_group(
            requests,
            value_weight,
            shrink_weight,
            expand_weight,
            destination,
            adapter_ids,
            cache_lists,
            home_table,
        )

    return lax.cond(
        fits, by_home_group, any_input, requests, value_weight, shrink_weight, expand_weight
    )


def solution(mesh):
    in_specs = (
        P("rep", "tp"),
        P("tp", None),
        P("rep", None, "tp"),
        P("rep", None, "tp"),
        P(),
        P(),
        P(),
        P(),
    )
    out_specs = P("rep", "tp")
    return jax.shard_map(
        on_device, mesh=mesh, in_specs=in_specs, out_specs=out_specs, check_vma=False
    )
```

```python
import functools

import jax
import jax.numpy as jnp
from jax import lax
from jax.experimental import pallas as pl
from jax.experimental.pallas import tpu as pltpu
from jax.sharding import PartitionSpec as P

PAIR = 2


def by_serving_group(
    requests,
    value_weight,
    shrink_weight,
    expand_weight,
    destination,
    adapter_ids,
    cache_lists,
    home_table,
):
    groups = lax.axis_size("rep")
    own_group = lax.axis_index("rep")
    tok_dev = requests.shape[0]
    rowcap = 3 * tok_dev // groups
    buffer_rows = groups * rowcap
    home_count = shrink_weight.shape[0]
    cache_len = cache_lists.shape[1]
    rank_width = shrink_weight.shape[1]
    width_out = expand_weight.shape[2]
    places = jnp.arange(cache_len, dtype=jnp.int32)
    blocks = destination.reshape(groups, tok_dev)
    targets = jnp.arange(groups, dtype=jnp.int32)
    member = (blocks[:, :, None] == targets[None, None, :]).astype(jnp.int32)
    earlier = jnp.sum(member * (jnp.cumsum(member, axis=1) - 1), axis=2)
    slot_all = targets[:, None] * rowcap + earlier
    own_slot = lax.dynamic_index_in_dim(
        blocks, own_group, 0, keepdims=False
    ) * rowcap + lax.dynamic_index_in_dim(earlier, own_group, 0, keepdims=False)
    send_rows = (
        jnp.zeros((buffer_rows, requests.shape[1]), requests.dtype).at[own_slot].set(requests)
    )
    arrived = lax.all_to_all(send_rows, "rep", split_axis=0, concat_axis=0, tiled=True)
    landing = jnp.where(blocks == own_group, slot_all, buffer_rows).reshape(-1)
    slot_place = jnp.full((buffer_rows,), -1, jnp.int32).at[landing].set(adapter_ids, mode="drop")
    selector = (slot_place[:, None] == places[None, :]).astype(jnp.float32)
    positions = home_table[cache_lists]
    home_group = positions // home_count
    local_slot = positions % home_count
    homed_here = home_group == own_group
    ranking = jnp.cumsum(homed_here.astype(jnp.int32), axis=1) - 1
    outgoing = jnp.where(homed_here, targets[:, None] * PAIR + ranking, groups * PAIR).reshape(-1)
    send_index = (
        jnp.zeros((groups * PAIR,), jnp.int32).at[outgoing].set(local_slot.reshape(-1), mode="drop")
    )
    send_valid = (
        jnp.zeros((groups * PAIR,), jnp.bfloat16).at[outgoing].set(jnp.bfloat16(1.0), mode="drop")
    )
    send_down = shrink_weight[send_index] * send_valid[:, None, None]
    send_up = expand_weight[send_index] * send_valid[:, None, None]
    got_down, got_up = (
        lax.all_to_all(send_down, "rep", split_axis=0, concat_axis=0, tiled=True),
        lax.all_to_all(send_up, "rep", split_axis=0, concat_axis=0, tiled=True),
    )
    own_homes = lax.dynamic_index_in_dim(home_group, own_group, 0, keepdims=False)
    same_before = jnp.sum(
        ((own_homes[None, :] == own_homes[:, None]) & (places[None, :] < places[:, None])).astype(
            jnp.int32
        ),
        axis=1,
    )
    fetch_index = own_homes * PAIR + same_before
    cached_down = got_down[fetch_index].reshape(cache_len * rank_width, -1)
    cached_up = got_up[fetch_index].reshape(cache_len * rank_width, width_out).astype(jnp.float32)
    shrunk_all = lax.dot_general(
        arrived, cached_down, (((1,), (1,)), ((), ())), preferred_element_type=jnp.float32
    )
    shrunk_part = jnp.sum(
        shrunk_all.reshape(buffer_rows, cache_len, rank_width) * selector[:, :, None], axis=1
    )
    shrunk = lax.psum(shrunk_part, "tp")
    spread_rows = (selector[:, :, None] * shrunk[:, None, :]).reshape(
        buffer_rows, cache_len * rank_width
    )
    expanded = jnp.dot(spread_rows, cached_up, precision=lax.Precision.HIGHEST)
    partial_all = jnp.dot(arrived, value_weight, preferred_element_type=jnp.float32)
    projected = lax.psum_scatter(partial_all, "tp", scatter_dimension=1, tiled=True)
    return (projected + expanded).astype(jnp.bfloat16)


MESH = pl.DeviceIdType.MESH
NX = 4
ROWS_Z = 64
ROWS_X = 128
BACK = 32
CHUNKS = 4
LANES = 128
F32, BF16, I32 = jnp.float32, jnp.bfloat16, jnp.int32


def hot(mask):
    return mask.astype(F32).astype(BF16)


def iota(shape, axis):
    return lax.broadcasted_iota(I32, shape, axis)


def nn(a, b):
    return jnp.dot(a, b, preferred_element_type=F32)


def nt(a, b):
    return lax.dot_general(a, b, (((1,), (1,)), ((), ())), preferred_element_type=F32)


def fused_kernel(
    groups,
    peers,
    x_ref,
    v_ref,
    a_ref,
    e_ref,
    dest_ref,
    aid_ref,
    list_ref,
    table_ref,
    out_ref,
    over_ref,
    send1,
    recv1,
    send2,
    recv2,
    bsend,
    brecv,
    acc,
    pick2t,
    pick2,
    upper,
    entries,
    home_s,
    local_s,
    slot1_s,
    slot2_s,
    mine_s,
    adp,
    back_pick,
    fold,
    rs_send,
    rs_recv,
    ag,
    xsend,
    xrecv,
    osend,
    send1_sem,
    recv1_sem,
    send2_sem,
    recv2_sem,
    bsend_sem,
    brecv_sem,
    rs_send_sem,
    rs_recv_sem,
    ag_send_sem,
    ag_recv_sem,
    xsend_sem,
    xrecv_sem,
    osend_sem,
    orecv_sem,
    local_sem,
):
    me = lax.axis_index("rep")
    mt = lax.axis_index("tp")
    my = mt // 2
    mz, mx = me // NX, me % NX
    nz = groups // NX
    tok, depth = x_ref.shape
    part = depth // CHUNKS
    homes = table_ref.shape[1]
    cache = list_ref.shape[1] // groups
    rank = a_ref.shape[0] // homes
    per = LANES // rank
    slots = NX * ROWS_X
    rowcap = out_ref.shape[1]

    barrier = pltpu.get_barrier_semaphore()

    def greet_rep(k, c):
        pl.semaphore_signal(
            barrier, inc=1, device_id={"rep": lax.rem(me + k, groups)}, device_id_type=MESH
        )
        return c

    def greet_tp(k, c):
        pl.semaphore_signal(
            barrier, inc=1, device_id={"tp": lax.rem(mt + k, peers)}, device_id_type=MESH
        )
        return c

    lax.fori_loop(1, groups, greet_rep, 0)
    lax.fori_loop(1, peers, greet_tp, 0)

    upper[...] = hot(iota((tok, tok), 0) < iota((tok, tok), 1))

    listed = list_ref[...]
    count = groups * cache
    table = table_ref[...]
    both = jnp.concatenate([hot_value(table // homes), hot_value(table % homes)], axis=0)
    major = iota((table.shape[0], count), 0) == listed // homes
    minor = iota((homes, count), 0) == listed % homes
    found = nn(both, hot(minor))
    of_home = jnp.sum(jnp.where(major, found[: table.shape[0]], 0.0), axis=0, keepdims=True)
    of_local = jnp.sum(jnp.where(major, found[table.shape[0] :], 0.0), axis=0, keepdims=True)
    owner = iota((groups, count), 1) // cache == iota((groups, count), 0)
    spread = jnp.concatenate(
        [jnp.where(owner, of_home, 0.0), jnp.where(owner, of_local, 0.0)], axis=0
    ).astype(BF16)
    entries[...] = nn(spread, hot(iota((count, cache), 0) % cache == iota((count, cache), 1))).astype(
        BF16
    )

    def look_up(dest, aid):
        n = dest.shape[1]
        rows = nn(entries[...], hot(iota((cache, n), 0) == aid))
        serve = iota((groups, n), 0) == dest
        home = jnp.sum(jnp.where(serve, rows[:groups], 0.0), axis=0, keepdims=True)
        local = jnp.sum(jnp.where(serve, rows[groups:], 0.0), axis=0, keepdims=True)
        return home.astype(I32), local.astype(I32)

    def rank_in(member):
        earlier = nn(hot(member), upper[...])
        return jnp.sum(jnp.where(member, earlier, 0.0), axis=0, keepdims=True).astype(I32)

    own_dest = dest_ref[pl.ds(me, 1), :]
    own_home, _ = look_up(own_dest, aid_ref[pl.ds(me, 1), :])
    own_plane = own_home // NX
    own_rank1 = rank_in(iota((nz, tok), 0) == own_plane)
    own_slot1 = jnp.where(own_rank1 < ROWS_Z, own_plane * ROWS_Z + own_rank1, -1)
    pick1 = hot(iota((nz * ROWS_Z, tok), 0) == own_slot1)

    def pack(c):
        rows = nn(pick1, x_ref[:, c * part : (c + 1) * part])
        send1[c] = rows.astype(BF16).reshape(nz, ROWS_Z, part)

    pack(0)
    pl.semaphore_wait(barrier, groups + peers - 2)

    def z_step(k):
        return lax.rem(nz // 2 + (1 - 2 * lax.rem(k, 2)) * ((k + 1) // 2) + nz, nz)

    def z_copy(c, to, frm):
        return pltpu.make_async_remote_copy(
            src_ref=send1.at[c, to],
            dst_ref=recv1.at[c, frm],
            send_sem=send1_sem.at[c, to],
            recv_sem=recv1_sem.at[c, frm],
            device_id={"rep": to * NX + mx},
            device_id_type=MESH,
        )

    def x_copy(c, to, frm):
        return pltpu.make_async_remote_copy(
            src_ref=send2.at[c, to],
            dst_ref=recv2.at[c, frm],
            send_sem=send2_sem.at[c, to],
            recv_sem=recv2_sem.at[c, frm],
            device_id={"rep": mz * NX + to},
            device_id_type=MESH,
        )

    def z_start(c):
        def body(k, w):
            z_copy(c, lax.rem(mz + z_step(k), nz), mz).start()
            return w

        lax.fori_loop(0, nz - 1, body, 0)

    z_start(0)
    for c in range(1, CHUNKS):
        pack(c)
        z_start(c)
    for c in range(CHUNKS):
        recv1[c, mz] = send1[c, mz]

    def target_of(k):
        z = lax.rem(mz + z_step(k // NX), nz)
        return z * NX + lax.rem(mx + 1 + lax.rem(k, NX), NX)

    def source_of(k):
        z = lax.rem(mz + nz - z_step(k // NX), nz)
        return z * NX + lax.rem(mx + 2 * NX - 1 - lax.rem(k, NX), NX)

    def rep_copy(src, dst, ssem, rsem, to, frm):
        return pltpu.make_async_remote_copy(
            src_ref=src.at[to],
            dst_ref=dst.at[frm],
            send_sem=ssem.at[to],
            recv_sem=rsem.at[frm],
            device_id={"rep": to},
            device_id_type=MESH,
        )

    def start_rep(src, dst, ssem, rsem):
        def body(k, w):
            rep_copy(src, dst, ssem, rsem, target_of(k), me).start()
            return w

        lax.fori_loop(0, groups - 1, body, 0)

    def finish_rep_send(src, dst, ssem, rsem):
        def body(k, w):
            rep_copy(src, dst, ssem, rsem, target_of(k), me).wait_send()
            return w

        lax.fori_loop(0, groups - 1, body, 0)

    def finish_rep_recv(src, dst, ssem, rsem):
        def body(k, w):
            s = source_of(k)
            rep_copy(src, dst, ssem, rsem, s, s).wait_recv()
            return w

        lax.fori_loop(0, groups - 1, body, 0)

    width = bsend.shape[1]
    step = 256
    for n in range(v_ref.shape[1] // step):
        bt = nn(x_ref[...], v_ref[:, n * step : (n + 1) * step]).T
        for i in range(step // width):
            bsend[n * (step // width) + i] = bt[i * width : (i + 1) * width]

    def base_copy(to, frm):
        return pltpu.make_async_remote_copy(
            src_ref=bsend.at[to],
            dst_ref=brecv.at[frm],
            send_sem=bsend_sem.at[to],
            recv_sem=brecv_sem.at[frm],
            device_id={"tp": to},
            device_id_type=MESH,
        )

    def base_start(k, w):
        base_copy(lax.rem(mt + k, peers), mt).start()
        return w

    lax.fori_loop(1, peers, base_start, 0)

    batch = 8
    counts = jnp.zeros((groups, LANES), F32)
    for q in range(groups // batch):
        ids = range(q * batch, (q + 1) * batch)
        dest = jnp.concatenate([dest_ref[g : g + 1, :] for g in ids], axis=1)
        aid = jnp.concatenate([aid_ref[g : g + 1, :] for g in ids], axis=1)
        home, local = look_up(dest, aid)
        for j, g in enumerate(ids):
            home_s[g : g + 1, :] = home[:, j * tok : (j + 1) * tok]
            local_s[g : g + 1, :] = local[:, j * tok : (j + 1) * tok]
        n = batch * tok
        counts += nn(
            hot(iota((groups, n), 0) == home),
            hot(iota((n, LANES), 0) // tok + q * batch == iota((n, LANES), 1)),
        )
    by_plane = nn(hot(iota((nz, groups), 0) == iota((nz, groups), 1) // NX), counts.astype(BF16))
    by_column = nn(
        counts.astype(BF16), hot(iota((LANES, LANES), 0) % NX == iota((LANES, LANES), 1))
    )
    over = (
        jnp.max(jnp.where(counts > BACK, 1.0, 0.0), axis=0, keepdims=True)
        + jnp.max(jnp.where(by_plane > ROWS_Z, 1.0, 0.0), axis=0, keepdims=True)
        + jnp.max(jnp.where(by_column > ROWS_X, 1.0, 0.0), axis=0, keepdims=True)
    )
    over_ref[...] = jnp.broadcast_to(over, over_ref.shape)

    homes_all = home_s[...]
    before = hot(
        (iota((groups, groups), 1) % NX == iota((groups, groups), 0) % NX)
        & (iota((groups, groups), 1) < iota((groups, groups), 0))
    )
    ones = jnp.ones((tok, LANES), BF16)

    def rank2(member):
        picked = hot(member)
        earlier = nn(picked, upper[...])
        total = nn(before, nn(picked, ones).astype(BF16))
        return (earlier + jnp.concatenate([total] * (tok // LANES), axis=1)).astype(I32), earlier

    here = homes_all // NX == mz
    place1 = nn(hot(here), upper[...]).astype(I32)
    slot1_s[...] = jnp.where(here & (place1 < ROWS_Z), place1, -1)
    target = jnp.full((groups, tok), -1, I32)
    for i in range(NX):
        member = homes_all == mz * NX + i
        place, _ = rank2(member)
        target = jnp.where(member & (place < ROWS_X), i * ROWS_X + place, target)
    slot2_s[...] = target
    member = homes_all == me
    place, back_rank = rank2(member)
    mine_s[0] = jnp.where(member & (place < ROWS_X), place, -1)
    mine_s[1] = jnp.where(member, back_rank.astype(I32), -1)

    def route(z, w):
        g = z * NX + mx
        first = hot(iota((ROWS_Z, tok), 0) == slot1_s[pl.ds(g, 1), :])
        second = hot(iota((slots, tok), 0) == slot2_s[pl.ds(g, 1), :])
        pick2t[pl.ds(pl.multiple_of(z * ROWS_Z, ROWS_Z), ROWS_Z), :] = nt(first, second)
        return w

    lax.fori_loop(0, nz, route, 0)
    pick2[...] = pick2t[...].T.astype(BF16)

    adp[...] = jnp.zeros_like(adp)
    acc[...] = jnp.zeros_like(acc)

    def shrink(c):
        def wait_x(k, w):
            frm = lax.rem(mx + k, NX)
            x_copy(c, frm, frm).wait_recv()
            return w

        lax.fori_loop(1, NX, wait_x, 0)
        rows = recv2[c].reshape(slots, part)
        acc[...] += nt(rows, a_ref[:, c * part : (c + 1) * part])

    def stage(c):
        def wait_z(k, w):
            frm = lax.rem(mz + nz - z_step(k), nz)
            z_copy(c, frm, frm).wait_recv()
            return w

        lax.fori_loop(0, nz - 1, wait_z, 0)
        rows = nn(pick2[...], recv1[c].reshape(nz * ROWS_Z, part))
        send2[c] = rows.astype(BF16).reshape(NX, ROWS_X, part)

        def send_x(k, w):
            x_copy(c, lax.rem(mx + k, NX), mx).start()
            return w

        lax.fori_loop(1, NX, send_x, 0)
        recv2[c, mx] = send2[c, mx]

    def homed(g, w):
        column = lax.rem(g, NX)
        second = hot(iota((ROWS_X, tok), 0) == mine_s[0, pl.ds(g, 1), :])
        back = hot(iota((BACK, tok), 0) == mine_s[1, pl.ds(g, 1), :])
        value = (local_s[pl.ds(g, 1), :] + 1).astype(F32).astype(BF16)
        at = pl.ds(pl.multiple_of(column * ROWS_X, ROWS_X), ROWS_X)
        adp[at, :] += nt(second, jnp.broadcast_to(value, (LANES, tok)))
        back_pick[column, g // NX] = nt(back, second)
        return w

    quarter = groups // CHUNKS
    for c in range(CHUNKS):
        stage(c)
        lax.fori_loop(c * quarter, (c + 1) * quarter, homed, 0)
        if c:
            shrink(c - 1)
    column = jnp.broadcast_to(own_home.astype(F32), (LANES, tok))
    own_back = rank_in(iota((groups, tok), 0) == own_home)
    own_back = jnp.where(own_back < BACK, own_home * BACK + own_back, -1)
    column = jnp.broadcast_to(own_back.astype(F32), (LANES, tok)).T[:, 0:1].astype(I32)
    unpack = hot(iota((tok, groups * BACK), 1) == column)
    own_out = own_dest * rowcap + rank_in(iota((groups, tok), 0) == own_dest)
    place_out = hot(iota((groups * rowcap, tok), 0) == own_out)
    shrink(CHUNKS - 1)

    wanted = adp[...].astype(I32) - 1
    lane = iota((slots, LANES), 1) // rank
    folded = jnp.zeros((slots, LANES), F32)
    for n in range(homes // per):
        folded += jnp.where(wanted == n * per + lane, acc[:, n * LANES : (n + 1) * LANES], 0.0)

    low = jnp.sum(folded.T.reshape(per, rank, slots), axis=0)
    tiles = peers // 2
    half = rank // 2
    for t in range(tiles):
        rs_send[t] = low[
            half * (t % 2) : half * (t % 2 + 1), (t // 2) * LANES : (t // 2 + 1) * LANES
        ]

    def rs_copy(tile, frm):
        return pltpu.make_async_remote_copy(
            src_ref=rs_send.at[tile],
            dst_ref=rs_recv.at[frm],
            send_sem=rs_send_sem.at[tile],
            recv_sem=rs_recv_sem.at[frm],
            device_id={"tp": 2 * tile},
            device_id_type=MESH,
        )

    def ag_copy(tile, to):
        return pltpu.make_async_remote_copy(
            src_ref=ag.at[tile],
            dst_ref=ag.at[tile],
            send_sem=ag_send_sem.at[to],
            recv_sem=ag_recv_sem.at[tile],
            device_id={"tp": to},
            device_id_type=MESH,
        )

    def rs_start(k, w):
        tile = lax.rem(my + tiles // 2 + k, tiles)

        @pl.when(2 * tile != mt)
        def _():
            rs_copy(tile, mt).start()

        return w

    lax.fori_loop(0, tiles, rs_start, 0)

    @pl.when(lax.rem(mt, 2) == 0)
    def _():
        rs_recv[mt] = rs_send[my]

        def rs_wait(k, w):
            rs_copy(my, lax.rem(mt + k, peers)).wait_recv()
            return w

        lax.fori_loop(1, peers, rs_wait, 0)
        ag[my] = jnp.sum(rs_recv[...], axis=0)

        def ag_start(k, w):
            ag_copy(my, lax.rem(mt + k, peers)).start()
            return w

        lax.fori_loop(1, peers, ag_start, 0)

    def ag_wait(k, w):
        tile = lax.rem(my + k, tiles)

        @pl.when(2 * tile != mt)
        def _():
            ag_copy(tile, mt).wait_recv()

        return w

    lax.fori_loop(0, tiles, ag_wait, 0)

    e2 = jnp.concatenate([e_ref[...], e_ref[...]], axis=1)
    lane1 = iota((ROWS_X, LANES), 1)
    for y in range(NX):
        tile = jnp.concatenate([ag[2 * y], ag[2 * y + 1]] * per, axis=0).T
        chosen = wanted[y * ROWS_X : (y + 1) * ROWS_X]
        spread = jnp.concatenate(
            [
                jnp.where(chosen == n * per + lane1 // rank, tile, 0.0)
                for n in range(homes // per)
            ],
            axis=1,
        )
        hi = spread.astype(BF16)
        lo = (spread - hi.astype(F32)).astype(BF16)
        full = nn(hi, e2) + nn(lo, e2)
        top = full.astype(BF16).astype(F32)
        pair = jnp.where(lane1 < width, full, full - top).astype(BF16)
        sel = back_pick[y].reshape(nz * BACK, LANES).astype(BF16)
        rows = nn(sel, pair)
        for z in range(nz):
            xsend[z * NX + y] = rows[z * BACK : (z + 1) * BACK].astype(BF16)
    start_rep(xsend, xrecv, xsend_sem, xrecv_sem)
    keep2 = pltpu.make_async_copy(xsend.at[me], xrecv.at[me], local_sem.at[0])
    keep2.start()

    def base_wait(k, w):
        frm = lax.rem(mt + k, peers)
        base_copy(frm, frm).wait_recv()
        return w

    lax.fori_loop(1, peers, base_wait, 0)
    brecv[mt] = bsend[mt]
    base = jnp.sum(brecv[...], axis=0)

    keep2.wait()
    finish_rep_recv(xsend, xrecv, xsend_sem, xrecv_sem)
    extra = nn(unpack, xrecv[...].reshape(groups * BACK, LANES)).T
    total = (base + extra[:width] + extra[width:]).astype(BF16)
    final = nt(place_out, total)
    for s in range(groups):
        osend[s] = final[s * rowcap : (s + 1) * rowcap].astype(BF16)
    start_rep(osend, out_ref, osend_sem, orecv_sem)
    keep3 = pltpu.make_async_copy(osend.at[me], out_ref.at[me], local_sem.at[1])
    keep3.start()

    for c in range(CHUNKS):

        def z_sent(k, w):
            z_copy(c, lax.rem(mz + z_step(k), nz), mz).wait_send()
            return w

        def x_sent(k, w):
            x_copy(c, lax.rem(mx + k, NX), mx).wait_send()
            return w

        lax.fori_loop(0, nz - 1, z_sent, 0)
        lax.fori_loop(1, NX, x_sent, 0)

    def base_sent(k, w):
        base_copy(lax.rem(mt + k, peers), mt).wait_send()
        return w

    lax.fori_loop(1, peers, base_sent, 0)

    def rs_sent(k, w):
        tile = lax.rem(my + k, tiles)

        @pl.when(2 * tile != mt)
        def _():
            rs_copy(tile, mt).wait_send()

        return w

    lax.fori_loop(0, tiles, rs_sent, 0)

    @pl.when(lax.rem(mt, 2) == 0)
    def _():
        def ag_sent(k, w):
            ag_copy(my, lax.rem(mt + k, peers)).wait_send()
            return w

        lax.fori_loop(1, peers, ag_sent, 0)

    finish_rep_send(xsend, xrecv, xsend_sem, xrecv_sem)
    keep3.wait()
    finish_rep_send(osend, out_ref, osend_sem, orecv_sem)
    finish_rep_recv(osend, out_ref, osend_sem, orecv_sem)


def hot_value(a):
    return a.astype(F32).astype(BF16)


def fused(groups, peers, requests, value_weight, shrink, expand, dest, aid, lists, table):
    tok, depth = requests.shape
    width = expand.shape[1]
    rowcap = 3 * tok // groups
    nz, part, slots = groups // NX, depth // CHUNKS, NX * ROWS_X
    vmem = pl.BlockSpec(memory_space=pltpu.VMEM)
    dma = pltpu.SemaphoreType.DMA
    return pl.pallas_call(
        functools.partial(fused_kernel, groups, peers),
        out_shape=[
            jax.ShapeDtypeStruct((groups, rowcap, width), BF16),
            jax.ShapeDtypeStruct((8, LANES), F32),
        ],
        in_specs=[vmem] * 8,
        out_specs=[vmem, vmem],
        scratch_shapes=[
            pltpu.VMEM((CHUNKS, nz, ROWS_Z, part), BF16),
            pltpu.VMEM((CHUNKS, nz, ROWS_Z, part), BF16),
            pltpu.VMEM((CHUNKS, NX, ROWS_X, part), BF16),
            pltpu.VMEM((CHUNKS, NX, ROWS_X, part), BF16),
            pltpu.VMEM((peers, width, tok), F32),
            pltpu.VMEM((peers, width, tok), F32),
            pltpu.VMEM((slots, shrink.shape[0]), F32),
            pltpu.VMEM((nz * ROWS_Z, slots), F32),
            pltpu.VMEM((slots, nz * ROWS_Z), BF16),
            pltpu.VMEM((tok, tok), BF16),
            pltpu.VMEM((2 * groups, lists.shape[1] // groups), BF16),
            pltpu.VMEM((groups, tok), I32),
            pltpu.VMEM((groups, tok), I32),
            pltpu.VMEM((groups, tok), I32),
            pltpu.VMEM((groups, tok), I32),
            pltpu.VMEM((2, groups, tok), I32),
            pltpu.VMEM((slots, LANES), F32),
            pltpu.VMEM((NX, nz, BACK, LANES), F32),
            pltpu.VMEM((slots, LANES), F32),
            pltpu.VMEM((peers // 2, 8, LANES), F32),
            pltpu.VMEM((peers, 8, LANES), F32),
            pltpu.VMEM((peers // 2, 8, LANES), F32),
            pltpu.VMEM((groups, BACK, LANES), BF16),
            pltpu.VMEM((groups, BACK, LANES), BF16),
            pltpu.VMEM((groups, rowcap, width), BF16),
            dma((CHUNKS, nz)),
            dma((CHUNKS, nz)),
            dma((CHUNKS, NX)),
            dma((CHUNKS, NX)),
            dma((peers,)),
            dma((peers,)),
            dma((peers // 2,)),
            dma((peers,)),
            dma((peers,)),
            dma((peers // 2,)),
            dma((groups,)),
            dma((groups,)),
            dma((groups,)),
            dma((groups,)),
            dma((2,)),
        ],
        compiler_params=pltpu.CompilerParams(
            collective_id=0, has_side_effects=True, vmem_limit_bytes=48 * 1024 * 1024
        ),
        name="fused",
    )(requests, value_weight, shrink, expand, dest, aid, lists, table)


def on_device(
    requests,
    value_weight,
    shrink_weight,
    expand_weight,
    destination,
    adapter_ids,
    cache_lists,
    home_table,
):
    groups = lax.axis_size("rep")
    tok = requests.shape[0]
    home_count, rank, depth = shrink_weight.shape
    width = expand_weight.shape[2]
    out, over = fused(
        groups,
        lax.axis_size("tp"),
        requests,
        value_weight,
        shrink_weight.reshape(home_count * rank, depth),
        expand_weight.reshape(home_count * rank, width),
        destination.reshape(groups, tok),
        adapter_ids.reshape(groups, tok),
        cache_lists.reshape(1, -1),
        home_table.reshape(-1, home_count),
    )
    out = out.reshape(-1, width)

    def any_input(out):
        return by_serving_group(
            requests,
            value_weight,
            shrink_weight,
            expand_weight,
            destination,
            adapter_ids,
            cache_lists,
            home_table,
        )

    return lax.cond(jnp.max(over) > 0.0, any_input, lambda out: out, out)


def solution(mesh):
    in_specs = (
        P("rep", "tp"),
        P("tp", None),
        P("rep", None, "tp"),
        P("rep", None, "tp"),
        P(),
        P(),
        P(),
        P(),
    )
    out_specs = P("rep", "tp")
    return jax.shard_map(
        on_device, mesh=mesh, in_specs=in_specs, out_specs=out_specs, check_vma=False
    )
```

```python
import functools

import jax
import jax.numpy as jnp
from jax import lax
from jax.experimental import pallas as pl
from jax.experimental.pallas import tpu as pltpu
from jax.sharding import PartitionSpec as P

PAIR = 2


def by_serving_group(
    requests,
    value_weight,
    shrink_weight,
    expand_weight,
    destination,
    adapter_ids,
    cache_lists,
    home_table,
):
    groups = lax.axis_size("rep")
    own_group = lax.axis_index("rep")
    tok_dev = requests.shape[0]
    rowcap = 3 * tok_dev // groups
    buffer_rows = groups * rowcap
    home_count = shrink_weight.shape[0]
    cache_len = cache_lists.shape[1]
    rank_width = shrink_weight.shape[1]
    width_out = expand_weight.shape[2]
    places = jnp.arange(cache_len, dtype=jnp.int32)
    blocks = destination.reshape(groups, tok_dev)
    targets = jnp.arange(groups, dtype=jnp.int32)
    member = (blocks[:, :, None] == targets[None, None, :]).astype(jnp.int32)
    earlier = jnp.sum(member * (jnp.cumsum(member, axis=1) - 1), axis=2)
    slot_all = targets[:, None] * rowcap + earlier
    own_slot = lax.dynamic_index_in_dim(
        blocks, own_group, 0, keepdims=False
    ) * rowcap + lax.dynamic_index_in_dim(earlier, own_group, 0, keepdims=False)
    send_rows = (
        jnp.zeros((buffer_rows, requests.shape[1]), requests.dtype).at[own_slot].set(requests)
    )
    arrived = lax.all_to_all(send_rows, "rep", split_axis=0, concat_axis=0, tiled=True)
    landing = jnp.where(blocks == own_group, slot_all, buffer_rows).reshape(-1)
    slot_place = jnp.full((buffer_rows,), -1, jnp.int32).at[landing].set(adapter_ids, mode="drop")
    selector = (slot_place[:, None] == places[None, :]).astype(jnp.float32)
    positions = home_table[cache_lists]
    home_group = positions // home_count
    local_slot = positions % home_count
    homed_here = home_group == own_group
    ranking = jnp.cumsum(homed_here.astype(jnp.int32), axis=1) - 1
    outgoing = jnp.where(homed_here, targets[:, None] * PAIR + ranking, groups * PAIR).reshape(-1)
    send_index = (
        jnp.zeros((groups * PAIR,), jnp.int32).at[outgoing].set(local_slot.reshape(-1), mode="drop")
    )
    send_valid = (
        jnp.zeros((groups * PAIR,), jnp.bfloat16).at[outgoing].set(jnp.bfloat16(1.0), mode="drop")
    )
    send_down = shrink_weight[send_index] * send_valid[:, None, None]
    send_up = expand_weight[send_index] * send_valid[:, None, None]
    got_down, got_up = (
        lax.all_to_all(send_down, "rep", split_axis=0, concat_axis=0, tiled=True),
        lax.all_to_all(send_up, "rep", split_axis=0, concat_axis=0, tiled=True),
    )
    own_homes = lax.dynamic_index_in_dim(home_group, own_group, 0, keepdims=False)
    same_before = jnp.sum(
        ((own_homes[None, :] == own_homes[:, None]) & (places[None, :] < places[:, None])).astype(
            jnp.int32
        ),
        axis=1,
    )
    fetch_index = own_homes * PAIR + same_before
    cached_down = got_down[fetch_index].reshape(cache_len * rank_width, -1)
    cached_up = got_up[fetch_index].reshape(cache_len * rank_width, width_out).astype(jnp.float32)
    shrunk_all = lax.dot_general(
        arrived, cached_down, (((1,), (1,)), ((), ())), preferred_element_type=jnp.float32
    )
    shrunk_part = jnp.sum(
        shrunk_all.reshape(buffer_rows, cache_len, rank_width) * selector[:, :, None], axis=1
    )
    shrunk = lax.psum(shrunk_part, "tp")
    spread_rows = (selector[:, :, None] * shrunk[:, None, :]).reshape(
        buffer_rows, cache_len * rank_width
    )
    expanded = jnp.dot(spread_rows, cached_up, precision=lax.Precision.HIGHEST)
    partial_all = jnp.dot(arrived, value_weight, preferred_element_type=jnp.float32)
    projected = lax.psum_scatter(partial_all, "tp", scatter_dimension=1, tiled=True)
    return (projected + expanded).astype(jnp.bfloat16)


MESH = pl.DeviceIdType.MESH
NX = 4
ROWS_Z = 64
ROWS_X = 128
BACK = 32
CHUNKS = 4
LANES = 128
F32, BF16, I32 = jnp.float32, jnp.bfloat16, jnp.int32


def hot(mask):
    return mask.astype(F32).astype(BF16)


def iota(shape, axis):
    return lax.broadcasted_iota(I32, shape, axis)


def nn(a, b):
    return jnp.dot(a, b, preferred_element_type=F32)


def nt(a, b):
    return lax.dot_general(a, b, (((1,), (1,)), ((), ())), preferred_element_type=F32)


def fused_kernel(
    groups,
    peers,
    x_ref,
    v_ref,
    a_ref,
    e_ref,
    dest_ref,
    aid_ref,
    list_ref,
    table_ref,
    out_ref,
    over_ref,
    send1,
    recv1,
    send2,
    recv2,
    bsend,
    brecv,
    acc,
    pick2t,
    pick2,
    upper,
    entries,
    home_s,
    local_s,
    slot1_s,
    slot2_s,
    mine_s,
    adp,
    back_pick,
    rs_send,
    rs_recv,
    tile_sum,
    ag,
    xsend,
    xrecv,
    osend,
    send1_sem,
    recv1_sem,
    send2_sem,
    recv2_sem,
    bsend_sem,
    brecv_sem,
    rs_send_sem,
    rs_recv_sem,
    ag_send_sem,
    ag_recv_sem,
    xsend_sem,
    xrecv_sem,
    osend_sem,
    orecv_sem,
):
    me = lax.axis_index("rep")
    mt = lax.axis_index("tp")
    my = mt // 2
    mz, mx = me // NX, me % NX
    nz = groups // NX
    tok, depth = x_ref.shape
    part = depth // CHUNKS
    cache = list_ref.shape[1]
    homes = table_ref.shape[0] * LANES // groups
    rank = a_ref.shape[0] // homes
    rows_of = tok // LANES
    per = LANES // rank
    slots = NX * ROWS_X
    rowcap = out_ref.shape[1]

    barrier = pltpu.get_barrier_semaphore()

    def z_of(d):
        return lax.rem(mz + d, nz)

    def x_of(d):
        return lax.rem(mx + d, NX)

    def tp_of(d):
        return lax.rem(mt + d, peers)

    def greet(**where):
        pl.semaphore_signal(barrier, inc=1, device_id=where, device_id_type=MESH)

    z_steps = sorted(range(1, nz), key=lambda d: -min(d, nz - d))
    for d in z_steps:
        greet(rep=z_of(d) * NX + mx)
    for d in range(1, peers):
        greet(tp=tp_of(d))
    for d in range(1, NX):
        greet(rep=mz * NX + x_of(d))

    upper[...] = hot(iota((tok, tok), 0) < iota((tok, tok), 1))

    count = groups * cache
    lists = list_ref[...]
    place_of = hot(iota((cache, count), 0) == iota((cache, count), 1) % cache)
    owner = iota((groups, count), 1) // cache == iota((groups, count), 0)
    high = jnp.where(owner, nn(hot_value(lists // LANES), place_of), 0.0)
    low = jnp.where(owner, nn(hot_value(lists % LANES), place_of), 0.0)
    high = jnp.sum(high, axis=0, keepdims=True).astype(I32)
    low = jnp.sum(low, axis=0, keepdims=True).astype(I32)
    table = table_ref[...]
    both = jnp.concatenate([hot_value(table // homes), hot_value(table % homes)], axis=0)
    major = iota((table.shape[0], count), 0) == high
    minor = iota((LANES, count), 0) == low
    found = nn(both, hot(minor))
    of_home = jnp.sum(jnp.where(major, found[: table.shape[0]], 0.0), axis=0, keepdims=True)
    of_local = jnp.sum(jnp.where(major, found[table.shape[0] :], 0.0), axis=0, keepdims=True)
    spread = jnp.concatenate(
        [jnp.where(owner, of_home, 0.0), jnp.where(owner, of_local, 0.0)], axis=0
    ).astype(BF16)
    entries[...] = nn(spread, hot(iota((count, cache), 0) % cache == iota((count, cache), 1))).astype(
        BF16
    )

    def look_up(dest, aid):
        n = dest.shape[1]
        rows = nn(entries[...], hot(iota((cache, n), 0) == aid))
        serve = iota((groups, n), 0) == dest
        home = jnp.sum(jnp.where(serve, rows[:groups], 0.0), axis=0, keepdims=True)
        local = jnp.sum(jnp.where(serve, rows[groups:], 0.0), axis=0, keepdims=True)
        return home.astype(I32), local.astype(I32)

    def rank_in(member):
        earlier = nn(hot(member), upper[...])
        return jnp.sum(jnp.where(member, earlier, 0.0), axis=0, keepdims=True).astype(I32)

    def own(ref):
        return jnp.concatenate([ref[pl.ds(rows_of * me + i, 1), :] for i in range(rows_of)], axis=1)

    own_dest = own(dest_ref)
    own_home, _ = look_up(own_dest, own(aid_ref))
    own_plane = own_home // NX
    own_rank1 = rank_in(iota((nz, tok), 0) == own_plane)
    own_slot1 = jnp.where(own_rank1 < ROWS_Z, own_plane * ROWS_Z + own_rank1, -1)
    pick1 = hot(iota((nz * ROWS_Z, tok), 0) == own_slot1)

    def pack(c):
        rows = nn(pick1, x_ref[:, c * part : (c + 1) * part])
        send1[c] = rows.astype(BF16).reshape(nz, ROWS_Z, part)

    pack(0)
    pl.semaphore_wait(barrier, nz + NX + peers - 3)

    def arrived(buffer, sem):
        pltpu.make_async_copy(buffer, buffer, sem).wait()

    def push(src, dst, ssem, rsem, **where):
        pltpu.make_async_remote_copy(
            src_ref=src,
            dst_ref=dst,
            send_sem=ssem,
            recv_sem=rsem,
            device_id=where,
            device_id_type=MESH,
        ).start()

    def z_start(c):
        for d in z_steps:
            to = z_of(d)
            push(
                send1.at[c, to],
                recv1.at[c, mz],
                send1_sem.at[c],
                recv1_sem.at[c],
                rep=to * NX + mx,
            )
        pltpu.make_async_copy(send1.at[c, mz], recv1.at[c, mz], recv1_sem.at[c]).start()

    z_start(0)
    for c in range(1, CHUNKS):
        pack(c)
        z_start(c)

    def to_groups(src, dst, ssem, rsem):
        for dz in z_steps + [0]:
            for dx in range(NX):
                if dz or dx:
                    to = z_of(dz) * NX + x_of(dx)
                    push(src.at[to], dst.at[me], ssem.at[0], rsem.at[0], rep=to)
        pltpu.make_async_copy(src.at[me], dst.at[me], rsem.at[0]).start()

    width = bsend.shape[1]
    step = 256
    for n in range(v_ref.shape[1] // step):
        bt = nn(x_ref[...], v_ref[:, n * step : (n + 1) * step]).T
        for i in range(step // width):
            bsend[n * (step // width) + i] = bt[i * width : (i + 1) * width]

    for d in range(1, peers):
        to = tp_of(d)
        push(bsend.at[to], brecv.at[mt], bsend_sem.at[0], brecv_sem.at[0], tp=to)
    pltpu.make_async_copy(bsend.at[mt], brecv.at[mt], brecv_sem.at[0]).start()

    batch = 8
    counts = jnp.zeros((groups, LANES), F32)
    for q in range(groups // batch):
        ids = range(q * batch, (q + 1) * batch)
        lines = range(q * batch * rows_of, (q + 1) * batch * rows_of)
        dest = jnp.concatenate([dest_ref[r : r + 1, :] for r in lines], axis=1)
        aid = jnp.concatenate([aid_ref[r : r + 1, :] for r in lines], axis=1)
        home, local = look_up(dest, aid)
        for j, g in enumerate(ids):
            home_s[g : g + 1, :] = home[:, j * tok : (j + 1) * tok]
            local_s[g : g + 1, :] = local[:, j * tok : (j + 1) * tok]
        n = batch * tok
        counts += nn(
            hot(iota((groups, n), 0) == home),
            hot(iota((n, LANES), 0) // tok + q * batch == iota((n, LANES), 1)),
        )
    by_plane = nn(hot(iota((nz, groups), 0) == iota((nz, groups), 1) // NX), counts.astype(BF16))
    by_column = nn(
        counts.astype(BF16), hot(iota((LANES, LANES), 0) % NX == iota((LANES, LANES), 1))
    )
    over = (
        jnp.max(jnp.where(counts > BACK, 1.0, 0.0), axis=0, keepdims=True)
        + jnp.max(jnp.where(by_plane > ROWS_Z, 1.0, 0.0), axis=0, keepdims=True)
        + jnp.max(jnp.where(by_column > ROWS_X, 1.0, 0.0), axis=0, keepdims=True)
    )
    over_ref[0, 0] = jnp.max(over).astype(I32)

    homes_all = home_s[...]
    before = hot(
        (iota((groups, groups), 1) % NX == iota((groups, groups), 0) % NX)
        & (iota((groups, groups), 1) < iota((groups, groups), 0))
    )
    ones = jnp.ones((tok, LANES), BF16)

    def rank2(member):
        picked = hot(member)
        earlier = nn(picked, upper[...])
        total = nn(before, nn(picked, ones).astype(BF16))
        return (earlier + jnp.concatenate([total] * (tok // LANES), axis=1)).astype(I32), earlier

    here = homes_all // NX == mz
    place1 = nn(hot(here), upper[...]).astype(I32)
    slot1_s[...] = jnp.where(here & (place1 < ROWS_Z), place1, -1)
    target = jnp.full((groups, tok), -1, I32)
    for i in range(NX):
        member = homes_all == mz * NX + i
        place, _ = rank2(member)
        target = jnp.where(member & (place < ROWS_X), i * ROWS_X + place, target)
    slot2_s[...] = target
    member = homes_all == me
    place, back_rank = rank2(member)
    mine_s[0] = jnp.where(member & (place < ROWS_X), place, -1)
    mine_s[1] = jnp.where(member, back_rank.astype(I32), -1)

    def route(z, w):
        g = z * NX + mx
        first = hot(iota((ROWS_Z, tok), 0) == slot1_s[pl.ds(g, 1), :])
        second = hot(iota((slots, tok), 0) == slot2_s[pl.ds(g, 1), :])
        pick2t[pl.ds(pl.multiple_of(z * ROWS_Z, ROWS_Z), ROWS_Z), :] = nt(first, second)
        return w

    lax.fori_loop(0, nz, route, 0)
    pick2[...] = pick2t[...].T.astype(BF16)

    adp[...] = jnp.zeros_like(adp)
    acc[...] = jnp.zeros_like(acc)

    def shrink(c):
        arrived(recv2.at[c], recv2_sem.at[c])
        rows = recv2[c].reshape(slots, part)
        acc[...] += nt(rows, a_ref[:, c * part : (c + 1) * part])

    def stage(c):
        arrived(recv1.at[c], recv1_sem.at[c])
        rows = nn(pick2[...], recv1[c].reshape(nz * ROWS_Z, part))
        send2[c] = rows.astype(BF16).reshape(NX, ROWS_X, part)

        for d in range(1, NX):
            to = x_of(d)
            push(
                send2.at[c, to],
                recv2.at[c, mx],
                send2_sem.at[c],
                recv2_sem.at[c],
                rep=mz * NX + to,
            )
        pltpu.make_async_copy(send2.at[c, mx], recv2.at[c, mx], recv2_sem.at[c]).start()

    def homed(g, w):
        column = lax.rem(g, NX)
        second = hot(iota((ROWS_X, tok), 0) == mine_s[0, pl.ds(g, 1), :])
        back = hot(iota((BACK, tok), 0) == mine_s[1, pl.ds(g, 1), :])
        value = (local_s[pl.ds(g, 1), :] + 1).astype(F32).astype(BF16)
        at = pl.ds(pl.multiple_of(column * ROWS_X, ROWS_X), ROWS_X)
        adp[at, :] += nt(second, jnp.broadcast_to(value, (LANES, tok)))
        back_pick[column, g // NX] = nt(back, second)
        return w

    quarter = groups // CHUNKS
    for c in range(CHUNKS):
        stage(c)
        lax.fori_loop(c * quarter, (c + 1) * quarter, homed, 0)
        if c:
            shrink(c - 1)
    own_back = rank_in(iota((groups, tok), 0) == own_home)
    own_back = jnp.where(own_back < BACK, own_home * BACK + own_back, -1)
    column = jnp.broadcast_to(own_back.astype(F32), (LANES, tok)).T[:, 0:1].astype(I32)
    unpack = hot(iota((tok, groups * BACK), 1) == column)
    own_out = own_dest * rowcap + rank_in(iota((groups, tok), 0) == own_dest)
    place_out = hot(iota((groups * rowcap, tok), 0) == own_out)
    shrink(CHUNKS - 1)

    wanted = adp[...].astype(I32) - 1
    lane = iota((slots, LANES), 1) // rank
    folded = jnp.zeros((slots, LANES), F32)
    for n in range(homes // per):
        folded += jnp.where(wanted == n * per + lane, acc[:, n * LANES : (n + 1) * LANES], 0.0)

    low = jnp.sum(folded.T.reshape(per, rank, slots), axis=0)
    tiles = peers // 2
    half = rank // 2
    for t in range(tiles):
        rs_send[t] = low[
            half * (t % 2) : half * (t % 2 + 1), (t // 2) * LANES : (t // 2 + 1) * LANES
        ]

    first_core = lax.rem(mt, 2) == 0
    for d in sorted(range(1, tiles), key=lambda d: -min(d, tiles - d)):
        tile = lax.rem(my + d, tiles)
        push(rs_send.at[tile], rs_recv.at[mt], rs_send_sem.at[0], rs_recv_sem.at[0], tp=2 * tile)

    @pl.when(jnp.logical_not(first_core))
    def _():
        push(rs_send.at[my], rs_recv.at[mt], rs_send_sem.at[0], rs_recv_sem.at[0], tp=2 * my)

    @pl.when(first_core)
    def _():
        pltpu.make_async_copy(rs_send.at[my], rs_recv.at[mt], rs_recv_sem.at[0]).start()
        arrived(rs_recv, rs_recv_sem.at[0])
        tile_sum[...] = jnp.sum(rs_recv[...], axis=0)
        for d in sorted(range(1, peers), key=lambda d: -min(d, peers - d)):
            push(tile_sum, ag.at[my], ag_send_sem.at[0], ag_recv_sem.at[0], tp=tp_of(d))
        pltpu.make_async_copy(tile_sum, ag.at[my], ag_recv_sem.at[0]).start()

    arrived(ag, ag_recv_sem.at[0])

    e2 = jnp.concatenate([e_ref[...], e_ref[...]], axis=1)
    lane1 = iota((ROWS_X, LANES), 1)
    for y in range(NX):
        tile = jnp.concatenate([ag[2 * y], ag[2 * y + 1]] * per, axis=0).T
        chosen = wanted[y * ROWS_X : (y + 1) * ROWS_X]
        spread = jnp.concatenate(
            [
                jnp.where(chosen == n * per + lane1 // rank, tile, 0.0)
                for n in range(homes // per)
            ],
            axis=1,
        )
        hi = spread.astype(BF16)
        lo = (spread - hi.astype(F32)).astype(BF16)
        full = nn(hi, e2) + nn(lo, e2)
        top = full.astype(BF16).astype(F32)
        pair = jnp.where(lane1 < width, full, full - top).astype(BF16)
        sel = back_pick[y].reshape(nz * BACK, LANES).astype(BF16)
        rows = nn(sel, pair)
        for z in range(nz):
            xsend[z * NX + y] = rows[z * BACK : (z + 1) * BACK].astype(BF16)
    to_groups(xsend, xrecv, xsend_sem, xrecv_sem)

    arrived(brecv, brecv_sem.at[0])
    base = jnp.sum(brecv[...], axis=0)

    arrived(xrecv, xrecv_sem.at[0])
    extra = nn(unpack, xrecv[...].reshape(groups * BACK, LANES)).T
    total = (base + extra[:width] + extra[width:]).astype(BF16)
    final = nt(place_out, total)
    for s in range(groups):
        osend[s] = final[s * rowcap : (s + 1) * rowcap].astype(BF16)
    to_groups(osend, out_ref, osend_sem, orecv_sem)

    for c in range(CHUNKS):
        arrived(send1.at[c, pl.ds(0, nz - 1)], send1_sem.at[c])
        arrived(send2.at[c, pl.ds(0, NX - 1)], send2_sem.at[c])
    arrived(bsend.at[pl.ds(0, peers - 1)], bsend_sem.at[0])
    arrived(rs_send.at[pl.ds(0, tiles - 1)], rs_send_sem.at[0])

    @pl.when(jnp.logical_not(first_core))
    def _():
        arrived(rs_send.at[0], rs_send_sem.at[0])

    @pl.when(first_core)
    def _():
        arrived(rs_recv.at[pl.ds(0, peers - 1)], ag_send_sem.at[0])

    arrived(xsend.at[pl.ds(0, groups - 1)], xsend_sem.at[0])
    arrived(osend.at[pl.ds(0, groups - 1)], osend_sem.at[0])
    arrived(out_ref, orecv_sem.at[0])


def hot_value(a):
    return a.astype(F32).astype(BF16)


def fused(groups, peers, requests, value_weight, shrink, expand, dest, aid, lists, table):
    tok, depth = requests.shape
    width = expand.shape[1]
    rowcap = 3 * tok // groups
    nz, part, slots = groups // NX, depth // CHUNKS, NX * ROWS_X
    vmem = pl.BlockSpec(memory_space=pltpu.VMEM)
    dma = pltpu.SemaphoreType.DMA
    return pl.pallas_call(
        functools.partial(fused_kernel, groups, peers),
        out_shape=[
            jax.ShapeDtypeStruct((groups, rowcap, width), BF16),
            jax.ShapeDtypeStruct((1, 1), I32),
        ],
        in_specs=[vmem] * 8,
        out_specs=[vmem, pl.BlockSpec(memory_space=pltpu.SMEM)],
        scratch_shapes=[
            pltpu.VMEM((CHUNKS, nz, ROWS_Z, part), BF16),
            pltpu.VMEM((CHUNKS, nz, ROWS_Z, part), BF16),
            pltpu.VMEM((CHUNKS, NX, ROWS_X, part), BF16),
            pltpu.VMEM((CHUNKS, NX, ROWS_X, part), BF16),
            pltpu.VMEM((peers, width, tok), F32),
            pltpu.VMEM((peers, width, tok), F32),
            pltpu.VMEM((slots, shrink.shape[0]), F32),
            pltpu.VMEM((nz * ROWS_Z, slots), F32),
            pltpu.VMEM((slots, nz * ROWS_Z), BF16),
            pltpu.VMEM((tok, tok), BF16),
            pltpu.VMEM((2 * groups, lists.shape[1]), BF16),
            pltpu.VMEM((groups, tok), I32),
            pltpu.VMEM((groups, tok), I32),
            pltpu.VMEM((groups, tok), I32),
            pltpu.VMEM((groups, tok), I32),
            pltpu.VMEM((2, groups, tok), I32),
            pltpu.VMEM((slots, LANES), F32),
            pltpu.VMEM((NX, nz, BACK, LANES), F32),
            pltpu.VMEM((peers // 2, 8, LANES), F32),
            pltpu.VMEM((peers, 8, LANES), F32),
            pltpu.VMEM((8, LANES), F32),
            pltpu.VMEM((peers // 2, 8, LANES), F32),
            pltpu.VMEM((groups, BACK, LANES), BF16),
            pltpu.VMEM((groups, BACK, LANES), BF16),
            pltpu.VMEM((groups, rowcap, width), BF16),
            *[dma((CHUNKS,))] * 4,
            *[dma((1,))] * 10,
        ],
        compiler_params=pltpu.CompilerParams(
            collective_id=0, has_side_effects=True, vmem_limit_bytes=48 * 1024 * 1024
        ),
        name="fused",
    )(requests, value_weight, shrink, expand, dest, aid, lists, table)


def on_device(
    requests,
    value_weight,
    shrink_weight,
    expand_weight,
    destination,
    adapter_ids,
    cache_lists,
    home_table,
):
    groups = lax.axis_size("rep")
    tok = requests.shape[0]
    home_count, rank, depth = shrink_weight.shape
    width = expand_weight.shape[2]
    out, over = fused(
        groups,
        lax.axis_size("tp"),
        requests,
        value_weight,
        shrink_weight.reshape(home_count * rank, depth),
        expand_weight.reshape(home_count * rank, width),
        destination.reshape(-1, LANES),
        adapter_ids.reshape(-1, LANES),
        cache_lists,
        home_table.reshape(-1, LANES),
    )
    out = out.reshape(-1, width)

    def any_input(out):
        return by_serving_group(
            requests,
            value_weight,
            shrink_weight,
            expand_weight,
            destination,
            adapter_ids,
            cache_lists,
            home_table,
        )

    return lax.cond(over[0, 0] > 0, any_input, lambda out: out, out)


def solution(mesh):
    in_specs = (
        P("rep", "tp"),
        P("tp", None),
        P("rep", None, "tp"),
        P("rep", None, "tp"),
        P(),
        P(),
        P(),
        P(),
    )
    out_specs = P("rep", "tp")
    return jax.shard_map(
        on_device, mesh=mesh, in_specs=in_specs, out_specs=out_specs, check_vma=False
    )
```

```python
import functools

import jax
import jax.numpy as jnp
from jax import lax
from jax.experimental import pallas as pl
from jax.experimental.pallas import tpu as pltpu
from jax.sharding import PartitionSpec as P

PAIR = 2


def by_serving_group(
    requests,
    value_weight,
    shrink_weight,
    expand_weight,
    destination,
    adapter_ids,
    cache_lists,
    home_table,
):
    groups = lax.axis_size("rep")
    own_group = lax.axis_index("rep")
    tok_dev = requests.shape[0]
    rowcap = 3 * tok_dev // groups
    buffer_rows = groups * rowcap
    home_count = shrink_weight.shape[0]
    cache_len = cache_lists.shape[1]
    rank_width = shrink_weight.shape[1]
    width_out = expand_weight.shape[2]
    places = jnp.arange(cache_len, dtype=jnp.int32)
    blocks = destination.reshape(groups, tok_dev)
    targets = jnp.arange(groups, dtype=jnp.int32)
    member = (blocks[:, :, None] == targets[None, None, :]).astype(jnp.int32)
    earlier = jnp.sum(member * (jnp.cumsum(member, axis=1) - 1), axis=2)
    slot_all = targets[:, None] * rowcap + earlier
    own_slot = lax.dynamic_index_in_dim(
        blocks, own_group, 0, keepdims=False
    ) * rowcap + lax.dynamic_index_in_dim(earlier, own_group, 0, keepdims=False)
    send_rows = (
        jnp.zeros((buffer_rows, requests.shape[1]), requests.dtype).at[own_slot].set(requests)
    )
    arrived = lax.all_to_all(send_rows, "rep", split_axis=0, concat_axis=0, tiled=True)
    landing = jnp.where(blocks == own_group, slot_all, buffer_rows).reshape(-1)
    slot_place = jnp.full((buffer_rows,), -1, jnp.int32).at[landing].set(adapter_ids, mode="drop")
    selector = (slot_place[:, None] == places[None, :]).astype(jnp.float32)
    positions = home_table[cache_lists]
    home_group = positions // home_count
    local_slot = positions % home_count
    homed_here = home_group == own_group
    ranking = jnp.cumsum(homed_here.astype(jnp.int32), axis=1) - 1
    outgoing = jnp.where(homed_here, targets[:, None] * PAIR + ranking, groups * PAIR).reshape(-1)
    send_index = (
        jnp.zeros((groups * PAIR,), jnp.int32).at[outgoing].set(local_slot.reshape(-1), mode="drop")
    )
    send_valid = (
        jnp.zeros((groups * PAIR,), jnp.bfloat16).at[outgoing].set(jnp.bfloat16(1.0), mode="drop")
    )
    send_down = shrink_weight[send_index] * send_valid[:, None, None]
    send_up = expand_weight[send_index] * send_valid[:, None, None]
    got_down, got_up = (
        lax.all_to_all(send_down, "rep", split_axis=0, concat_axis=0, tiled=True),
        lax.all_to_all(send_up, "rep", split_axis=0, concat_axis=0, tiled=True),
    )
    own_homes = lax.dynamic_index_in_dim(home_group, own_group, 0, keepdims=False)
    same_before = jnp.sum(
        ((own_homes[None, :] == own_homes[:, None]) & (places[None, :] < places[:, None])).astype(
            jnp.int32
        ),
        axis=1,
    )
    fetch_index = own_homes * PAIR + same_before
    cached_down = got_down[fetch_index].reshape(cache_len * rank_width, -1)
    cached_up = got_up[fetch_index].reshape(cache_len * rank_width, width_out).astype(jnp.float32)
    shrunk_all = lax.dot_general(
        arrived, cached_down, (((1,), (1,)), ((), ())), preferred_element_type=jnp.float32
    )
    shrunk_part = jnp.sum(
        shrunk_all.reshape(buffer_rows, cache_len, rank_width) * selector[:, :, None], axis=1
    )
    shrunk = lax.psum(shrunk_part, "tp")
    spread_rows = (selector[:, :, None] * shrunk[:, None, :]).reshape(
        buffer_rows, cache_len * rank_width
    )
    expanded = jnp.dot(spread_rows, cached_up, precision=lax.Precision.HIGHEST)
    partial_all = jnp.dot(arrived, value_weight, preferred_element_type=jnp.float32)
    projected = lax.psum_scatter(partial_all, "tp", scatter_dimension=1, tiled=True)
    return (projected + expanded).astype(jnp.bfloat16)


MESH = pl.DeviceIdType.MESH
NX = 4
ROWS_Z = 64
ROWS_X = 128
BACK = 32
EIGHTHS = (3, 2, 2, 1)
CHUNKS = len(EIGHTHS)
LANES = 128
TILE = 16
F32, BF16, I32 = jnp.float32, jnp.bfloat16, jnp.int32


def hot(mask):
    return mask.astype(F32).astype(BF16)


def iota(shape, axis):
    return lax.broadcasted_iota(I32, shape, axis)


def nn(a, b):
    return jnp.dot(a, b, preferred_element_type=F32)


def nt(a, b):
    return lax.dot_general(a, b, (((1,), (1,)), ((), ())), preferred_element_type=F32)


def spans_of(depth):
    ends = [depth * sum(EIGHTHS[:c]) // sum(EIGHTHS) for c in range(CHUNKS + 1)]
    return list(zip(ends[:-1], ends[1:]))


def fused_kernel(
    groups,
    peers,
    x_ref,
    v_ref,
    a_ref,
    e_ref,
    dest_ref,
    aid_ref,
    list_ref,
    table_ref,
    out_ref,
    over_ref,
    send1,
    recv1,
    send2,
    recv2,
    bsend,
    brecv,
    acc,
    pick2t,
    pick2,
    upper,
    entries,
    home_s,
    local_s,
    slot1_s,
    slot2_s,
    mine_s,
    adp,
    back_pick,
    rs_send,
    rs_recv,
    tile_sum,
    ag,
    xsend,
    xrecv,
    osend,
    orecv,
    send1_sem,
    recv1_sem,
    send2_sem,
    recv2_sem,
    bsend_sem,
    brecv_sem,
    rs_send_sem,
    rs_recv_sem,
    ag_send_sem,
    ag_recv_sem,
    xsend_sem,
    xrecv_sem,
    osend_sem,
    orecv_sem,
):
    me = lax.axis_index("rep")
    mt = lax.axis_index("tp")
    my = mt // 2
    mz, mx = me // NX, me % NX
    nz = groups // NX
    tok, depth = x_ref.shape
    spans = spans_of(depth)
    cache = list_ref.shape[1]
    homes = table_ref.shape[0] * LANES // groups
    rank = a_ref.shape[0] // homes
    rows_of = tok // LANES
    per = LANES // rank
    slots = NX * ROWS_X
    rowcap = out_ref.shape[1]

    barrier = pltpu.get_barrier_semaphore()

    def z_of(d):
        return lax.rem(mz + d, nz)

    def x_of(d):
        return lax.rem(mx + d, NX)

    def tp_of(d):
        return lax.rem(mt + d, peers)

    def greet(**where):
        pl.semaphore_signal(barrier, inc=1, device_id=where, device_id_type=MESH)

    z_steps = sorted(range(1, nz), key=lambda d: -min(d, nz - d))
    for d in z_steps:
        greet(rep=z_of(d) * NX + mx)
    for d in range(1, peers):
        greet(tp=tp_of(d))
    for d in range(1, NX):
        greet(rep=mz * NX + x_of(d))

    upper[...] = hot(iota((tok, tok), 0) < iota((tok, tok), 1))

    count = groups * cache
    lists = list_ref[...]
    place_of = hot(iota((cache, count), 0) == iota((cache, count), 1) % cache)
    owner = iota((groups, count), 1) // cache == iota((groups, count), 0)
    high = jnp.where(owner, nn(hot_value(lists // LANES), place_of), 0.0)
    low = jnp.where(owner, nn(hot_value(lists % LANES), place_of), 0.0)
    high = jnp.sum(high, axis=0, keepdims=True).astype(I32)
    low = jnp.sum(low, axis=0, keepdims=True).astype(I32)
    table = table_ref[...]
    both = jnp.concatenate([hot_value(table // homes), hot_value(table % homes)], axis=0)
    major = iota((table.shape[0], count), 0) == high
    minor = iota((LANES, count), 0) == low
    found = nn(both, hot(minor))
    of_home = jnp.sum(jnp.where(major, found[: table.shape[0]], 0.0), axis=0, keepdims=True)
    of_local = jnp.sum(jnp.where(major, found[table.shape[0] :], 0.0), axis=0, keepdims=True)
    spread = jnp.concatenate(
        [jnp.where(owner, of_home, 0.0), jnp.where(owner, of_local, 0.0)], axis=0
    ).astype(BF16)
    entries[...] = nn(spread, hot(iota((count, cache), 0) % cache == iota((count, cache), 1))).astype(
        BF16
    )

    def look_up(dest, aid):
        n = dest.shape[1]
        rows = nn(entries[...], hot(iota((cache, n), 0) == aid))
        serve = iota((groups, n), 0) == dest
        home = jnp.sum(jnp.where(serve, rows[:groups], 0.0), axis=0, keepdims=True)
        local = jnp.sum(jnp.where(serve, rows[groups:], 0.0), axis=0, keepdims=True)
        return home.astype(I32), local.astype(I32)

    def rank_in(member):
        earlier = nn(hot(member), upper[...])
        return jnp.sum(jnp.where(member, earlier, 0.0), axis=0, keepdims=True).astype(I32)

    def own(ref):
        return jnp.concatenate([ref[pl.ds(rows_of * me + i, 1), :] for i in range(rows_of)], axis=1)

    own_dest = own(dest_ref)
    own_home, _ = look_up(own_dest, own(aid_ref))
    own_plane = own_home // NX
    own_rank1 = rank_in(iota((nz, tok), 0) == own_plane)
    own_slot1 = jnp.where(own_rank1 < ROWS_Z, own_plane * ROWS_Z + own_rank1, -1)
    pick1 = hot(iota((nz * ROWS_Z, tok), 0) == own_slot1)

    def pack(c):
        first, last = spans[c]
        rows = nn(pick1, x_ref[:, first:last])
        send1[c][...] = rows.astype(BF16).reshape(nz, ROWS_Z, last - first)

    pack(0)
    pl.semaphore_wait(barrier, nz + NX + peers - 3)

    def arrived(buffer, sem):
        pltpu.make_async_copy(buffer, buffer, sem).wait()

    def push(src, dst, ssem, rsem, **where):
        pltpu.make_async_remote_copy(
            src_ref=src,
            dst_ref=dst,
            send_sem=ssem,
            recv_sem=rsem,
            device_id=where,
            device_id_type=MESH,
        ).start()

    def z_start(c):
        for d in z_steps:
            to = z_of(d)
            push(
                send1[c].at[to],
                recv1[c].at[mz],
                send1_sem.at[c],
                recv1_sem.at[c],
                rep=to * NX + mx,
            )
        pltpu.make_async_copy(send1[c].at[mz], recv1[c].at[mz], recv1_sem.at[c]).start()

    z_start(0)
    for c in range(1, CHUNKS):
        pack(c)
        z_start(c)

    width = bsend.shape[1]
    step = 256
    for n in range(v_ref.shape[1] // step):
        bt = nn(x_ref[...], v_ref[:, n * step : (n + 1) * step]).T
        for i in range(step // width):
            bsend[n * (step // width) + i] = bt[i * width : (i + 1) * width]

    for d in range(1, peers):
        to = tp_of(d)
        push(bsend.at[to], brecv.at[mt], bsend_sem.at[0], brecv_sem.at[0], tp=to)
    pltpu.make_async_copy(bsend.at[mt], brecv.at[mt], brecv_sem.at[0]).start()

    batch = 8
    counts = jnp.zeros((groups, LANES), F32)
    for q in range(groups // batch):
        ids = range(q * batch, (q + 1) * batch)
        lines = range(q * batch * rows_of, (q + 1) * batch * rows_of)
        dest = jnp.concatenate([dest_ref[r : r + 1, :] for r in lines], axis=1)
        aid = jnp.concatenate([aid_ref[r : r + 1, :] for r in lines], axis=1)
        home, local = look_up(dest, aid)
        for j, g in enumerate(ids):
            home_s[g : g + 1, :] = home[:, j * tok : (j + 1) * tok]
            local_s[g : g + 1, :] = local[:, j * tok : (j + 1) * tok]
        n = batch * tok
        counts += nn(
            hot(iota((groups, n), 0) == home),
            hot(iota((n, LANES), 0) // tok + q * batch == iota((n, LANES), 1)),
        )
    by_plane = nn(hot(iota((nz, groups), 0) == iota((nz, groups), 1) // NX), counts.astype(BF16))
    by_column = nn(
        counts.astype(BF16), hot(iota((LANES, LANES), 0) % NX == iota((LANES, LANES), 1))
    )
    over = (
        jnp.max(jnp.where(counts > BACK, 1.0, 0.0), axis=0, keepdims=True)
        + jnp.max(jnp.where(by_plane > ROWS_Z, 1.0, 0.0), axis=0, keepdims=True)
        + jnp.max(jnp.where(by_column > ROWS_X, 1.0, 0.0), axis=0, keepdims=True)
    )
    over_ref[0, 0] = jnp.max(over).astype(I32)

    homes_all = home_s[...]
    before = hot(
        (iota((groups, groups), 1) % NX == iota((groups, groups), 0) % NX)
        & (iota((groups, groups), 1) < iota((groups, groups), 0))
    )
    ones = jnp.ones((tok, LANES), BF16)

    def rank2(member):
        picked = hot(member)
        earlier = nn(picked, upper[...])
        total = nn(before, nn(picked, ones).astype(BF16))
        return (earlier + jnp.concatenate([total] * (tok // LANES), axis=1)).astype(I32), earlier

    here = homes_all // NX == mz
    place1 = nn(hot(here), upper[...]).astype(I32)
    slot1_s[...] = jnp.where(here & (place1 < ROWS_Z), place1, -1)
    target = jnp.full((groups, tok), -1, I32)
    for i in range(NX):
        member = homes_all == mz * NX + i
        place, _ = rank2(member)
        target = jnp.where(member & (place < ROWS_X), i * ROWS_X + place, target)
    slot2_s[...] = target
    member = homes_all == me
    place, back_rank = rank2(member)
    mine_s[0] = jnp.where(member & (place < ROWS_X), place, -1)
    mine_s[1] = jnp.where(member, back_rank.astype(I32), -1)

    def route(z, w):
        g = z * NX + mx
        first = hot(iota((ROWS_Z, tok), 0) == slot1_s[pl.ds(g, 1), :])
        second = hot(iota((slots, tok), 0) == slot2_s[pl.ds(g, 1), :])
        pick2t[pl.ds(pl.multiple_of(z * ROWS_Z, ROWS_Z), ROWS_Z), :] = nt(first, second)
        return w

    lax.fori_loop(0, nz, route, 0)
    pick2[...] = pick2t[...].T.astype(BF16)

    adp[...] = jnp.zeros_like(adp)
    acc[...] = jnp.zeros_like(acc)

    def shrink(c):
        arrived(recv2[c], recv2_sem.at[c])
        first, last = spans[c]
        rows = recv2[c][...].reshape(slots, last - first)
        return nt(rows, a_ref[:, first:last])

    def stage(c):
        arrived(recv1[c], recv1_sem.at[c])
        wide = spans[c][1] - spans[c][0]
        rows = nn(pick2[...], recv1[c][...].reshape(nz * ROWS_Z, wide))
        send2[c][...] = rows.astype(BF16).reshape(NX, ROWS_X, wide)

        for d in range(1, NX):
            to = x_of(d)
            push(
                send2[c].at[to],
                recv2[c].at[mx],
                send2_sem.at[c],
                recv2_sem.at[c],
                rep=mz * NX + to,
            )
        pltpu.make_async_copy(send2[c].at[mx], recv2[c].at[mx], recv2_sem.at[c]).start()

    def homed(g, w):
        column = lax.rem(g, NX)
        second = hot(iota((ROWS_X, tok), 0) == mine_s[0, pl.ds(g, 1), :])
        back = hot(iota((BACK, tok), 0) == mine_s[1, pl.ds(g, 1), :])
        value = (local_s[pl.ds(g, 1), :] + 1).astype(F32).astype(BF16)
        at = pl.ds(pl.multiple_of(column * ROWS_X, ROWS_X), ROWS_X)
        adp[at, :] += nt(second, jnp.broadcast_to(value, (LANES, tok)))
        back_pick[column, g // NX] = nt(back, second)
        return w

    shares = (0, 12 * groups // 32, 22 * groups // 32, groups, groups)
    for c in range(CHUNKS):
        stage(c)
        lax.fori_loop(shares[c], shares[c + 1], homed, 0)
        if c:
            acc[...] += shrink(c - 1)
    own_back = rank_in(iota((groups, tok), 0) == own_home)
    own_back = jnp.where(own_back < BACK, own_home * BACK + own_back, -1)
    column = jnp.broadcast_to(own_back.astype(F32), (LANES, tok)).T[:, 0:1].astype(I32)
    unpack = hot(iota((tok, groups * BACK), 1) == column)
    own_out = own_dest * rowcap + rank_in(iota((groups, tok), 0) == own_dest)
    got = acc[...] + shrink(CHUNKS - 1)

    wanted = adp[...].astype(I32) - 1
    lane = iota((slots, LANES), 1) // rank
    folded = jnp.zeros((slots, LANES), F32)
    for n in range(homes // per):
        folded += jnp.where(wanted == n * per + lane, got[:, n * LANES : (n + 1) * LANES], 0.0)

    low = jnp.sum(folded.T.reshape(per, rank, slots), axis=0)
    tiles = peers // 2
    half = rank // 2
    for t in range(tiles):
        rs_send[t] = low[
            half * (t % 2) : half * (t % 2 + 1), (t // 2) * LANES : (t // 2 + 1) * LANES
        ]

    first_core = lax.rem(mt, 2) == 0
    for d in sorted(range(1, tiles), key=lambda d: -min(d, tiles - d)):
        tile = lax.rem(my + d, tiles)
        push(rs_send.at[tile], rs_recv.at[mt], rs_send_sem.at[0], rs_recv_sem.at[0], tp=2 * tile)

    @pl.when(jnp.logical_not(first_core))
    def _():
        push(rs_send.at[my], rs_recv.at[mt], rs_send_sem.at[0], rs_recv_sem.at[0], tp=2 * my)

    @pl.when(first_core)
    def _():
        pltpu.make_async_copy(rs_send.at[my], rs_recv.at[mt], rs_recv_sem.at[0]).start()
        arrived(rs_recv, rs_recv_sem.at[0])
        tile_sum[...] = jnp.sum(rs_recv[...], axis=0)
        for d in sorted(range(1, peers), key=lambda d: -min(d, peers - d)):
            push(tile_sum, ag.at[my], ag_send_sem.at[0], ag_recv_sem.at[0], tp=tp_of(d))
        pltpu.make_async_copy(tile_sum, ag.at[my], ag_recv_sem.at[0]).start()

    arrived(ag, ag_recv_sem.at[0])

    e2 = jnp.concatenate([e_ref[...], e_ref[...]], axis=1)
    lane1 = iota((ROWS_X, LANES), 1)
    for dx in (2, 1, 3, 0):
        y = x_of(dx)
        tile = jnp.concatenate([ag[2 * y], ag[2 * y + 1]] * per, axis=0).T
        chosen = adp[pl.ds(pl.multiple_of(y * ROWS_X, ROWS_X), ROWS_X), :].astype(I32) - 1
        spread = jnp.concatenate(
            [
                jnp.where(chosen == n * per + lane1 // rank, tile, 0.0)
                for n in range(homes // per)
            ],
            axis=1,
        )
        hi = spread.astype(BF16)
        lo = (spread - hi.astype(F32)).astype(BF16)
        full = nn(hi, e2) + nn(lo, e2)
        top = full.astype(BF16).astype(F32)
        pair = jnp.where(lane1 < width, full, full - top).astype(BF16)
        sel = back_pick[y].reshape(nz * BACK, LANES).astype(BF16)
        rows = nn(sel, pair)
        for z in range(nz):
            xsend[z * NX + y] = rows[z * BACK : (z + 1) * BACK].astype(BF16)
        for dz in z_steps + [0]:
            if dz or dx:
                to = z_of(dz) * NX + y
                push(xsend.at[to], xrecv.at[me], xsend_sem.at[0], xrecv_sem.at[0], rep=to)
    pltpu.make_async_copy(xsend.at[me], xrecv.at[me], xrecv_sem.at[0]).start()

    arrived(brecv, brecv_sem.at[0])
    base = jnp.sum(brecv[...], axis=0)

    arrived(xrecv, xrecv_sem.at[0])
    extra = nn(unpack, xrecv[...].reshape(groups * BACK, LANES)).T
    total = (base + extra[:width] + extra[width:]).astype(BF16)
    blank = jnp.zeros_like(total)
    sides = jnp.concatenate(
        [jnp.concatenate([total, blank], axis=1), jnp.concatenate([blank, total], axis=1)], axis=0
    )
    line = iota((NX * TILE, tok), 0)
    for dz in z_steps + [0]:
        z = z_of(dz)
        slot = z * NX * rowcap + line // TILE * rowcap + line % TILE
        high = (slot + TILE == own_out) & (line % TILE < rowcap - TILE)
        rows = nt(jnp.concatenate([hot(slot == own_out), hot(high)], axis=1), sides)
        for i in range(NX):
            osend[z * NX + i] = rows[i * TILE : (i + 1) * TILE].astype(BF16)
        for dx in range(NX):
            if dz or dx:
                to = z * NX + x_of(dx)
                push(osend.at[to], orecv.at[me], osend_sem.at[0], orecv_sem.at[0], rep=to)
    pltpu.make_async_copy(osend.at[me], orecv.at[me], orecv_sem.at[0]).start()

    for c in range(CHUNKS):
        arrived(send1[c].at[pl.ds(0, nz - 1)], send1_sem.at[c])
        arrived(send2[c].at[pl.ds(0, NX - 1)], send2_sem.at[c])
    arrived(bsend.at[pl.ds(0, peers - 1)], bsend_sem.at[0])
    arrived(rs_send.at[pl.ds(0, tiles - 1)], rs_send_sem.at[0])

    @pl.when(jnp.logical_not(first_core))
    def _():
        arrived(rs_send.at[0], rs_send_sem.at[0])

    @pl.when(first_core)
    def _():
        arrived(rs_recv.at[pl.ds(0, peers - 1)], ag_send_sem.at[0])

    arrived(xsend.at[pl.ds(0, groups - 1)], xsend_sem.at[0])
    arrived(osend.at[pl.ds(0, groups - 1)], osend_sem.at[0])
    arrived(orecv, orecv_sem.at[0])
    done = orecv[...].astype(F32)
    out_ref[:, :TILE, :] = done[:, :, :width].astype(BF16)
    out_ref[:, TILE:, :] = done[:, : rowcap - TILE, width:].astype(BF16)


def hot_value(a):
    return a.astype(F32).astype(BF16)


def fused(groups, peers, requests, value_weight, shrink, expand, dest, aid, lists, table):
    tok, depth = requests.shape
    width = expand.shape[1]
    rowcap = 3 * tok // groups
    nz, slots = groups // NX, NX * ROWS_X
    wide = [last - first for first, last in spans_of(depth)]
    vmem = pl.BlockSpec(memory_space=pltpu.VMEM)
    dma = pltpu.SemaphoreType.DMA
    return pl.pallas_call(
        functools.partial(fused_kernel, groups, peers),
        out_shape=[
            jax.ShapeDtypeStruct((groups, rowcap, width), BF16),
            jax.ShapeDtypeStruct((1, 1), I32),
        ],
        in_specs=[vmem] * 8,
        out_specs=[vmem, pl.BlockSpec(memory_space=pltpu.SMEM)],
        scratch_shapes=[
            [pltpu.VMEM((nz, ROWS_Z, n), BF16) for n in wide],
            [pltpu.VMEM((nz, ROWS_Z, n), BF16) for n in wide],
            [pltpu.VMEM((NX, ROWS_X, n), BF16) for n in wide],
            [pltpu.VMEM((NX, ROWS_X, n), BF16) for n in wide],
            pltpu.VMEM((peers, width, tok), F32),
            pltpu.VMEM((peers, width, tok), F32),
            pltpu.VMEM((slots, shrink.shape[0]), F32),
            pltpu.VMEM((nz * ROWS_Z, slots), F32),
            pltpu.VMEM((slots, nz * ROWS_Z), BF16),
            pltpu.VMEM((tok, tok), BF16),
            pltpu.VMEM((2 * groups, lists.shape[1]), BF16),
            pltpu.VMEM((groups, tok), I32),
            pltpu.VMEM((groups, tok), I32),
            pltpu.VMEM((groups, tok), I32),
            pltpu.VMEM((groups, tok), I32),
            pltpu.VMEM((2, groups, tok), I32),
            pltpu.VMEM((slots, LANES), F32),
            pltpu.VMEM((NX, nz, BACK, LANES), F32),
            pltpu.VMEM((peers // 2, 8, LANES), F32),
            pltpu.VMEM((peers, 8, LANES), F32),
            pltpu.VMEM((8, LANES), F32),
            pltpu.VMEM((peers // 2, 8, LANES), F32),
            pltpu.VMEM((groups, BACK, LANES), BF16),
            pltpu.VMEM((groups, BACK, LANES), BF16),
            pltpu.VMEM((groups, TILE, LANES), BF16),
            pltpu.VMEM((groups, TILE, LANES), BF16),
            *[dma((CHUNKS,))] * 4,
            *[dma((1,))] * 10,
        ],
        compiler_params=pltpu.CompilerParams(
            collective_id=0, has_side_effects=True, vmem_limit_bytes=48 * 1024 * 1024
        ),
        name="fused",
    )(requests, value_weight, shrink, expand, dest, aid, lists, table)


def on_device(
    requests,
    value_weight,
    shrink_weight,
    expand_weight,
    destination,
    adapter_ids,
    cache_lists,
    home_table,
):
    groups = lax.axis_size("rep")
    tok = requests.shape[0]
    home_count, rank, depth = shrink_weight.shape
    width = expand_weight.shape[2]
    out, over = fused(
        groups,
        lax.axis_size("tp"),
        requests,
        value_weight,
        shrink_weight.reshape(home_count * rank, depth),
        expand_weight.reshape(home_count * rank, width),
        destination.reshape(-1, LANES),
        adapter_ids.reshape(-1, LANES),
        cache_lists,
        home_table.reshape(-1, LANES),
    )
    out = out.reshape(-1, width)

    def any_input(out):
        return by_serving_group(
            requests,
            value_weight,
            shrink_weight,
            expand_weight,
            destination,
            adapter_ids,
            cache_lists,
            home_table,
        )

    return lax.cond(over[0, 0] > 0, any_input, lambda out: out, out)


def solution(mesh):
    in_specs = (
        P("rep", "tp"),
        P("tp", None),
        P("rep", None, "tp"),
        P("rep", None, "tp"),
        P(),
        P(),
        P(),
        P(),
    )
    out_specs = P("rep", "tp")
    return jax.shard_map(
        on_device, mesh=mesh, in_specs=in_specs, out_specs=out_specs, check_vma=False
    )
```

```python
import functools

import jax
import jax.numpy as jnp
from jax import lax
from jax.experimental import pallas as pl
from jax.experimental.pallas import tpu as pltpu
from jax.sharding import PartitionSpec as P

PAIR = 2


def by_serving_group(
    requests,
    value_weight,
    shrink_weight,
    expand_weight,
    destination,
    adapter_ids,
    cache_lists,
    home_table,
):
    groups = lax.axis_size("rep")
    own_group = lax.axis_index("rep")
    tok_dev = requests.shape[0]
    rowcap = 3 * tok_dev // groups
    buffer_rows = groups * rowcap
    home_count = shrink_weight.shape[0]
    cache_len = cache_lists.shape[1]
    rank_width = shrink_weight.shape[1]
    width_out = expand_weight.shape[2]
    places = jnp.arange(cache_len, dtype=jnp.int32)
    blocks = destination.reshape(groups, tok_dev)
    targets = jnp.arange(groups, dtype=jnp.int32)
    member = (blocks[:, :, None] == targets[None, None, :]).astype(jnp.int32)
    earlier = jnp.sum(member * (jnp.cumsum(member, axis=1) - 1), axis=2)
    slot_all = targets[:, None] * rowcap + earlier
    own_slot = lax.dynamic_index_in_dim(
        blocks, own_group, 0, keepdims=False
    ) * rowcap + lax.dynamic_index_in_dim(earlier, own_group, 0, keepdims=False)
    send_rows = (
        jnp.zeros((buffer_rows, requests.shape[1]), requests.dtype).at[own_slot].set(requests)
    )
    arrived = lax.all_to_all(send_rows, "rep", split_axis=0, concat_axis=0, tiled=True)
    landing = jnp.where(blocks == own_group, slot_all, buffer_rows).reshape(-1)
    slot_place = jnp.full((buffer_rows,), -1, jnp.int32).at[landing].set(adapter_ids, mode="drop")
    selector = (slot_place[:, None] == places[None, :]).astype(jnp.float32)
    positions = home_table[cache_lists]
    home_group = positions // home_count
    local_slot = positions % home_count
    homed_here = home_group == own_group
    ranking = jnp.cumsum(homed_here.astype(jnp.int32), axis=1) - 1
    outgoing = jnp.where(homed_here, targets[:, None] * PAIR + ranking, groups * PAIR).reshape(-1)
    send_index = (
        jnp.zeros((groups * PAIR,), jnp.int32).at[outgoing].set(local_slot.reshape(-1), mode="drop")
    )
    send_valid = (
        jnp.zeros((groups * PAIR,), jnp.bfloat16).at[outgoing].set(jnp.bfloat16(1.0), mode="drop")
    )
    send_down = shrink_weight[send_index] * send_valid[:, None, None]
    send_up = expand_weight[send_index] * send_valid[:, None, None]
    got_down, got_up = (
        lax.all_to_all(send_down, "rep", split_axis=0, concat_axis=0, tiled=True),
        lax.all_to_all(send_up, "rep", split_axis=0, concat_axis=0, tiled=True),
    )
    own_homes = lax.dynamic_index_in_dim(home_group, own_group, 0, keepdims=False)
    same_before = jnp.sum(
        ((own_homes[None, :] == own_homes[:, None]) & (places[None, :] < places[:, None])).astype(
            jnp.int32
        ),
        axis=1,
    )
    fetch_index = own_homes * PAIR + same_before
    cached_down = got_down[fetch_index].reshape(cache_len * rank_width, -1)
    cached_up = got_up[fetch_index].reshape(cache_len * rank_width, width_out).astype(jnp.float32)
    shrunk_all = lax.dot_general(
        arrived, cached_down, (((1,), (1,)), ((), ())), preferred_element_type=jnp.float32
    )
    shrunk_part = jnp.sum(
        shrunk_all.reshape(buffer_rows, cache_len, rank_width) * selector[:, :, None], axis=1
    )
    peers = lax.axis_size("tp")
    pieces = lax.all_to_all(shrunk_part, "tp", split_axis=0, concat_axis=0, tiled=True)
    piece = jnp.sum(pieces.reshape(peers, -1, rank_width), axis=0)
    shrunk = lax.all_to_all(
        jnp.tile(piece, (peers, 1)), "tp", split_axis=0, concat_axis=0, tiled=True
    )
    spread_rows = (selector[:, :, None] * shrunk[:, None, :]).reshape(
        buffer_rows, cache_len * rank_width
    )
    expanded = jnp.dot(spread_rows, cached_up, precision=lax.Precision.HIGHEST)
    partial_all = jnp.dot(arrived, value_weight, preferred_element_type=jnp.float32)
    columns = lax.all_to_all(partial_all, "tp", split_axis=1, concat_axis=0, tiled=True)
    projected = jnp.sum(columns.reshape(peers, buffer_rows, width_out), axis=0)
    return (projected + expanded).astype(jnp.bfloat16)


MESH = pl.DeviceIdType.MESH
NX = 4
ROWS_Z = 64
ROWS_X = 128
BACK = 32
EIGHTHS = (3, 2, 2, 1)
CHUNKS = len(EIGHTHS)
LANES = 128
TILE = 16
NEAR = 4
F32, BF16, I32 = jnp.float32, jnp.bfloat16, jnp.int32


def hot(mask):
    return mask.astype(F32).astype(BF16)


def iota(shape, axis):
    return lax.broadcasted_iota(I32, shape, axis)


def nn(a, b):
    return jnp.dot(a, b, preferred_element_type=F32)


def nt(a, b):
    return lax.dot_general(a, b, (((1,), (1,)), ((), ())), preferred_element_type=F32)


def spans_of(depth):
    ends = [depth * sum(EIGHTHS[:c]) // sum(EIGHTHS) for c in range(CHUNKS + 1)]
    return list(zip(ends[:-1], ends[1:]))


def fused_kernel(
    groups,
    peers,
    x_ref,
    v_ref,
    a_ref,
    e_ref,
    dest_ref,
    aid_ref,
    list_ref,
    table_ref,
    out_ref,
    over_ref,
    send1,
    recv1,
    send2,
    recv2,
    bsend,
    brecv,
    acc,
    pick2t,
    pick2,
    upper,
    entries,
    home_s,
    local_s,
    slot1_s,
    slot2_s,
    mine_s,
    adp,
    back_pick,
    far_src,
    far,
    near_src,
    near,
    low_sum,
    xsend,
    xrecv,
    osend,
    orecv,
    send1_sem,
    recv1_sem,
    send2_sem,
    recv2_sem,
    bsend_sem,
    brecv_sem,
    far_send_sem,
    far_recv_sem,
    near_send_sem,
    near_recv_sem,
    xsend_sem,
    xrecv_sem,
    osend_sem,
    orecv_sem,
):
    me = lax.axis_index("rep")
    mt = lax.axis_index("tp")
    mz, mx = me // NX, me % NX
    nz = groups // NX
    tok, depth = x_ref.shape
    spans = spans_of(depth)
    cache = list_ref.shape[1]
    homes = table_ref.shape[0] * LANES // groups
    rank = a_ref.shape[0] // homes
    rows_of = tok // LANES
    per = LANES // rank
    slots = NX * ROWS_X
    rowcap = out_ref.shape[1]

    barrier = pltpu.get_barrier_semaphore()

    def z_of(d):
        return lax.rem(mz + d, nz)

    def x_of(d):
        return lax.rem(mx + d, NX)

    def tp_of(d):
        return lax.rem(mt + d, peers)

    def greet(**where):
        pl.semaphore_signal(barrier, inc=1, device_id=where, device_id_type=MESH)

    z_steps = sorted(range(1, nz), key=lambda d: -min(d, nz - d))
    for d in z_steps:
        greet(rep=z_of(d) * NX + mx)
    for d in range(1, peers):
        greet(tp=tp_of(d))
    for d in range(1, NX):
        greet(rep=mz * NX + x_of(d))

    upper[...] = hot(iota((tok, tok), 0) < iota((tok, tok), 1))

    count = groups * cache
    lists = list_ref[...]
    place_of = hot(iota((cache, count), 0) == iota((cache, count), 1) % cache)
    owner = iota((groups, count), 1) // cache == iota((groups, count), 0)
    high = jnp.where(owner, nn(hot_value(lists // LANES), place_of), 0.0)
    low = jnp.where(owner, nn(hot_value(lists % LANES), place_of), 0.0)
    high = jnp.sum(high, axis=0, keepdims=True).astype(I32)
    low = jnp.sum(low, axis=0, keepdims=True).astype(I32)
    table = table_ref[...]
    both = jnp.concatenate([hot_value(table // homes), hot_value(table % homes)], axis=0)
    major = iota((table.shape[0], count), 0) == high
    minor = iota((LANES, count), 0) == low
    found = nn(both, hot(minor))
    of_home = jnp.sum(jnp.where(major, found[: table.shape[0]], 0.0), axis=0, keepdims=True)
    of_local = jnp.sum(jnp.where(major, found[table.shape[0] :], 0.0), axis=0, keepdims=True)
    spread = jnp.concatenate(
        [jnp.where(owner, of_home, 0.0), jnp.where(owner, of_local, 0.0)], axis=0
    ).astype(BF16)
    entries[...] = nn(spread, hot(iota((count, cache), 0) % cache == iota((count, cache), 1))).astype(
        BF16
    )

    def look_up(dest, aid):
        n = dest.shape[1]
        rows = nn(entries[...], hot(iota((cache, n), 0) == aid))
        serve = iota((groups, n), 0) == dest
        home = jnp.sum(jnp.where(serve, rows[:groups], 0.0), axis=0, keepdims=True)
        local = jnp.sum(jnp.where(serve, rows[groups:], 0.0), axis=0, keepdims=True)
        return home.astype(I32), local.astype(I32)

    def rank_in(member):
        earlier = nn(hot(member), upper[...])
        return jnp.sum(jnp.where(member, earlier, 0.0), axis=0, keepdims=True).astype(I32)

    def own(ref):
        return jnp.concatenate([ref[pl.ds(rows_of * me + i, 1), :] for i in range(rows_of)], axis=1)

    own_dest = own(dest_ref)
    own_home, _ = look_up(own_dest, own(aid_ref))
    own_plane = own_home // NX
    own_rank1 = rank_in(iota((nz, tok), 0) == own_plane)
    own_slot1 = jnp.where(own_rank1 < ROWS_Z, own_plane * ROWS_Z + own_rank1, -1)
    pick1 = hot(iota((nz * ROWS_Z, tok), 0) == own_slot1)

    def pack(c):
        first, last = spans[c]
        rows = nn(pick1, x_ref[:, first:last])
        send1[c][...] = rows.astype(BF16).reshape(nz, ROWS_Z, last - first)

    pack(0)
    pl.semaphore_wait(barrier, nz + NX + peers - 3)

    def arrived(buffer, sem):
        pltpu.make_async_copy(buffer, buffer, sem).wait()

    def push(src, dst, ssem, rsem, **where):
        pltpu.make_async_remote_copy(
            src_ref=src,
            dst_ref=dst,
            send_sem=ssem,
            recv_sem=rsem,
            device_id=where,
            device_id_type=MESH,
        ).start()

    def z_start(c):
        for d in z_steps:
            to = z_of(d)
            push(
                send1[c].at[to],
                recv1[c].at[mz],
                send1_sem.at[c],
                recv1_sem.at[c],
                rep=to * NX + mx,
            )
        pltpu.make_async_copy(send1[c].at[mz], recv1[c].at[mz], recv1_sem.at[c]).start()

    z_start(0)
    for c in range(1, CHUNKS):
        pack(c)
        z_start(c)

    width = bsend.shape[1]
    step = 256
    for n in range(v_ref.shape[1] // step):
        bt = nn(x_ref[...], v_ref[:, n * step : (n + 1) * step]).T
        for i in range(step // width):
            bsend[n * (step // width) + i] = bt[i * width : (i + 1) * width]

    for d in range(1, peers):
        to = tp_of(d)
        push(bsend.at[to], brecv.at[mt], bsend_sem.at[0], brecv_sem.at[0], tp=to)
    pltpu.make_async_copy(bsend.at[mt], brecv.at[mt], brecv_sem.at[0]).start()

    batch = 8
    counts = jnp.zeros((groups, LANES), F32)
    for q in range(groups // batch):
        ids = range(q * batch, (q + 1) * batch)
        lines = range(q * batch * rows_of, (q + 1) * batch * rows_of)
        dest = jnp.concatenate([dest_ref[r : r + 1, :] for r in lines], axis=1)
        aid = jnp.concatenate([aid_ref[r : r + 1, :] for r in lines], axis=1)
        home, local = look_up(dest, aid)
        for j, g in enumerate(ids):
            home_s[g : g + 1, :] = home[:, j * tok : (j + 1) * tok]
            local_s[g : g + 1, :] = local[:, j * tok : (j + 1) * tok]
        n = batch * tok
        counts += nn(
            hot(iota((groups, n), 0) == home),
            hot(iota((n, LANES), 0) // tok + q * batch == iota((n, LANES), 1)),
        )
    by_plane = nn(hot(iota((nz, groups), 0) == iota((nz, groups), 1) // NX), counts.astype(BF16))
    by_column = nn(
        counts.astype(BF16), hot(iota((LANES, LANES), 0) % NX == iota((LANES, LANES), 1))
    )
    over = (
        jnp.max(jnp.where(counts > BACK, 1.0, 0.0), axis=0, keepdims=True)
        + jnp.max(jnp.where(by_plane > ROWS_Z, 1.0, 0.0), axis=0, keepdims=True)
        + jnp.max(jnp.where(by_column > ROWS_X, 1.0, 0.0), axis=0, keepdims=True)
    )
    over_ref[0, 0] = jnp.max(over).astype(I32)

    homes_all = home_s[...]
    before = hot(
        (iota((groups, groups), 1) % NX == iota((groups, groups), 0) % NX)
        & (iota((groups, groups), 1) < iota((groups, groups), 0))
    )
    ones = jnp.ones((tok, LANES), BF16)

    def rank2(member):
        picked = hot(member)
        earlier = nn(picked, upper[...])
        total = nn(before, nn(picked, ones).astype(BF16))
        return (earlier + jnp.concatenate([total] * (tok // LANES), axis=1)).astype(I32), earlier

    here = homes_all // NX == mz
    place1 = nn(hot(here), upper[...]).astype(I32)
    slot1_s[...] = jnp.where(here & (place1 < ROWS_Z), place1, -1)
    target = jnp.full((groups, tok), -1, I32)
    for i in range(NX):
        member = homes_all == mz * NX + i
        place, _ = rank2(member)
        target = jnp.where(member & (place < ROWS_X), i * ROWS_X + place, target)
    slot2_s[...] = target
    member = homes_all == me
    place, back_rank = rank2(member)
    mine_s[0] = jnp.where(member & (place < ROWS_X), place, -1)
    mine_s[1] = jnp.where(member, back_rank.astype(I32), -1)

    def route(z, w):
        g = z * NX + mx
        first = hot(iota((ROWS_Z, tok), 0) == slot1_s[pl.ds(g, 1), :])
        second = hot(iota((slots, tok), 0) == slot2_s[pl.ds(g, 1), :])
        pick2t[pl.ds(pl.multiple_of(z * ROWS_Z, ROWS_Z), ROWS_Z), :] = nt(first, second)
        return w

    lax.fori_loop(0, nz, route, 0)
    pick2[...] = pick2t[...].T.astype(BF16)

    adp[...] = jnp.zeros_like(adp)
    acc[...] = jnp.zeros_like(acc)

    def shrink(c):
        arrived(recv2[c], recv2_sem.at[c])
        first, last = spans[c]
        rows = recv2[c][...].reshape(slots, last - first)
        return nt(rows, a_ref[:, first:last])

    def stage(c):
        arrived(recv1[c], recv1_sem.at[c])
        wide = spans[c][1] - spans[c][0]
        rows = nn(pick2[...], recv1[c][...].reshape(nz * ROWS_Z, wide))
        send2[c][...] = rows.astype(BF16).reshape(NX, ROWS_X, wide)

        for d in range(1, NX):
            to = x_of(d)
            push(
                send2[c].at[to],
                recv2[c].at[mx],
                send2_sem.at[c],
                recv2_sem.at[c],
                rep=mz * NX + to,
            )
        pltpu.make_async_copy(send2[c].at[mx], recv2[c].at[mx], recv2_sem.at[c]).start()

    def homed(g, w):
        column = lax.rem(g, NX)
        second = hot(iota((ROWS_X, tok), 0) == mine_s[0, pl.ds(g, 1), :])
        back = hot(iota((BACK, tok), 0) == mine_s[1, pl.ds(g, 1), :])
        value = (local_s[pl.ds(g, 1), :] + 1).astype(F32).astype(BF16)
        at = pl.ds(pl.multiple_of(column * ROWS_X, ROWS_X), ROWS_X)
        adp[at, :] += nt(second, jnp.broadcast_to(value, (LANES, tok)))
        back_pick[column, g // NX] = nt(back, second)
        return w

    shares = (0, 12 * groups // 32, 22 * groups // 32, groups, groups)
    for c in range(CHUNKS):
        stage(c)
        lax.fori_loop(shares[c], shares[c + 1], homed, 0)
        if c:
            acc[...] += shrink(c - 1)
    own_back = rank_in(iota((groups, tok), 0) == own_home)
    own_back = jnp.where(own_back < BACK, own_home * BACK + own_back, -1)
    column = jnp.broadcast_to(own_back.astype(F32), (LANES, tok)).T[:, 0:1].astype(I32)
    unpack = hot(iota((tok, groups * BACK), 1) == column)
    own_out = own_dest * rowcap + rank_in(iota((groups, tok), 0) == own_dest)
    got = acc[...] + shrink(CHUNKS - 1)

    wanted = adp[...].astype(I32) - 1
    lane = iota((slots, LANES), 1) // rank
    folded = jnp.zeros((slots, LANES), F32)
    for n in range(homes // per):
        folded += jnp.where(wanted == n * per + lane, got[:, n * LANES : (n + 1) * LANES], 0.0)

    low = jnp.sum(folded.T.reshape(per, rank, slots), axis=0)
    for i in range(NX):
        far_src[i] = low[:, i * LANES : (i + 1) * LANES]
    team = NEAR
    for k in sorted(range(1, peers // team), key=lambda k: -min(k, peers // team - k)):
        to = tp_of(team * k)
        push(far_src, far.at[mt // team], far_send_sem.at[0], far_recv_sem.at[0], tp=to)
    pltpu.make_async_copy(far_src, far.at[mt // team], far_recv_sem.at[0]).start()
    arrived(far, far_recv_sem.at[0])
    near_src[...] = jnp.sum(far[...], axis=0)
    first = mt // team * team
    for k in range(1, team):
        to = first + lax.rem(mt + k, team)
        push(near_src, near.at[mt - first], near_send_sem.at[0], near_recv_sem.at[0], tp=to)
    pltpu.make_async_copy(near_src, near.at[mt - first], near_recv_sem.at[0]).start()
    arrived(near, near_recv_sem.at[0])
    low_sum[...] = jnp.sum(near[...], axis=0)

    e2 = jnp.concatenate([e_ref[...], e_ref[...]], axis=1)
    lane1 = iota((ROWS_X, LANES), 1)
    for dx in (2, 1, 3, 0):
        y = x_of(dx)
        tile = jnp.concatenate([low_sum[y]] * per, axis=0).T
        chosen = adp[pl.ds(pl.multiple_of(y * ROWS_X, ROWS_X), ROWS_X), :].astype(I32) - 1
        spread = jnp.concatenate(
            [
                jnp.where(chosen == n * per + lane1 // rank, tile, 0.0)
                for n in range(homes // per)
            ],
            axis=1,
        )
        hi = spread.astype(BF16)
        lo = (spread - hi.astype(F32)).astype(BF16)
        full = nn(hi, e2) + nn(lo, e2)
        top = full.astype(BF16).astype(F32)
        pair = jnp.where(lane1 < width, full, full - top).astype(BF16)
        sel = back_pick[y].reshape(nz * BACK, LANES).astype(BF16)
        rows = nn(sel, pair)
        for z in range(nz):
            xsend[z * NX + y] = rows[z * BACK : (z + 1) * BACK].astype(BF16)
        for dz in z_steps + [0]:
            if dz or dx:
                to = z_of(dz) * NX + y
                push(xsend.at[to], xrecv.at[me], xsend_sem.at[0], xrecv_sem.at[0], rep=to)
    pltpu.make_async_copy(xsend.at[me], xrecv.at[me], xrecv_sem.at[0]).start()

    arrived(brecv, brecv_sem.at[0])
    base = jnp.sum(brecv[...], axis=0)

    arrived(xrecv, xrecv_sem.at[0])
    extra = nn(unpack, xrecv[...].reshape(groups * BACK, LANES)).T
    total = (base + extra[:width] + extra[width:]).astype(BF16)
    blank = jnp.zeros_like(total)
    sides = jnp.concatenate(
        [jnp.concatenate([total, blank], axis=1), jnp.concatenate([blank, total], axis=1)], axis=0
    )
    line = iota((NX * TILE, tok), 0)
    for dz in z_steps + [0]:
        z = z_of(dz)
        slot = z * NX * rowcap + line // TILE * rowcap + line % TILE
        high = (slot + TILE == own_out) & (line % TILE < rowcap - TILE)
        rows = nt(jnp.concatenate([hot(slot == own_out), hot(high)], axis=1), sides)
        for i in range(NX):
            osend[z * NX + i] = rows[i * TILE : (i + 1) * TILE].astype(BF16)
        for dx in range(NX):
            if dz or dx:
                to = z * NX + x_of(dx)
                push(osend.at[to], orecv.at[me], osend_sem.at[0], orecv_sem.at[0], rep=to)
    pltpu.make_async_copy(osend.at[me], orecv.at[me], orecv_sem.at[0]).start()

    for c in range(CHUNKS):
        arrived(send1[c].at[pl.ds(0, nz - 1)], send1_sem.at[c])
        arrived(send2[c].at[pl.ds(0, NX - 1)], send2_sem.at[c])
    arrived(bsend.at[pl.ds(0, peers - 1)], bsend_sem.at[0])
    arrived(far.at[pl.ds(0, peers // team - 1)], far_send_sem.at[0])
    arrived(near.at[pl.ds(0, team - 1)], near_send_sem.at[0])
    arrived(xsend.at[pl.ds(0, groups - 1)], xsend_sem.at[0])
    arrived(osend.at[pl.ds(0, groups - 1)], osend_sem.at[0])
    arrived(orecv, orecv_sem.at[0])
    done = orecv[...].astype(F32)
    out_ref[:, :TILE, :] = done[:, :, :width].astype(BF16)
    out_ref[:, TILE:, :] = done[:, : rowcap - TILE, width:].astype(BF16)


def hot_value(a):
    return a.astype(F32).astype(BF16)


def fused(groups, peers, requests, value_weight, shrink, expand, dest, aid, lists, table):
    tok, depth = requests.shape
    width = expand.shape[1]
    rowcap = 3 * tok // groups
    nz, slots = groups // NX, NX * ROWS_X
    rank = shrink.shape[0] * groups // (table.size)
    wide = [last - first for first, last in spans_of(depth)]
    vmem = pl.BlockSpec(memory_space=pltpu.VMEM)
    dma = pltpu.SemaphoreType.DMA
    return pl.pallas_call(
        functools.partial(fused_kernel, groups, peers),
        out_shape=[
            jax.ShapeDtypeStruct((groups, rowcap, width), BF16),
            jax.ShapeDtypeStruct((1, 1), I32),
        ],
        in_specs=[vmem] * 8,
        out_specs=[vmem, pl.BlockSpec(memory_space=pltpu.SMEM)],
        scratch_shapes=[
            [pltpu.VMEM((nz, ROWS_Z, n), BF16) for n in wide],
            [pltpu.VMEM((nz, ROWS_Z, n), BF16) for n in wide],
            [pltpu.VMEM((NX, ROWS_X, n), BF16) for n in wide],
            [pltpu.VMEM((NX, ROWS_X, n), BF16) for n in wide],
            pltpu.VMEM((peers, width, tok), F32),
            pltpu.VMEM((peers, width, tok), F32),
            pltpu.VMEM((slots, shrink.shape[0]), F32),
            pltpu.VMEM((nz * ROWS_Z, slots), F32),
            pltpu.VMEM((slots, nz * ROWS_Z), BF16),
            pltpu.VMEM((tok, tok), BF16),
            pltpu.VMEM((2 * groups, lists.shape[1]), BF16),
            pltpu.VMEM((groups, tok), I32),
            pltpu.VMEM((groups, tok), I32),
            pltpu.VMEM((groups, tok), I32),
            pltpu.VMEM((groups, tok), I32),
            pltpu.VMEM((2, groups, tok), I32),
            pltpu.VMEM((slots, LANES), F32),
            pltpu.VMEM((NX, nz, BACK, LANES), F32),
            pltpu.VMEM((NX, rank, LANES), F32),
            pltpu.VMEM((peers // NEAR, NX, rank, LANES), F32),
            pltpu.VMEM((NX, rank, LANES), F32),
            pltpu.VMEM((NEAR, NX, rank, LANES), F32),
            pltpu.VMEM((NX, rank, LANES), F32),
            pltpu.VMEM((groups, BACK, LANES), BF16),
            pltpu.VMEM((groups, BACK, LANES), BF16),
            pltpu.VMEM((groups, TILE, LANES), BF16),
            pltpu.VMEM((groups, TILE, LANES), BF16),
            *[dma((CHUNKS,))] * 4,
            *[dma((1,))] * 10,
        ],
        compiler_params=pltpu.CompilerParams(
            collective_id=0, has_side_effects=True, vmem_limit_bytes=48 * 1024 * 1024
        ),
        name="fused",
    )(requests, value_weight, shrink, expand, dest, aid, lists, table)


def on_device(
    requests,
    value_weight,
    shrink_weight,
    expand_weight,
    destination,
    adapter_ids,
    cache_lists,
    home_table,
):
    groups = lax.axis_size("rep")
    tok = requests.shape[0]
    home_count, rank, depth = shrink_weight.shape
    width = expand_weight.shape[2]
    out, over = fused(
        groups,
        lax.axis_size("tp"),
        requests,
        value_weight,
        shrink_weight.reshape(home_count * rank, depth),
        expand_weight.reshape(home_count * rank, width),
        destination.reshape(-1, LANES),
        adapter_ids.reshape(-1, LANES),
        cache_lists,
        home_table.reshape(-1, LANES),
    )
    out = out.reshape(-1, width)

    def any_input(out):
        return by_serving_group(
            requests,
            value_weight,
            shrink_weight,
            expand_weight,
            destination,
            adapter_ids,
            cache_lists,
            home_table,
        )

    return lax.cond(over[0, 0] > 0, any_input, lambda out: out, out)


def solution(mesh):
    in_specs = (
        P("rep", "tp"),
        P("tp", None),
        P("rep", None, "tp"),
        P("rep", None, "tp"),
        P(),
        P(),
        P(),
        P(),
    )
    out_specs = P("rep", "tp")
    return jax.shard_map(
        on_device, mesh=mesh, in_specs=in_specs, out_specs=out_specs, check_vma=False
    )
```

```python
import functools

import jax
import jax.numpy as jnp
from jax import lax
from jax.experimental import pallas as pl
from jax.experimental.pallas import tpu as pltpu
from jax.sharding import PartitionSpec as P

PAIR = 2


def by_serving_group(
    requests,
    value_weight,
    shrink_weight,
    expand_weight,
    destination,
    adapter_ids,
    cache_lists,
    home_table,
):
    groups = lax.axis_size("rep")
    own_group = lax.axis_index("rep")
    tok_dev = requests.shape[0]
    rowcap = 3 * tok_dev // groups
    buffer_rows = groups * rowcap
    home_count = shrink_weight.shape[0]
    cache_len = cache_lists.shape[1]
    rank_width = shrink_weight.shape[1]
    width_out = expand_weight.shape[2]
    places = jnp.arange(cache_len, dtype=jnp.int32)
    blocks = destination.reshape(groups, tok_dev)
    targets = jnp.arange(groups, dtype=jnp.int32)
    member = (blocks[:, :, None] == targets[None, None, :]).astype(jnp.int32)
    earlier = jnp.sum(member * (jnp.cumsum(member, axis=1) - 1), axis=2)
    slot_all = targets[:, None] * rowcap + earlier
    own_slot = lax.dynamic_index_in_dim(
        blocks, own_group, 0, keepdims=False
    ) * rowcap + lax.dynamic_index_in_dim(earlier, own_group, 0, keepdims=False)
    send_rows = (
        jnp.zeros((buffer_rows, requests.shape[1]), requests.dtype).at[own_slot].set(requests)
    )
    arrived = lax.all_to_all(send_rows, "rep", split_axis=0, concat_axis=0, tiled=True)
    landing = jnp.where(blocks == own_group, slot_all, buffer_rows).reshape(-1)
    slot_place = jnp.full((buffer_rows,), -1, jnp.int32).at[landing].set(adapter_ids, mode="drop")
    selector = (slot_place[:, None] == places[None, :]).astype(jnp.float32)
    positions = home_table[cache_lists]
    home_group = positions // home_count
    local_slot = positions % home_count
    homed_here = home_group == own_group
    ranking = jnp.cumsum(homed_here.astype(jnp.int32), axis=1) - 1
    outgoing = jnp.where(homed_here, targets[:, None] * PAIR + ranking, groups * PAIR).reshape(-1)
    send_index = (
        jnp.zeros((groups * PAIR,), jnp.int32).at[outgoing].set(local_slot.reshape(-1), mode="drop")
    )
    send_valid = (
        jnp.zeros((groups * PAIR,), jnp.bfloat16).at[outgoing].set(jnp.bfloat16(1.0), mode="drop")
    )
    send_down = shrink_weight[send_index] * send_valid[:, None, None]
    send_up = expand_weight[send_index] * send_valid[:, None, None]
    got_down, got_up = (
        lax.all_to_all(send_down, "rep", split_axis=0, concat_axis=0, tiled=True),
        lax.all_to_all(send_up, "rep", split_axis=0, concat_axis=0, tiled=True),
    )
    own_homes = lax.dynamic_index_in_dim(home_group, own_group, 0, keepdims=False)
    same_before = jnp.sum(
        ((own_homes[None, :] == own_homes[:, None]) & (places[None, :] < places[:, None])).astype(
            jnp.int32
        ),
        axis=1,
    )
    fetch_index = own_homes * PAIR + same_before
    cached_down = got_down[fetch_index].reshape(cache_len * rank_width, -1)
    cached_up = got_up[fetch_index].reshape(cache_len * rank_width, width_out).astype(jnp.float32)
    shrunk_all = lax.dot_general(
        arrived, cached_down, (((1,), (1,)), ((), ())), preferred_element_type=jnp.float32
    )
    shrunk_part = jnp.sum(
        shrunk_all.reshape(buffer_rows, cache_len, rank_width) * selector[:, :, None], axis=1
    )
    peers = lax.axis_size("tp")
    pieces = lax.all_to_all(shrunk_part, "tp", split_axis=0, concat_axis=0, tiled=True)
    piece = jnp.sum(pieces.reshape(peers, -1, rank_width), axis=0)
    shrunk = lax.all_to_all(
        jnp.tile(piece, (peers, 1)), "tp", split_axis=0, concat_axis=0, tiled=True
    )
    spread_rows = (selector[:, :, None] * shrunk[:, None, :]).reshape(
        buffer_rows, cache_len * rank_width
    )
    expanded = jnp.dot(spread_rows, cached_up, precision=lax.Precision.HIGHEST)
    partial_all = jnp.dot(arrived, value_weight, preferred_element_type=jnp.float32)
    columns = lax.all_to_all(partial_all, "tp", split_axis=1, concat_axis=0, tiled=True)
    projected = jnp.sum(columns.reshape(peers, buffer_rows, width_out), axis=0)
    return (projected + expanded).astype(jnp.bfloat16)


MESH = pl.DeviceIdType.MESH
NX = 4
ROWS_Z = 64
ROWS_X = 128
BACK = 32
EIGHTHS = (3, 2, 2, 1)
CHUNKS = len(EIGHTHS)
LANES = 128
TILE = 16
NEAR = 4
F32, BF16, I32 = jnp.float32, jnp.bfloat16, jnp.int32


def hot(mask):
    return mask.astype(F32).astype(BF16)


def iota(shape, axis):
    return lax.broadcasted_iota(I32, shape, axis)


def nn(a, b):
    return jnp.dot(a, b, preferred_element_type=F32)


def nt(a, b):
    return lax.dot_general(a, b, (((1,), (1,)), ((), ())), preferred_element_type=F32)


def spans_of(depth):
    ends = [depth * sum(EIGHTHS[:c]) // sum(EIGHTHS) for c in range(CHUNKS + 1)]
    return list(zip(ends[:-1], ends[1:]))


def fused_kernel(
    groups,
    peers,
    x_hbm,
    v_hbm,
    a_hbm,
    e_hbm,
    dest_ref,
    aid_ref,
    list_ref,
    table_ref,
    out_ref,
    over_ref,
    x_ref,
    v_ref,
    a_ref,
    e_ref,
    send1,
    recv1,
    send2,
    recv2,
    bsend,
    brecv,
    acc,
    pick2t,
    pick2,
    upper,
    entries,
    home_s,
    local_s,
    slot1_s,
    slot2_s,
    mine_s,
    adp,
    back_pick,
    far_src,
    far,
    near_src,
    near,
    low_sum,
    xsend,
    xrecv,
    osend,
    orecv,
    send1_sem,
    recv1_sem,
    send2_sem,
    recv2_sem,
    bsend_sem,
    brecv_sem,
    far_send_sem,
    far_recv_sem,
    near_send_sem,
    near_recv_sem,
    xsend_sem,
    xrecv_sem,
    osend_sem,
    orecv_sem,
    load_sem,
):
    me = lax.axis_index("rep")
    mt = lax.axis_index("tp")
    mz, mx = me // NX, me % NX
    nz = groups // NX
    tok, depth = x_ref.shape
    spans = spans_of(depth)
    cache = list_ref.shape[1]
    homes = table_ref.shape[0] * LANES // groups
    rank = a_ref.shape[0] // homes
    rows_of = tok // LANES
    per = LANES // rank
    slots = NX * ROWS_X
    rowcap = out_ref.shape[1]

    loads = [
        pltpu.make_async_copy(src, dst, load_sem.at[i])
        for i, (src, dst) in enumerate(
            [(x_hbm, x_ref), (v_hbm, v_ref), (a_hbm, a_ref), (e_hbm, e_ref)]
        )
    ]
    for load in loads:
        load.start()

    barrier = pltpu.get_barrier_semaphore()

    def z_of(d):
        return lax.rem(mz + d, nz)

    def x_of(d):
        return lax.rem(mx + d, NX)

    def tp_of(d):
        return lax.rem(mt + d, peers)

    def greet(**where):
        pl.semaphore_signal(barrier, inc=1, device_id=where, device_id_type=MESH)

    z_steps = sorted(range(1, nz), key=lambda d: -min(d, nz - d))
    for d in z_steps:
        greet(rep=z_of(d) * NX + mx)
    for d in range(1, peers):
        greet(tp=tp_of(d))
    for d in range(1, NX):
        greet(rep=mz * NX + x_of(d))

    upper[...] = hot(iota((tok, tok), 0) < iota((tok, tok), 1))

    count = groups * cache
    lists = list_ref[...]
    place_of = hot(iota((cache, count), 0) == iota((cache, count), 1) % cache)
    owner = iota((groups, count), 1) // cache == iota((groups, count), 0)
    high = jnp.where(owner, nn(hot_value(lists // LANES), place_of), 0.0)
    low = jnp.where(owner, nn(hot_value(lists % LANES), place_of), 0.0)
    high = jnp.sum(high, axis=0, keepdims=True).astype(I32)
    low = jnp.sum(low, axis=0, keepdims=True).astype(I32)
    table = table_ref[...]
    both = jnp.concatenate([hot_value(table // homes), hot_value(table % homes)], axis=0)
    major = iota((table.shape[0], count), 0) == high
    minor = iota((LANES, count), 0) == low
    found = nn(both, hot(minor))
    of_home = jnp.sum(jnp.where(major, found[: table.shape[0]], 0.0), axis=0, keepdims=True)
    of_local = jnp.sum(jnp.where(major, found[table.shape[0] :], 0.0), axis=0, keepdims=True)
    spread = jnp.concatenate(
        [jnp.where(owner, of_home, 0.0), jnp.where(owner, of_local, 0.0)], axis=0
    ).astype(BF16)
    entries[...] = nn(spread, hot(iota((count, cache), 0) % cache == iota((count, cache), 1))).astype(
        BF16
    )

    def look_up(dest, aid):
        n = dest.shape[1]
        rows = nn(entries[...], hot(iota((cache, n), 0) == aid))
        serve = iota((groups, n), 0) == dest
        home = jnp.sum(jnp.where(serve, rows[:groups], 0.0), axis=0, keepdims=True)
        local = jnp.sum(jnp.where(serve, rows[groups:], 0.0), axis=0, keepdims=True)
        return home.astype(I32), local.astype(I32)

    def rank_in(member):
        earlier = nn(hot(member), upper[...])
        return jnp.sum(jnp.where(member, earlier, 0.0), axis=0, keepdims=True).astype(I32)

    def own(ref):
        return jnp.concatenate([ref[pl.ds(rows_of * me + i, 1), :] for i in range(rows_of)], axis=1)

    own_dest = own(dest_ref)
    own_home, _ = look_up(own_dest, own(aid_ref))
    own_plane = own_home // NX
    own_rank1 = rank_in(iota((nz, tok), 0) == own_plane)
    own_slot1 = jnp.where(own_rank1 < ROWS_Z, own_plane * ROWS_Z + own_rank1, -1)
    pick1 = hot(iota((nz * ROWS_Z, tok), 0) == own_slot1)

    def pack(c):
        first, last = spans[c]
        rows = nn(pick1, x_ref[:, first:last])
        send1[c][...] = rows.astype(BF16).reshape(nz, ROWS_Z, last - first)

    loads[0].wait()
    pack(0)
    pl.semaphore_wait(barrier, nz + NX + peers - 3)

    def arrived(buffer, sem):
        pltpu.make_async_copy(buffer, buffer, sem).wait()

    def push(src, dst, ssem, rsem, **where):
        pltpu.make_async_remote_copy(
            src_ref=src,
            dst_ref=dst,
            send_sem=ssem,
            recv_sem=rsem,
            device_id=where,
            device_id_type=MESH,
        ).start()

    def z_start(c):
        for d in z_steps:
            to = z_of(d)
            push(
                send1[c].at[to],
                recv1[c].at[mz],
                send1_sem.at[c],
                recv1_sem.at[c],
                rep=to * NX + mx,
            )
        pltpu.make_async_copy(send1[c].at[mz], recv1[c].at[mz], recv1_sem.at[c]).start()

    z_start(0)
    for c in range(1, CHUNKS):
        pack(c)
        z_start(c)

    width = bsend.shape[1]
    loads[1].wait()
    step = 256
    for n in range(v_ref.shape[1] // step):
        bt = nn(x_ref[...], v_ref[:, n * step : (n + 1) * step]).T
        for i in range(step // width):
            bsend[n * (step // width) + i] = bt[i * width : (i + 1) * width]

    for d in range(1, peers):
        to = tp_of(d)
        push(bsend.at[to], brecv.at[mt], bsend_sem.at[0], brecv_sem.at[0], tp=to)
    pltpu.make_async_copy(bsend.at[mt], brecv.at[mt], brecv_sem.at[0]).start()

    batch = 8
    counts = jnp.zeros((groups, LANES), F32)
    for q in range(groups // batch):
        ids = range(q * batch, (q + 1) * batch)
        lines = range(q * batch * rows_of, (q + 1) * batch * rows_of)
        dest = jnp.concatenate([dest_ref[r : r + 1, :] for r in lines], axis=1)
        aid = jnp.concatenate([aid_ref[r : r + 1, :] for r in lines], axis=1)
        home, local = look_up(dest, aid)
        for j, g in enumerate(ids):
            home_s[g : g + 1, :] = home[:, j * tok : (j + 1) * tok]
            local_s[g : g + 1, :] = local[:, j * tok : (j + 1) * tok]
        n = batch * tok
        counts += nn(
            hot(iota((groups, n), 0) == home),
            hot(iota((n, LANES), 0) // tok + q * batch == iota((n, LANES), 1)),
        )
    by_plane = nn(hot(iota((nz, groups), 0) == iota((nz, groups), 1) // NX), counts.astype(BF16))
    by_column = nn(
        counts.astype(BF16), hot(iota((LANES, LANES), 0) % NX == iota((LANES, LANES), 1))
    )
    over = (
        jnp.max(jnp.where(counts > BACK, 1.0, 0.0), axis=0, keepdims=True)
        + jnp.max(jnp.where(by_plane > ROWS_Z, 1.0, 0.0), axis=0, keepdims=True)
        + jnp.max(jnp.where(by_column > ROWS_X, 1.0, 0.0), axis=0, keepdims=True)
    )
    over_ref[0, 0] = jnp.max(over).astype(I32)

    homes_all = home_s[...]
    before = hot(
        (iota((groups, groups), 1) % NX == iota((groups, groups), 0) % NX)
        & (iota((groups, groups), 1) < iota((groups, groups), 0))
    )
    ones = jnp.ones((tok, LANES), BF16)

    def rank2(member):
        picked = hot(member)
        earlier = nn(picked, upper[...])
        total = nn(before, nn(picked, ones).astype(BF16))
        return (earlier + jnp.concatenate([total] * (tok // LANES), axis=1)).astype(I32), earlier

    here = homes_all // NX == mz
    place1 = nn(hot(here), upper[...]).astype(I32)
    slot1_s[...] = jnp.where(here & (place1 < ROWS_Z), place1, -1)
    target = jnp.full((groups, tok), -1, I32)
    for i in range(NX):
        member = homes_all == mz * NX + i
        place, _ = rank2(member)
        target = jnp.where(member & (place < ROWS_X), i * ROWS_X + place, target)
    slot2_s[...] = target
    member = homes_all == me
    place, back_rank = rank2(member)
    mine_s[0] = jnp.where(member & (place < ROWS_X), place, -1)
    mine_s[1] = jnp.where(member, back_rank.astype(I32), -1)

    def route(z, w):
        g = z * NX + mx
        first = hot(iota((ROWS_Z, tok), 0) == slot1_s[pl.ds(g, 1), :])
        second = hot(iota((slots, tok), 0) == slot2_s[pl.ds(g, 1), :])
        pick2t[pl.ds(pl.multiple_of(z * ROWS_Z, ROWS_Z), ROWS_Z), :] = nt(first, second)
        return w

    lax.fori_loop(0, nz, route, 0)
    pick2[...] = pick2t[...].T.astype(BF16)

    loads[2].wait()
    loads[3].wait()
    adp[...] = jnp.zeros_like(adp)
    acc[...] = jnp.zeros_like(acc)

    def shrink(c):
        arrived(recv2[c], recv2_sem.at[c])
        first, last = spans[c]
        rows = recv2[c][...].reshape(slots, last - first)
        return nt(rows, a_ref[:, first:last])

    def stage(c):
        arrived(recv1[c], recv1_sem.at[c])
        wide = spans[c][1] - spans[c][0]
        rows = nn(pick2[...], recv1[c][...].reshape(nz * ROWS_Z, wide))
        send2[c][...] = rows.astype(BF16).reshape(NX, ROWS_X, wide)

        for d in range(1, NX):
            to = x_of(d)
            push(
                send2[c].at[to],
                recv2[c].at[mx],
                send2_sem.at[c],
                recv2_sem.at[c],
                rep=mz * NX + to,
            )
        pltpu.make_async_copy(send2[c].at[mx], recv2[c].at[mx], recv2_sem.at[c]).start()

    def homed(g, w):
        column = lax.rem(g, NX)
        second = hot(iota((ROWS_X, tok), 0) == mine_s[0, pl.ds(g, 1), :])
        back = hot(iota((BACK, tok), 0) == mine_s[1, pl.ds(g, 1), :])
        value = (local_s[pl.ds(g, 1), :] + 1).astype(F32).astype(BF16)
        at = pl.ds(pl.multiple_of(column * ROWS_X, ROWS_X), ROWS_X)
        adp[at, :] += nt(second, jnp.broadcast_to(value, (LANES, tok)))
        back_pick[column, g // NX] = nt(back, second)
        return w

    shares = (0, 12 * groups // 32, 22 * groups // 32, groups, groups)
    for c in range(CHUNKS):
        stage(c)
        lax.fori_loop(shares[c], shares[c + 1], homed, 0)
        if c:
            acc[...] += shrink(c - 1)
    own_back = rank_in(iota((groups, tok), 0) == own_home)
    own_back = jnp.where(own_back < BACK, own_home * BACK + own_back, -1)
    column = jnp.broadcast_to(own_back.astype(F32), (LANES, tok)).T[:, 0:1].astype(I32)
    unpack = hot(iota((tok, groups * BACK), 1) == column)
    own_out = own_dest * rowcap + rank_in(iota((groups, tok), 0) == own_dest)
    got = acc[...] + shrink(CHUNKS - 1)

    wanted = adp[...].astype(I32) - 1
    lane = iota((slots, LANES), 1) // rank
    folded = jnp.zeros((slots, LANES), F32)
    for n in range(homes // per):
        folded += jnp.where(wanted == n * per + lane, got[:, n * LANES : (n + 1) * LANES], 0.0)

    low = jnp.sum(folded.T.reshape(per, rank, slots), axis=0)
    for i in range(NX):
        far_src[i] = low[:, i * LANES : (i + 1) * LANES]
    team = NEAR
    for k in sorted(range(1, peers // team), key=lambda k: -min(k, peers // team - k)):
        to = tp_of(team * k)
        push(far_src, far.at[mt // team], far_send_sem.at[0], far_recv_sem.at[0], tp=to)
    pltpu.make_async_copy(far_src, far.at[mt // team], far_recv_sem.at[0]).start()
    arrived(far, far_recv_sem.at[0])
    near_src[...] = jnp.sum(far[...], axis=0)
    first = mt // team * team
    for k in range(1, team):
        to = first + lax.rem(mt + k, team)
        push(near_src, near.at[mt - first], near_send_sem.at[0], near_recv_sem.at[0], tp=to)
    pltpu.make_async_copy(near_src, near.at[mt - first], near_recv_sem.at[0]).start()
    arrived(near, near_recv_sem.at[0])
    low_sum[...] = jnp.sum(near[...], axis=0)

    e2 = jnp.concatenate([e_ref[...], e_ref[...]], axis=1)
    lane1 = iota((ROWS_X, LANES), 1)
    for dx in (2, 1, 3, 0):
        y = x_of(dx)
        tile = jnp.concatenate([low_sum[y]] * per, axis=0).T
        chosen = adp[pl.ds(pl.multiple_of(y * ROWS_X, ROWS_X), ROWS_X), :].astype(I32) - 1
        spread = jnp.concatenate(
            [
                jnp.where(chosen == n * per + lane1 // rank, tile, 0.0)
                for n in range(homes // per)
            ],
            axis=1,
        )
        hi = spread.astype(BF16)
        lo = (spread - hi.astype(F32)).astype(BF16)
        full = nn(hi, e2) + nn(lo, e2)
        top = full.astype(BF16).astype(F32)
        pair = jnp.where(lane1 < width, full, full - top).astype(BF16)
        sel = back_pick[y].reshape(nz * BACK, LANES).astype(BF16)
        rows = nn(sel, pair)
        for z in range(nz):
            xsend[z * NX + y] = rows[z * BACK : (z + 1) * BACK].astype(BF16)
        for dz in z_steps + [0]:
            if dz or dx:
                to = z_of(dz) * NX + y
                push(xsend.at[to], xrecv.at[me], xsend_sem.at[0], xrecv_sem.at[0], rep=to)
    pltpu.make_async_copy(xsend.at[me], xrecv.at[me], xrecv_sem.at[0]).start()

    arrived(brecv, brecv_sem.at[0])
    base = jnp.sum(brecv[...], axis=0)

    arrived(xrecv, xrecv_sem.at[0])
    extra = nn(unpack, xrecv[...].reshape(groups * BACK, LANES)).T
    total = (base + extra[:width] + extra[width:]).astype(BF16)
    blank = jnp.zeros_like(total)
    sides = jnp.concatenate(
        [jnp.concatenate([total, blank], axis=1), jnp.concatenate([blank, total], axis=1)], axis=0
    )
    line = iota((NX * TILE, tok), 0)
    for dz in z_steps + [0]:
        z = z_of(dz)
        slot = z * NX * rowcap + line // TILE * rowcap + line % TILE
        high = (slot + TILE == own_out) & (line % TILE < rowcap - TILE)
        rows = nt(jnp.concatenate([hot(slot == own_out), hot(high)], axis=1), sides)
        for i in range(NX):
            osend[z * NX + i] = rows[i * TILE : (i + 1) * TILE].astype(BF16)
        for dx in range(NX):
            if dz or dx:
                to = z * NX + x_of(dx)
                push(osend.at[to], orecv.at[me], osend_sem.at[0], orecv_sem.at[0], rep=to)
    pltpu.make_async_copy(osend.at[me], orecv.at[me], orecv_sem.at[0]).start()

    for c in range(CHUNKS):
        arrived(send1[c].at[pl.ds(0, nz - 1)], send1_sem.at[c])
        arrived(send2[c].at[pl.ds(0, NX - 1)], send2_sem.at[c])
    arrived(bsend.at[pl.ds(0, peers - 1)], bsend_sem.at[0])
    arrived(far.at[pl.ds(0, peers // team - 1)], far_send_sem.at[0])
    arrived(near.at[pl.ds(0, team - 1)], near_send_sem.at[0])
    arrived(xsend.at[pl.ds(0, groups - 1)], xsend_sem.at[0])
    arrived(osend.at[pl.ds(0, groups - 1)], osend_sem.at[0])
    arrived(orecv, orecv_sem.at[0])
    done = orecv[...].astype(F32)
    out_ref[:, :TILE, :] = done[:, :, :width].astype(BF16)
    out_ref[:, TILE:, :] = done[:, : rowcap - TILE, width:].astype(BF16)


def hot_value(a):
    return a.astype(F32).astype(BF16)


def fused(groups, peers, requests, value_weight, shrink, expand, dest, aid, lists, table):
    tok, depth = requests.shape
    width = expand.shape[1]
    rowcap = 3 * tok // groups
    nz, slots = groups // NX, NX * ROWS_X
    rank = shrink.shape[0] * groups // (table.size)
    wide = [last - first for first, last in spans_of(depth)]
    vmem = pl.BlockSpec(memory_space=pltpu.VMEM)
    dma = pltpu.SemaphoreType.DMA
    return pl.pallas_call(
        functools.partial(fused_kernel, groups, peers),
        out_shape=[
            jax.ShapeDtypeStruct((groups, rowcap, width), BF16),
            jax.ShapeDtypeStruct((1, 1), I32),
        ],
        in_specs=[pl.BlockSpec(memory_space=pl.ANY)] * 4 + [vmem] * 4,
        out_specs=[vmem, pl.BlockSpec(memory_space=pltpu.SMEM)],
        scratch_shapes=[
            pltpu.VMEM(requests.shape, BF16),
            pltpu.VMEM(value_weight.shape, BF16),
            pltpu.VMEM(shrink.shape, BF16),
            pltpu.VMEM(expand.shape, BF16),
            [pltpu.VMEM((nz, ROWS_Z, n), BF16) for n in wide],
            [pltpu.VMEM((nz, ROWS_Z, n), BF16) for n in wide],
            [pltpu.VMEM((NX, ROWS_X, n), BF16) for n in wide],
            [pltpu.VMEM((NX, ROWS_X, n), BF16) for n in wide],
            pltpu.VMEM((peers, width, tok), F32),
            pltpu.VMEM((peers, width, tok), F32),
            pltpu.VMEM((slots, shrink.shape[0]), F32),
            pltpu.VMEM((nz * ROWS_Z, slots), F32),
            pltpu.VMEM((slots, nz * ROWS_Z), BF16),
            pltpu.VMEM((tok, tok), BF16),
            pltpu.VMEM((2 * groups, lists.shape[1]), BF16),
            pltpu.VMEM((groups, tok), I32),
            pltpu.VMEM((groups, tok), I32),
            pltpu.VMEM((groups, tok), I32),
            pltpu.VMEM((groups, tok), I32),
            pltpu.VMEM((2, groups, tok), I32),
            pltpu.VMEM((slots, LANES), F32),
            pltpu.VMEM((NX, nz, BACK, LANES), F32),
            pltpu.VMEM((NX, rank, LANES), F32),
            pltpu.VMEM((peers // NEAR, NX, rank, LANES), F32),
            pltpu.VMEM((NX, rank, LANES), F32),
            pltpu.VMEM((NEAR, NX, rank, LANES), F32),
            pltpu.VMEM((NX, rank, LANES), F32),
            pltpu.VMEM((groups, BACK, LANES), BF16),
            pltpu.VMEM((groups, BACK, LANES), BF16),
            pltpu.VMEM((groups, TILE, LANES), BF16),
            pltpu.VMEM((groups, TILE, LANES), BF16),
            *[dma((CHUNKS,))] * 4,
            *[dma((1,))] * 10,
            dma((4,)),
        ],
        compiler_params=pltpu.CompilerParams(
            collective_id=0, has_side_effects=True, vmem_limit_bytes=63 * 1024 * 1024
        ),
        name="fused",
    )(requests, value_weight, shrink, expand, dest, aid, lists, table)


def on_device(
    requests,
    value_weight,
    shrink_weight,
    expand_weight,
    destination,
    adapter_ids,
    cache_lists,
    home_table,
):
    groups = lax.axis_size("rep")
    tok = requests.shape[0]
    home_count, rank, depth = shrink_weight.shape
    width = expand_weight.shape[2]
    out, over = fused(
        groups,
        lax.axis_size("tp"),
        requests,
        value_weight,
        shrink_weight.reshape(home_count * rank, depth),
        expand_weight.reshape(home_count * rank, width),
        destination.reshape(-1, LANES),
        adapter_ids.reshape(-1, LANES),
        cache_lists,
        home_table.reshape(-1, LANES),
    )
    out = out.reshape(-1, width)

    def any_input(out):
        return by_serving_group(
            requests,
            value_weight,
            shrink_weight,
            expand_weight,
            destination,
            adapter_ids,
            cache_lists,
            home_table,
        )

    return lax.cond(over[0, 0] > 0, any_input, lambda out: out, out)


def solution(mesh):
    in_specs = (
        P("rep", "tp"),
        P("tp", None),
        P("rep", None, "tp"),
        P("rep", None, "tp"),
        P(),
        P(),
        P(),
        P(),
    )
    out_specs = P("rep", "tp")
    return jax.shard_map(
        on_device, mesh=mesh, in_specs=in_specs, out_specs=out_specs, check_vma=False
    )
```

```python
import functools

import jax
import jax.numpy as jnp
from jax import lax
from jax.experimental import pallas as pl
from jax.experimental.pallas import tpu as pltpu
from jax.sharding import PartitionSpec as P

PAIR = 2


def by_serving_group(
    requests,
    value_weight,
    shrink_weight,
    expand_weight,
    destination,
    adapter_ids,
    cache_lists,
    home_table,
):
    groups = lax.axis_size("rep")
    own_group = lax.axis_index("rep")
    tok_dev = requests.shape[0]
    rowcap = 3 * tok_dev // groups
    buffer_rows = groups * rowcap
    home_count = shrink_weight.shape[0]
    cache_len = cache_lists.shape[1]
    rank_width = shrink_weight.shape[1]
    width_out = expand_weight.shape[2]
    places = jnp.arange(cache_len, dtype=jnp.int32)
    blocks = destination.reshape(groups, tok_dev)
    targets = jnp.arange(groups, dtype=jnp.int32)
    member = (blocks[:, :, None] == targets[None, None, :]).astype(jnp.int32)
    earlier = jnp.sum(member * (jnp.cumsum(member, axis=1) - 1), axis=2)
    slot_all = targets[:, None] * rowcap + earlier
    own_slot = lax.dynamic_index_in_dim(
        blocks, own_group, 0, keepdims=False
    ) * rowcap + lax.dynamic_index_in_dim(earlier, own_group, 0, keepdims=False)
    send_rows = (
        jnp.zeros((buffer_rows, requests.shape[1]), requests.dtype).at[own_slot].set(requests)
    )
    arrived = lax.all_to_all(send_rows, "rep", split_axis=0, concat_axis=0, tiled=True)
    landing = jnp.where(blocks == own_group, slot_all, buffer_rows).reshape(-1)
    slot_place = jnp.full((buffer_rows,), -1, jnp.int32).at[landing].set(adapter_ids, mode="drop")
    selector = (slot_place[:, None] == places[None, :]).astype(jnp.float32)
    positions = home_table[cache_lists]
    home_group = positions // home_count
    local_slot = positions % home_count
    homed_here = home_group == own_group
    ranking = jnp.cumsum(homed_here.astype(jnp.int32), axis=1) - 1
    outgoing = jnp.where(homed_here, targets[:, None] * PAIR + ranking, groups * PAIR).reshape(-1)
    send_index = (
        jnp.zeros((groups * PAIR,), jnp.int32).at[outgoing].set(local_slot.reshape(-1), mode="drop")
    )
    send_valid = (
        jnp.zeros((groups * PAIR,), jnp.bfloat16).at[outgoing].set(jnp.bfloat16(1.0), mode="drop")
    )
    send_down = shrink_weight[send_index] * send_valid[:, None, None]
    send_up = expand_weight[send_index] * send_valid[:, None, None]
    got_down, got_up = (
        lax.all_to_all(send_down, "rep", split_axis=0, concat_axis=0, tiled=True),
        lax.all_to_all(send_up, "rep", split_axis=0, concat_axis=0, tiled=True),
    )
    own_homes = lax.dynamic_index_in_dim(home_group, own_group, 0, keepdims=False)
    same_before = jnp.sum(
        ((own_homes[None, :] == own_homes[:, None]) & (places[None, :] < places[:, None])).astype(
            jnp.int32
        ),
        axis=1,
    )
    fetch_index = own_homes * PAIR + same_before
    cached_down = got_down[fetch_index].reshape(cache_len * rank_width, -1)
    cached_up = got_up[fetch_index].reshape(cache_len * rank_width, width_out).astype(jnp.float32)
    shrunk_all = lax.dot_general(
        arrived, cached_down, (((1,), (1,)), ((), ())), preferred_element_type=jnp.float32
    )
    shrunk_part = jnp.sum(
        shrunk_all.reshape(buffer_rows, cache_len, rank_width) * selector[:, :, None], axis=1
    )
    peers = lax.axis_size("tp")
    pieces = lax.all_to_all(shrunk_part, "tp", split_axis=0, concat_axis=0, tiled=True)
    piece = jnp.sum(pieces.reshape(peers, -1, rank_width), axis=0)
    shrunk = lax.all_to_all(
        jnp.tile(piece, (peers, 1)), "tp", split_axis=0, concat_axis=0, tiled=True
    )
    spread_rows = (selector[:, :, None] * shrunk[:, None, :]).reshape(
        buffer_rows, cache_len * rank_width
    )
    expanded = jnp.dot(spread_rows, cached_up, precision=lax.Precision.HIGHEST)
    partial_all = jnp.dot(arrived, value_weight, preferred_element_type=jnp.float32)
    columns = lax.all_to_all(partial_all, "tp", split_axis=1, concat_axis=0, tiled=True)
    projected = jnp.sum(columns.reshape(peers, buffer_rows, width_out), axis=0)
    return (projected + expanded).astype(jnp.bfloat16)


MESH = pl.DeviceIdType.MESH
NX = 4
ROWS_Z = 64
ROWS_X = 128
BACK = 32
EIGHTHS = (3, 2, 2, 1)
CHUNKS = len(EIGHTHS)
LANES = 128
TILE = 16
NEAR = 4
F32, BF16, I32 = jnp.float32, jnp.bfloat16, jnp.int32


def hot(mask):
    return mask.astype(F32).astype(BF16)


def iota(shape, axis):
    return lax.broadcasted_iota(I32, shape, axis)


def nn(a, b):
    return jnp.dot(a, b, preferred_element_type=F32)


def nt(a, b):
    return lax.dot_general(a, b, (((1,), (1,)), ((), ())), preferred_element_type=F32)


def spans_of(depth):
    ends = [depth * sum(EIGHTHS[:c]) // sum(EIGHTHS) for c in range(CHUNKS + 1)]
    return list(zip(ends[:-1], ends[1:]))


def fused_kernel(
    groups,
    peers,
    x_hbm,
    v_hbm,
    a_hbm,
    e_hbm,
    dest_ref,
    aid_ref,
    list_ref,
    table_ref,
    out_ref,
    over_ref,
    x_ref,
    v_ref,
    a_ref,
    e_ref,
    send1,
    recv1,
    send2,
    recv2,
    bsend,
    brecv,
    acc,
    pick2t,
    pick2,
    upper,
    entries,
    home_s,
    local_s,
    slot1_s,
    slot2_s,
    mine_s,
    adp,
    early,
    back_pick,
    far_src,
    far,
    near_src,
    near,
    low_sum,
    xsend,
    xrecv,
    osend,
    orecv,
    send1_sem,
    recv1_sem,
    send2_sem,
    recv2_sem,
    bsend_sem,
    brecv_sem,
    far_send_sem,
    far_recv_sem,
    near_send_sem,
    near_recv_sem,
    xsend_sem,
    xrecv_sem,
    osend_sem,
    orecv_sem,
    load_sem,
):
    me = lax.axis_index("rep")
    mt = lax.axis_index("tp")
    mz, mx = me // NX, me % NX
    nz = groups // NX
    tok, depth = x_ref.shape
    spans = spans_of(depth)
    cache = list_ref.shape[1]
    homes = table_ref.shape[0] * LANES // groups
    rank = a_ref.shape[0] // homes
    rows_of = tok // LANES
    per = LANES // rank
    slots = NX * ROWS_X
    rowcap = out_ref.shape[1]

    loads = [
        pltpu.make_async_copy(src, dst, load_sem.at[i])
        for i, (src, dst) in enumerate(
            [(x_hbm, x_ref), (v_hbm, v_ref), (a_hbm, a_ref), (e_hbm, e_ref)]
        )
    ]
    for load in loads:
        load.start()

    barrier = pltpu.get_barrier_semaphore()

    def z_of(d):
        return lax.rem(mz + d, nz)

    def x_of(d):
        return lax.rem(mx + d, NX)

    def tp_of(d):
        return lax.rem(mt + d, peers)

    def greet(**where):
        pl.semaphore_signal(barrier, inc=1, device_id=where, device_id_type=MESH)

    z_steps = sorted(range(1, nz), key=lambda d: -min(d, nz - d))
    for d in z_steps:
        greet(rep=z_of(d) * NX + mx)
    for d in range(1, peers):
        greet(tp=tp_of(d))
    for d in range(1, NX):
        greet(rep=mz * NX + x_of(d))

    upper[...] = hot(iota((tok, tok), 0) < iota((tok, tok), 1))

    count = groups * cache
    lists = list_ref[...]
    place_of = hot(iota((cache, count), 0) == iota((cache, count), 1) % cache)
    owner = iota((groups, count), 1) // cache == iota((groups, count), 0)
    high = jnp.where(owner, nn(hot_value(lists // LANES), place_of), 0.0)
    low = jnp.where(owner, nn(hot_value(lists % LANES), place_of), 0.0)
    high = jnp.sum(high, axis=0, keepdims=True).astype(I32)
    low = jnp.sum(low, axis=0, keepdims=True).astype(I32)
    table = table_ref[...]
    both = jnp.concatenate([hot_value(table // homes), hot_value(table % homes)], axis=0)
    major = iota((table.shape[0], count), 0) == high
    minor = iota((LANES, count), 0) == low
    found = nn(both, hot(minor))
    of_home = jnp.sum(jnp.where(major, found[: table.shape[0]], 0.0), axis=0, keepdims=True)
    of_local = jnp.sum(jnp.where(major, found[table.shape[0] :], 0.0), axis=0, keepdims=True)
    spread = jnp.concatenate(
        [jnp.where(owner, of_home, 0.0), jnp.where(owner, of_local, 0.0)], axis=0
    ).astype(BF16)
    entries[...] = nn(spread, hot(iota((count, cache), 0) % cache == iota((count, cache), 1))).astype(
        BF16
    )

    def look_up(dest, aid):
        n = dest.shape[1]
        rows = nn(entries[...], hot(iota((cache, n), 0) == aid))
        serve = iota((groups, n), 0) == dest
        home = jnp.sum(jnp.where(serve, rows[:groups], 0.0), axis=0, keepdims=True)
        local = jnp.sum(jnp.where(serve, rows[groups:], 0.0), axis=0, keepdims=True)
        return home.astype(I32), local.astype(I32)

    def rank_in(member):
        earlier = nn(hot(member), upper[...])
        return jnp.sum(jnp.where(member, earlier, 0.0), axis=0, keepdims=True).astype(I32)

    def own(ref):
        return jnp.concatenate([ref[pl.ds(rows_of * me + i, 1), :] for i in range(rows_of)], axis=1)

    own_dest = own(dest_ref)
    own_home, _ = look_up(own_dest, own(aid_ref))
    own_plane = own_home // NX
    own_rank1 = rank_in(iota((nz, tok), 0) == own_plane)
    own_slot1 = jnp.where(own_rank1 < ROWS_Z, own_plane * ROWS_Z + own_rank1, -1)
    pick1 = hot(iota((nz * ROWS_Z, tok), 0) == own_slot1)

    def pack(c):
        first, last = spans[c]
        rows = nn(pick1, x_ref[:, first:last])
        send1[c][...] = rows.astype(BF16).reshape(nz, ROWS_Z, last - first)

    loads[0].wait()
    pack(0)
    pl.semaphore_wait(barrier, nz + NX + peers - 3)

    def arrived(buffer, sem):
        pltpu.make_async_copy(buffer, buffer, sem).wait()

    def push(src, dst, ssem, rsem, **where):
        pltpu.make_async_remote_copy(
            src_ref=src,
            dst_ref=dst,
            send_sem=ssem,
            recv_sem=rsem,
            device_id=where,
            device_id_type=MESH,
        ).start()

    def z_start(c):
        for d in z_steps:
            to = z_of(d)
            push(
                send1[c].at[to],
                recv1[c].at[mz],
                send1_sem.at[c],
                recv1_sem.at[c],
                rep=to * NX + mx,
            )
        pltpu.make_async_copy(send1[c].at[mz], recv1[c].at[mz], recv1_sem.at[c]).start()

    z_start(0)
    for c in range(1, CHUNKS):
        pack(c)
        z_start(c)

    width = bsend.shape[1]
    loads[1].wait()
    step = 256
    for n in range(v_ref.shape[1] // step):
        bt = nn(x_ref[...], v_ref[:, n * step : (n + 1) * step]).T
        for i in range(step // width):
            bsend[n * (step // width) + i] = bt[i * width : (i + 1) * width]

    for d in range(1, peers):
        to = tp_of(d)
        push(bsend.at[to], brecv.at[mt], bsend_sem.at[0], brecv_sem.at[0], tp=to)
    pltpu.make_async_copy(bsend.at[mt], brecv.at[mt], brecv_sem.at[0]).start()

    batch = 8
    counts = jnp.zeros((groups, LANES), F32)
    for q in range(groups // batch):
        ids = range(q * batch, (q + 1) * batch)
        lines = range(q * batch * rows_of, (q + 1) * batch * rows_of)
        dest = jnp.concatenate([dest_ref[r : r + 1, :] for r in lines], axis=1)
        aid = jnp.concatenate([aid_ref[r : r + 1, :] for r in lines], axis=1)
        home, local = look_up(dest, aid)
        for j, g in enumerate(ids):
            home_s[g : g + 1, :] = home[:, j * tok : (j + 1) * tok]
            local_s[g : g + 1, :] = local[:, j * tok : (j + 1) * tok]
        n = batch * tok
        counts += nn(
            hot(iota((groups, n), 0) == home),
            hot(iota((n, LANES), 0) // tok + q * batch == iota((n, LANES), 1)),
        )
    by_plane = nn(hot(iota((nz, groups), 0) == iota((nz, groups), 1) // NX), counts.astype(BF16))
    by_column = nn(
        counts.astype(BF16), hot(iota((LANES, LANES), 0) % NX == iota((LANES, LANES), 1))
    )
    over = (
        jnp.max(jnp.where(counts > BACK, 1.0, 0.0), axis=0, keepdims=True)
        + jnp.max(jnp.where(by_plane > ROWS_Z, 1.0, 0.0), axis=0, keepdims=True)
        + jnp.max(jnp.where(by_column > ROWS_X, 1.0, 0.0), axis=0, keepdims=True)
    )
    over_ref[0, 0] = jnp.max(over).astype(I32)

    homes_all = home_s[...]
    before = hot(
        (iota((groups, groups), 1) % NX == iota((groups, groups), 0) % NX)
        & (iota((groups, groups), 1) < iota((groups, groups), 0))
    )
    ones = jnp.ones((tok, LANES), BF16)

    def rank2(member):
        picked = hot(member)
        earlier = nn(picked, upper[...])
        total = nn(before, nn(picked, ones).astype(BF16))
        return (earlier + jnp.concatenate([total] * (tok // LANES), axis=1)).astype(I32), earlier

    here = homes_all // NX == mz
    place1 = nn(hot(here), upper[...]).astype(I32)
    slot1_s[...] = jnp.where(here & (place1 < ROWS_Z), place1, -1)
    target = jnp.full((groups, tok), -1, I32)
    for i in range(NX):
        member = homes_all == mz * NX + i
        place, _ = rank2(member)
        target = jnp.where(member & (place < ROWS_X), i * ROWS_X + place, target)
    slot2_s[...] = target
    member = homes_all == me
    place, back_rank = rank2(member)
    mine_s[0] = jnp.where(member & (place < ROWS_X), place, -1)
    mine_s[1] = jnp.where(member, back_rank.astype(I32), -1)

    def route(z, w):
        g = z * NX + mx
        first = hot(iota((ROWS_Z, tok), 0) == slot1_s[pl.ds(g, 1), :])
        second = hot(iota((slots, tok), 0) == slot2_s[pl.ds(g, 1), :])
        pick2t[pl.ds(pl.multiple_of(z * ROWS_Z, ROWS_Z), ROWS_Z), :] = nt(first, second)
        return w

    lax.fori_loop(0, nz, route, 0)
    pick2[...] = pick2t[...].T.astype(BF16)

    loads[2].wait()
    loads[3].wait()
    adp[...] = jnp.zeros_like(adp)
    acc[...] = jnp.zeros_like(acc)

    def shrink(c):
        arrived(recv2[c], recv2_sem.at[c])
        first, last = spans[c]
        rows = recv2[c][...].reshape(slots, last - first)
        return nt(rows, a_ref[:, first:last])

    def stage(c):
        arrived(recv1[c], recv1_sem.at[c])
        wide = spans[c][1] - spans[c][0]
        rows = nn(pick2[...], recv1[c][...].reshape(nz * ROWS_Z, wide))
        send2[c][...] = rows.astype(BF16).reshape(NX, ROWS_X, wide)

        for d in range(1, NX):
            to = x_of(d)
            push(
                send2[c].at[to],
                recv2[c].at[mx],
                send2_sem.at[c],
                recv2_sem.at[c],
                rep=mz * NX + to,
            )
        pltpu.make_async_copy(send2[c].at[mx], recv2[c].at[mx], recv2_sem.at[c]).start()

    def homed(g, w):
        column = lax.rem(g, NX)
        second = hot(iota((ROWS_X, tok), 0) == mine_s[0, pl.ds(g, 1), :])
        back = hot(iota((BACK, tok), 0) == mine_s[1, pl.ds(g, 1), :])
        value = (local_s[pl.ds(g, 1), :] + 1).astype(F32).astype(BF16)
        at = pl.ds(pl.multiple_of(column * ROWS_X, ROWS_X), ROWS_X)
        adp[at, :] += nt(second, jnp.broadcast_to(value, (LANES, tok)))
        back_pick[column, g // NX] = nt(back, second)
        return w

    shares = (0, 12 * groups // 32, 22 * groups // 32, groups, groups)
    for c in range(CHUNKS):
        stage(c)
        lax.fori_loop(shares[c], shares[c + 1], homed, 0)
        if c:
            acc[...] += shrink(c - 1)
    own_back = rank_in(iota((groups, tok), 0) == own_home)
    own_back = jnp.where(own_back < BACK, own_home * BACK + own_back, -1)
    column = jnp.broadcast_to(own_back.astype(F32), (LANES, tok)).T[:, 0:1].astype(I32)
    unpack = hot(iota((tok, groups * BACK), 1) == column)
    own_out = own_dest * rowcap + rank_in(iota((groups, tok), 0) == own_dest)
    wanted = adp[...].astype(I32) - 1
    lane = iota((slots, LANES), 1) // rank

    def fold(got):
        total = jnp.zeros((slots, LANES), F32)
        for n in range(homes // per):
            total += jnp.where(wanted == n * per + lane, got[:, n * LANES : (n + 1) * LANES], 0.0)
        return total

    early[...] = fold(acc[...])
    folded = early[...] + fold(shrink(CHUNKS - 1))

    low = jnp.sum(folded.T.reshape(per, rank, slots), axis=0)
    for i in range(NX):
        far_src[i] = low[:, i * LANES : (i + 1) * LANES]
    team = NEAR
    for k in sorted(range(1, peers // team), key=lambda k: -min(k, peers // team - k)):
        to = tp_of(team * k)
        push(far_src, far.at[mt // team], far_send_sem.at[0], far_recv_sem.at[0], tp=to)
    pltpu.make_async_copy(far_src, far.at[mt // team], far_recv_sem.at[0]).start()
    arrived(far, far_recv_sem.at[0])
    near_src[...] = jnp.sum(far[...], axis=0)
    first = mt // team * team
    for k in range(1, team):
        to = first + lax.rem(mt + k, team)
        push(near_src, near.at[mt - first], near_send_sem.at[0], near_recv_sem.at[0], tp=to)
    pltpu.make_async_copy(near_src, near.at[mt - first], near_recv_sem.at[0]).start()
    arrived(near, near_recv_sem.at[0])
    low_sum[...] = jnp.sum(near[...], axis=0)

    e2 = jnp.concatenate([e_ref[...], e_ref[...]], axis=1)
    lane1 = iota((ROWS_X, LANES), 1)
    for dx in (2, 1, 3, 0):
        y = x_of(dx)
        tile = jnp.concatenate([low_sum[y]] * per, axis=0).T
        chosen = adp[pl.ds(pl.multiple_of(y * ROWS_X, ROWS_X), ROWS_X), :].astype(I32) - 1
        spread = jnp.concatenate(
            [
                jnp.where(chosen == n * per + lane1 // rank, tile, 0.0)
                for n in range(homes // per)
            ],
            axis=1,
        )
        hi = spread.astype(BF16)
        lo = (spread - hi.astype(F32)).astype(BF16)
        full = nn(hi, e2) + nn(lo, e2)
        top = full.astype(BF16).astype(F32)
        pair = jnp.where(lane1 < width, full, full - top).astype(BF16)
        sel = back_pick[y].reshape(nz * BACK, LANES).astype(BF16)
        rows = nn(sel, pair)
        for z in range(nz):
            xsend[z * NX + y] = rows[z * BACK : (z + 1) * BACK].astype(BF16)
        for dz in z_steps + [0]:
            if dz or dx:
                to = z_of(dz) * NX + y
                push(xsend.at[to], xrecv.at[me], xsend_sem.at[0], xrecv_sem.at[0], rep=to)
    pltpu.make_async_copy(xsend.at[me], xrecv.at[me], xrecv_sem.at[0]).start()

    arrived(brecv, brecv_sem.at[0])
    base = jnp.sum(brecv[...], axis=0)

    arrived(xrecv, xrecv_sem.at[0])
    extra = nn(unpack, xrecv[...].reshape(groups * BACK, LANES)).T
    total = (base + extra[:width] + extra[width:]).astype(BF16)
    blank = jnp.zeros_like(total)
    sides = jnp.concatenate(
        [jnp.concatenate([total, blank], axis=1), jnp.concatenate([blank, total], axis=1)], axis=0
    )
    line = iota((NX * TILE, tok), 0)
    for dz in z_steps + [0]:
        z = z_of(dz)
        slot = z * NX * rowcap + line // TILE * rowcap + line % TILE
        high = (slot + TILE == own_out) & (line % TILE < rowcap - TILE)
        rows = nt(jnp.concatenate([hot(slot == own_out), hot(high)], axis=1), sides)
        for i in range(NX):
            osend[z * NX + i] = rows[i * TILE : (i + 1) * TILE].astype(BF16)
        for dx in range(NX):
            if dz or dx:
                to = z * NX + x_of(dx)
                push(osend.at[to], orecv.at[me], osend_sem.at[0], orecv_sem.at[0], rep=to)
    pltpu.make_async_copy(osend.at[me], orecv.at[me], orecv_sem.at[0]).start()

    for c in range(CHUNKS):
        arrived(send1[c].at[pl.ds(0, nz - 1)], send1_sem.at[c])
        arrived(send2[c].at[pl.ds(0, NX - 1)], send2_sem.at[c])
    arrived(bsend.at[pl.ds(0, peers - 1)], bsend_sem.at[0])
    arrived(far.at[pl.ds(0, peers // team - 1)], far_send_sem.at[0])
    arrived(near.at[pl.ds(0, team - 1)], near_send_sem.at[0])
    arrived(xsend.at[pl.ds(0, groups - 1)], xsend_sem.at[0])
    arrived(osend.at[pl.ds(0, groups - 1)], osend_sem.at[0])
    arrived(orecv, orecv_sem.at[0])
    done = orecv[...].astype(F32)
    out_ref[:, :TILE, :] = done[:, :, :width].astype(BF16)
    out_ref[:, TILE:, :] = done[:, : rowcap - TILE, width:].astype(BF16)


def hot_value(a):
    return a.astype(F32).astype(BF16)


def fused(groups, peers, requests, value_weight, shrink, expand, dest, aid, lists, table):
    tok, depth = requests.shape
    width = expand.shape[1]
    rowcap = 3 * tok // groups
    nz, slots = groups // NX, NX * ROWS_X
    rank = shrink.shape[0] * groups // (table.size)
    wide = [last - first for first, last in spans_of(depth)]
    vmem = pl.BlockSpec(memory_space=pltpu.VMEM)
    dma = pltpu.SemaphoreType.DMA
    return pl.pallas_call(
        functools.partial(fused_kernel, groups, peers),
        out_shape=[
            jax.ShapeDtypeStruct((groups, rowcap, width), BF16),
            jax.ShapeDtypeStruct((1, 1), I32),
        ],
        in_specs=[pl.BlockSpec(memory_space=pl.ANY)] * 4 + [vmem] * 4,
        out_specs=[vmem, pl.BlockSpec(memory_space=pltpu.SMEM)],
        scratch_shapes=[
            pltpu.VMEM(requests.shape, BF16),
            pltpu.VMEM(value_weight.shape, BF16),
            pltpu.VMEM(shrink.shape, BF16),
            pltpu.VMEM(expand.shape, BF16),
            [pltpu.VMEM((nz, ROWS_Z, n), BF16) for n in wide],
            [pltpu.VMEM((nz, ROWS_Z, n), BF16) for n in wide],
            [pltpu.VMEM((NX, ROWS_X, n), BF16) for n in wide],
            [pltpu.VMEM((NX, ROWS_X, n), BF16) for n in wide],
            pltpu.VMEM((peers, width, tok), F32),
            pltpu.VMEM((peers, width, tok), F32),
            pltpu.VMEM((slots, shrink.shape[0]), F32),
            pltpu.VMEM((nz * ROWS_Z, slots), F32),
            pltpu.VMEM((slots, nz * ROWS_Z), BF16),
            pltpu.VMEM((tok, tok), BF16),
            pltpu.VMEM((2 * groups, lists.shape[1]), BF16),
            pltpu.VMEM((groups, tok), I32),
            pltpu.VMEM((groups, tok), I32),
            pltpu.VMEM((groups, tok), I32),
            pltpu.VMEM((groups, tok), I32),
            pltpu.VMEM((2, groups, tok), I32),
            pltpu.VMEM((slots, LANES), F32),
            pltpu.VMEM((slots, LANES), F32),
            pltpu.VMEM((NX, nz, BACK, LANES), F32),
            pltpu.VMEM((NX, rank, LANES), F32),
            pltpu.VMEM((peers // NEAR, NX, rank, LANES), F32),
            pltpu.VMEM((NX, rank, LANES), F32),
            pltpu.VMEM((NEAR, NX, rank, LANES), F32),
            pltpu.VMEM((NX, rank, LANES), F32),
            pltpu.VMEM((groups, BACK, LANES), BF16),
            pltpu.VMEM((groups, BACK, LANES), BF16),
            pltpu.VMEM((groups, TILE, LANES), BF16),
            pltpu.VMEM((groups, TILE, LANES), BF16),
            *[dma((CHUNKS,))] * 4,
            *[dma((1,))] * 10,
            dma((4,)),
        ],
        compiler_params=pltpu.CompilerParams(
            collective_id=0, has_side_effects=True, vmem_limit_bytes=63 * 1024 * 1024
        ),
        name="fused",
    )(requests, value_weight, shrink, expand, dest, aid, lists, table)


def on_device(
    requests,
    value_weight,
    shrink_weight,
    expand_weight,
    destination,
    adapter_ids,
    cache_lists,
    home_table,
):
    groups = lax.axis_size("rep")
    tok = requests.shape[0]
    home_count, rank, depth = shrink_weight.shape
    width = expand_weight.shape[2]
    out, over = fused(
        groups,
        lax.axis_size("tp"),
        requests,
        value_weight,
        shrink_weight.reshape(home_count * rank, depth),
        expand_weight.reshape(home_count * rank, width),
        destination.reshape(-1, LANES),
        adapter_ids.reshape(-1, LANES),
        cache_lists,
        home_table.reshape(-1, LANES),
    )
    out = out.reshape(-1, width)

    def any_input(out):
        return by_serving_group(
            requests,
            value_weight,
            shrink_weight,
            expand_weight,
            destination,
            adapter_ids,
            cache_lists,
            home_table,
        )

    return lax.cond(over[0, 0] > 0, any_input, lambda out: out, out)


def solution(mesh):
    in_specs = (
        P("rep", "tp"),
        P("tp", None),
        P("rep", None, "tp"),
        P("rep", None, "tp"),
        P(),
        P(),
        P(),
        P(),
    )
    out_specs = P("rep", "tp")
    return jax.shard_map(
        on_device, mesh=mesh, in_specs=in_specs, out_specs=out_specs, check_vma=False
    )
```
